32 devices in a mesh: fsdp: 4 (over z), ctx: 4 (over y, core), tp: 2 (over x).
Axes of the slice: x: 2, y: 2, z: 4, core: 2. Of those that a mesh axis runs over, the one named last changes fastest.
Arguments:
- tokens: bfloat16 [8, 1024, 1536], P('fsdp', 'ctx'), may hold values from -6 to 6
- segments: int32 [8, 1024], P('fsdp'), may hold values from 0 to 1023, as said below
- cotangent: bfloat16 [8, 1024, 1536], P('fsdp', 'ctx'), may hold values from -6 to 6
- gain_attn: bfloat16 [1536], P(('fsdp', 'ctx')), may hold values from 0.5 to 1.5
- w_query: bfloat16 [1536, 1536], P(('fsdp', 'ctx'), 'tp'), may hold values from -0.15625 to 0.15625
- w_key: bfloat16 [1536, 768], P(('fsdp', 'ctx'), 'tp'), may hold values from -0.15625 to 0.15625
- w_value: bfloat16 [1536, 768], P(('fsdp', 'ctx'), 'tp'), may hold values from -0.15625 to 0.15625
- w_out: bfloat16 [1536, 1536], P('tp', ('fsdp', 'ctx')), may hold values from -1.75 to 1.75
- gain_mlp: bfloat16 [1536], P(('fsdp', 'ctx')), may hold values from 0.5 to 1.5
- w_gate: bfloat16 [1536, 4096], P(('fsdp', 'ctx'), 'tp'), may hold values from -0.15625 to 0.15625
- w_up: bfloat16 [1536, 4096], P(('fsdp', 'ctx'), 'tp'), may hold values from -0.15625 to 0.15625
- w_down: bfloat16 [4096, 1536], P('tp', ('fsdp', 'ctx')), may hold values from -0.09375 to 0.09375
Outputs:
- output: bfloat16 [8, 1024, 1536], P('fsdp', 'ctx')
- grad_tokens: float32 [8, 1024, 1536], P('fsdp', 'ctx')
- grad_gain_attn: float32 [1536], P(('fsdp', 'ctx'))
- grad_query: float32 [1536, 1536], P(('fsdp', 'ctx'), 'tp')
- grad_key: float32 [1536, 768], P(('fsdp', 'ctx'), 'tp')
- grad_value: float32 [1536, 768], P(('fsdp', 'ctx'), 'tp')
- grad_out: float32 [1536, 1536], P('tp', ('fsdp', 'ctx'))
- grad_gain_mlp: float32 [1536], P(('fsdp', 'ctx'))
- grad_gate: float32 [1536, 4096], P(('fsdp', 'ctx'), 'tp')
- grad_up: float32 [1536, 4096], P(('fsdp', 'ctx'), 'tp')
- grad_down: float32 [4096, 1536], P('tp', ('fsdp', 'ctx'))
The draws below stay inside these ranges and needn't reach their ends.
Inputs may be any that keep to these rules, and one draw needn't show every extreme that they name: `segments`: segment numbers start at 0 in each sequence and never fall; the last position of every sequence carries 1024 - 1; in every sequence one document covers positions 255 through 1024 - 256.
All inputs are finite; a program needn't handle non-finite values.
Results may differ from the reference program's by a relative error of at most 0.018.
Values may be sent and summed in bfloat16 or wider, within the bound.
A program may use at most 192 MiB of HBM per device.

```python
import math
import jax
import jax.numpy as jnp
from jax import lax

D = 1536
HEADS = 16
KV_HEADS = 8
HD = 96
FF = 4096
GROUP = 2
SEQ = 1024
SPAN = 256
SEQS = 8


def draw_segments(key, part):
    key = jax.random.fold_in(key, 11)
    key_start, key_end, key_cut = jax.random.split(key, 3)
    doc_start = jax.random.randint(key_start, (SEQS, 1), 0, SPAN)
    doc_end = jax.random.randint(key_end, (SEQS, 1), SEQ - SPAN + 1, SEQ + 1)
    places = jnp.arange(SEQ, dtype=jnp.int32)[None, :]
    cuts = jax.random.randint(key_cut, (SEQS, SEQ), 0, 24) == 0
    outside = (places < doc_start) | (places > doc_end)
    flags = cuts & outside | (places == doc_start) | (places == doc_end)
    flags = flags & (places > 0)
    numbers = jnp.cumsum(flags.astype(jnp.int32), axis=1).astype(jnp.int32)
    last_number = numbers[:, SEQ - 1:SEQ]
    return jnp.where(numbers == last_number, SEQ - 1, numbers).astype(jnp.int32)


def levels(rng, shape, cuts, least, largest):
    def one(dim, shards_of):
        draws = jax.random.uniform(jax.random.fold_in(jax.random.fold_in(rng, 6), dim), (shards_of,), jnp.float32, least / len(cuts), largest / len(cuts))
        return jnp.repeat(jnp.exp(draws), shape[dim] // shards_of).reshape((-1,) + (1,) * (len(shape) - dim - 1))

    loudness = one(*cuts[0])
    for cut in cuts[1:]:
        loudness = loudness * one(*cut)
    return loudness


def scatter_about(rng, dims, width, reach, pieces=(), held_as=jnp.bfloat16):
    values = width * jax.random.normal(rng, dims, jnp.float32)
    if pieces:
        values = values * levels(rng, dims, pieces, -0.22, 0.18)
    return jnp.clip(values, -reach, reach).astype(held_as)


def setup_inputs(seed: int = 0) -> dict:
    key_of = jax.random.split(jax.random.key(seed), 13)
    tokens = scatter_about(key_of[0], (SEQS, SEQ, D), 1.0, 6.0, ((0, 4), (1, 4)))
    segments = draw_segments(jax.random.fold_in(key_of[12], 71), 0)
    cotangent = scatter_about(key_of[2], (SEQS, SEQ, D), 1.0, 6.0, ((0, 4), (1, 4)))
    gain_attn = jnp.clip(1.0 + 0.1 * jax.random.normal(key_of[3], (D,), jnp.float32), 0.5, 1.5).astype(jnp.bfloat16)
    w_query = scatter_about(key_of[4], (D, HEADS * HD), D ** -0.5, 0.15625, ((0, 16), (1, 2)))
    w_key = scatter_about(key_of[5], (D, KV_HEADS * HD), D ** -0.5, 0.15625, ((0, 16), (1, 2)))
    w_value = scatter_about(key_of[6], (D, KV_HEADS * HD), D ** -0.5, 0.15625, ((0, 16), (1, 2)))
    w_out = scatter_about(key_of[7], (HEADS * HD, D), (HEADS * HD // 128) ** -0.5, 1.75, ((0, 2), (1, 16)))
    gain_mlp = jnp.clip(1.0 + 0.1 * jax.random.normal(key_of[8], (D,), jnp.float32), 0.5, 1.5).astype(jnp.bfloat16)
    w_gate = scatter_about(key_of[9], (D, FF), D ** -0.5, 0.15625, ((0, 16), (1, 2)))
    w_up = scatter_about(key_of[10], (D, FF), D ** -0.5, 0.15625, ((0, 16), (1, 2)))
    w_down = scatter_about(key_of[11], (FF, D), FF ** -0.5, 0.09375, ((0, 2), (1, 16)))
    return dict(tokens=tokens, segments=segments, cotangent=cotangent, gain_attn=gain_attn, w_query=w_query, w_key=w_key, w_value=w_value, w_out=w_out, gain_mlp=gain_mlp, w_gate=w_gate, w_up=w_up, w_down=w_down)


epsilon = 1e-05
rope_base = 100000.0
highest = lax.Precision.HIGHEST

@jax.custom_vjp
def low(v):
    return lax.optimization_barrier(v.astype(jnp.bfloat16)).astype(jnp.float32)

@jax.custom_vjp
def low_back(v):
    return v

def low_keep(v):
    return (low(v), None)

def low_pass(kept, grad):
    return (grad,)

def back_keep(v):
    return (v, None)

def back_low(kept, grad):
    return (low(grad),)
low.defvjp(low_keep, low_pass)
low_back.defvjp(back_keep, back_low)

def rope_tables(positions):
    half_width = HD // 2
    frequency = rope_base ** (-(2.0 * jnp.arange(half_width, dtype=jnp.float32)) / HD)
    angles = positions.astype(jnp.float32)[:, None] * frequency[None, :]
    return (jnp.cos(angles), jnp.sin(angles))

def rotate(vectors, cosine_table, sine_table):
    half_width = vectors.shape[-1] // 2
    former = vectors[..., :half_width]
    latter = vectors[..., half_width:]
    return jnp.concatenate([former * cosine_table - latter * sine_table, latter * cosine_table + former * sine_table], axis=-1)

def normalize(vectors, gain_row):
    scale_row = lax.rsqrt(lax.optimization_barrier(jnp.mean(vectors * vectors, axis=-1, keepdims=True)) + epsilon)
    return vectors * scale_row * gain_row

def attend(queries, key_rows, values, segment_row):
    length = queries.shape[0]
    block_rows = math.gcd(512, length)
    block_count = length // block_rows
    positions = jnp.arange(length, dtype=jnp.int32)
    score_scale = 1.0 / math.sqrt(HD)
    query_blocks = queries.reshape(block_count, block_rows, KV_HEADS, GROUP, HD)
    segment_blocks = segment_row.reshape(block_count, block_rows)
    position_blocks = positions.reshape(block_count, block_rows)

    def one_block(inputs):
        query_part, segment_part, position_part = inputs
        raw_scores = low_back(jnp.einsum('qhgd,khd->hgqk', query_part, key_rows, precision=highest))
        allowed = (segment_part[:, None] == segment_row[None, :]) & (position_part[:, None] >= positions[None, :])
        scores = jnp.where(allowed, raw_scores * score_scale, -1e+30)
        row_top = lax.optimization_barrier(jnp.max(scores, axis=-1, keepdims=True))
        weights = jnp.where(allowed, jnp.exp(scores - row_top), 0.0)
        probability = weights / lax.optimization_barrier(jnp.sum(weights, axis=-1, keepdims=True))
        return jnp.einsum('hgqk,khd->qhgd', low(probability), values, precision=highest)
    result = lax.map(jax.checkpoint(one_block), (query_blocks, segment_blocks, position_blocks))
    return result.reshape(length, HEADS * HD)

def block_layer(tokens, segment_row, cosine_table, sine_table, gain_attn, w_query, w_key, w_value, w_out, gain_mlp, w_gate, w_up, w_down):
    length = tokens.shape[0]
    normed = low(normalize(tokens, gain_attn))
    query_raw = low_back(jnp.dot(normed, w_query, precision=highest)).reshape(length, KV_HEADS, GROUP, HD)
    key_raw = low_back(jnp.dot(normed, w_key, precision=highest)).reshape(length, KV_HEADS, HD)
    values = low(low_back(jnp.dot(normed, w_value, precision=highest))).reshape(length, KV_HEADS, HD)
    queries = low(rotate(query_raw, cosine_table[:, None, None, :], sine_table[:, None, None, :]))
    key_rows = low(rotate(key_raw, cosine_table[:, None, :], sine_table[:, None, :]))
    mixed_low = low(low_back(attend(queries, key_rows, values, segment_row)))
    middle = tokens + low_back(jnp.dot(mixed_low, w_out, precision=highest))
    second = low(normalize(middle, gain_mlp))
    gate_part = low_back(jnp.dot(second, w_gate, precision=highest))
    upward = low_back(jnp.dot(second, w_up, precision=highest))
    hidden = low(jax.nn.silu(gate_part) * upward)
    return middle + low_back(jnp.dot(hidden, w_down, precision=highest))

def reference(tokens, segments, cotangent, gain_attn, w_query, w_key, w_value, w_out, gain_mlp, w_gate, w_up, w_down):
    params = tuple((weight.astype(jnp.float32) for weight in (gain_attn, w_query, w_key, w_value, w_out, gain_mlp, w_gate, w_up, w_down)))
    cosine_table, sine_table = rope_tables(jnp.arange(SEQ, dtype=jnp.int32))

    def one_sequence(running, inputs):
        token_rows, segment_row, grad_rows = inputs

        def forward_fn(token_arg, *weight_args):
            return block_layer(token_arg, segment_row, cosine_table, sine_table, *weight_args)
        result, pullback = jax.vjp(forward_fn, token_rows.astype(jnp.float32), *params)
        gradients = pullback(grad_rows.astype(jnp.float32))
        running = tuple((running_sum + addend for running_sum, addend in zip(running, gradients[1:])))
        return (running, (result.astype(jnp.bfloat16), gradients[0]))
    zeros_start = tuple((jnp.zeros(weight.shape, jnp.float32) for weight in params))
    running, (outputs, token_grads) = lax.scan(one_sequence, zeros_start, (tokens, segments, cotangent))
    return (outputs, token_grads, running[0], running[1], running[2], running[3], running[4], running[5], running[6], running[7], running[8])
```

```python
import math

import jax
import jax.numpy as jnp
from jax import lax
from jax.sharding import PartitionSpec as P

HD = 96
GROUP = 2


epsilon = 1e-05
rope_base = 100000.0
negative = -1e30


def rope_tables(positions):
    half_width = HD // 2
    frequency = rope_base ** (-(2.0 * jnp.arange(half_width, dtype=jnp.float32)) / HD)
    angles = positions.astype(jnp.float32)[:, None] * frequency[None, :]
    return (jnp.cos(angles), jnp.sin(angles))


def rotate(vectors, cosine_table, sine_table):
    half_width = vectors.shape[-1] // 2
    former = vectors[..., :half_width]
    latter = vectors[..., half_width:]
    return jnp.concatenate(
        [former * cosine_table - latter * sine_table, latter * cosine_table + former * sine_table],
        axis=-1,
    )


def head_sum(partial_rows):
    return lax.psum(partial_rows.astype(jnp.bfloat16), "tp").astype(jnp.float32)


def weight_gather(shards):
    row_parts = (
        lax.all_gather(shards[0], ("fsdp", "ctx"), axis=0, tiled=True),
        lax.all_gather(shards[1], ("fsdp", "ctx"), axis=0, tiled=True),
        lax.all_gather(shards[2], ("fsdp", "ctx"), axis=0, tiled=True),
        lax.all_gather(shards[3], ("fsdp", "ctx"), axis=0, tiled=True),
        lax.all_gather(shards[4], ("fsdp", "ctx"), axis=0, tiled=True),
        lax.all_gather(shards[5], ("fsdp", "ctx"), axis=0, tiled=True),
        lax.all_gather(shards[6], ("fsdp", "ctx"), axis=0, tiled=True),
    )
    column_parts = (
        lax.all_gather(shards[7], ("fsdp", "ctx"), axis=1, tiled=True),
        lax.all_gather(shards[8], ("fsdp", "ctx"), axis=1, tiled=True),
    )
    return tuple(row_parts) + tuple(column_parts)


def grad_reduce(gradients):
    row_parts = (
        lax.psum_scatter(gradients[0], ("fsdp", "ctx"), scatter_dimension=0, tiled=True),
        lax.psum_scatter(gradients[1], ("fsdp", "ctx"), scatter_dimension=0, tiled=True),
        lax.psum_scatter(gradients[2], ("fsdp", "ctx"), scatter_dimension=0, tiled=True),
        lax.psum_scatter(gradients[3], ("fsdp", "ctx"), scatter_dimension=0, tiled=True),
        lax.psum_scatter(gradients[4], ("fsdp", "ctx"), scatter_dimension=0, tiled=True),
        lax.psum_scatter(gradients[5], ("fsdp", "ctx"), scatter_dimension=0, tiled=True),
        lax.psum_scatter(gradients[6], ("fsdp", "ctx"), scatter_dimension=0, tiled=True),
    )
    column_parts = (
        lax.psum_scatter(gradients[7], ("fsdp", "ctx"), scatter_dimension=1, tiled=True),
        lax.psum_scatter(gradients[8], ("fsdp", "ctx"), scatter_dimension=1, tiled=True),
    )
    return tuple(row_parts) + tuple(column_parts)


def block_scores(queries, key_block, query_seg, positions, key_seg, key_start):
    score_scale = 1.0 / math.sqrt(queries.shape[-1])
    key_positions = key_start + jnp.arange(key_block.shape[0], dtype=jnp.int32)
    allowed = (query_seg[:, None] == key_seg[None, :]) & (
        positions[:, None] >= key_positions[None, :]
    )
    raw_scores = jnp.einsum(
        "qhgd,khd->hgqk", queries, key_block, preferred_element_type=jnp.float32
    )
    return (jnp.where(allowed, raw_scores * score_scale, negative), allowed)


def block_fetch(
    key_all, value_all, segment_row, block_index, block_keys, last_position, first_segment
):
    key_start = block_index * block_keys
    key_block = lax.dynamic_slice_in_dim(key_all, key_start, block_keys, 0)
    value_block = lax.dynamic_slice_in_dim(value_all, key_start, block_keys, 0)
    key_seg = lax.dynamic_slice_in_dim(segment_row, key_start, block_keys, 0)
    needed = (key_start <= last_position) & (key_seg[block_keys - 1] >= first_segment)
    return (key_start, key_block, value_block, key_seg, needed)


def attention_forward(queries, key_all, value_all, segment_row, query_seg, positions):
    row_count, heads_kv, group_size, head_dim = queries.shape
    length = key_all.shape[0]
    block_keys = math.gcd(512, length)
    block_total = length // block_keys
    last_position = positions[row_count - 1]
    first_segment = query_seg[0]

    def stats_step(block_index, state):
        key_start, key_block, value_block, key_seg, needed = block_fetch(
            key_all, value_all, segment_row, block_index, block_keys, last_position, first_segment
        )
        top_old, total_old = state
        scores, allowed = block_scores(queries, key_block, query_seg, positions, key_seg, key_start)
        top_new = jnp.maximum(top_old, jnp.max(scores, axis=-1))
        weights = jnp.where(allowed, jnp.exp(scores - top_new[..., None]), 0.0)
        return (top_new, total_old * jnp.exp(top_old - top_new) + jnp.sum(weights, axis=-1))

    start_top = jnp.full((heads_kv, group_size, row_count), negative, jnp.float32)
    row_top, row_total = lax.fori_loop(
        0, block_total, stats_step, (start_top, jnp.zeros_like(start_top))
    )

    def output_step(block_index, state):
        key_start, key_block, value_block, key_seg, needed = block_fetch(
            key_all, value_all, segment_row, block_index, block_keys, last_position, first_segment
        )
        scores, allowed = block_scores(queries, key_block, query_seg, positions, key_seg, key_start)
        probability = (
            jnp.where(allowed, jnp.exp(scores - row_top[..., None]), 0.0) / row_total[..., None]
        )
        return state + jnp.einsum(
            "hgqk,khd->qhgd",
            probability.astype(jnp.bfloat16),
            value_block,
            preferred_element_type=jnp.float32,
        )

    start_out = jnp.zeros((row_count, heads_kv, group_size, head_dim), jnp.float32)
    out_low = lax.fori_loop(0, block_total, output_step, start_out)
    return (row_top, row_total, out_low)


def attention_backward(
    queries,
    key_all,
    value_all,
    segment_row,
    query_seg,
    positions,
    row_top,
    row_total,
    grad_mixed,
    row_delta,
):
    row_count, heads_kv, group_size, head_dim = queries.shape
    length = key_all.shape[0]
    block_keys = math.gcd(512, length)
    block_total = length // block_keys
    last_position = positions[row_count - 1]
    first_segment = query_seg[0]
    score_scale = 1.0 / math.sqrt(head_dim)

    def grad_step(block_index, state):
        key_start, key_block, value_block, key_seg, needed = block_fetch(
            key_all, value_all, segment_row, block_index, block_keys, last_position, first_segment
        )
        grad_query, grad_keys, grad_values = state
        scores, allowed = block_scores(queries, key_block, query_seg, positions, key_seg, key_start)
        probability = (
            jnp.where(allowed, jnp.exp(scores - row_top[..., None]), 0.0) / row_total[..., None]
        )
        grad_prob = jnp.einsum(
            "qhgd,khd->hgqk", grad_mixed, value_block, preferred_element_type=jnp.float32
        )
        grad_score = (probability * (grad_prob - row_delta[..., None]) * score_scale).astype(
            jnp.bfloat16
        )
        grad_query = grad_query + jnp.einsum(
            "hgqk,khd->qhgd", grad_score, key_block, preferred_element_type=jnp.float32
        )
        key_part = jnp.einsum(
            "hgqk,qhgd->khd", grad_score, queries, preferred_element_type=jnp.float32
        )
        value_part = jnp.einsum(
            "hgqk,qhgd->khd",
            probability.astype(jnp.bfloat16),
            grad_mixed,
            preferred_element_type=jnp.float32,
        )
        grad_keys = lax.dynamic_update_slice_in_dim(grad_keys, key_part, key_start, 0)
        grad_values = lax.dynamic_update_slice_in_dim(grad_values, value_part, key_start, 0)
        return (grad_query, grad_keys, grad_values)

    start_query = jnp.zeros((row_count, heads_kv, group_size, head_dim), jnp.float32)
    start_keys = jnp.zeros((length, heads_kv, head_dim), jnp.float32)
    return lax.fori_loop(0, block_total, grad_step, (start_query, start_keys, start_keys))


def micro_step(gathered, token_rows, segment_row, grad_in, positions, cosine_table, sine_table):
    gain_attn, w_query, w_key, w_value, gain_mlp, w_gate, w_up, w_out, w_down = gathered
    row_count = token_rows.shape[0]
    heads_kv = w_key.shape[1] // HD
    cos_four = cosine_table[:, None, None, :]
    sin_four = sine_table[:, None, None, :]
    cos_three = cosine_table[:, None, :]
    sin_three = sine_table[:, None, :]
    query_seg = lax.dynamic_slice_in_dim(segment_row, positions[0], row_count, 0)
    gain_first = gain_attn.astype(jnp.float32)
    gain_second = gain_mlp.astype(jnp.float32)
    inputs = token_rows.astype(jnp.float32)
    scale_first = lax.rsqrt(jnp.mean(inputs * inputs, axis=-1, keepdims=True) + epsilon)
    normal_first = inputs * scale_first
    normed = (normal_first * gain_first).astype(jnp.bfloat16)
    query_raw = jnp.dot(normed, w_query, preferred_element_type=jnp.float32).reshape(
        row_count, heads_kv, GROUP, HD
    )
    key_raw = jnp.dot(normed, w_key, preferred_element_type=jnp.float32).reshape(
        row_count, heads_kv, HD
    )
    value_low = (
        jnp.dot(normed, w_value, preferred_element_type=jnp.float32)
        .astype(jnp.bfloat16)
        .reshape(row_count, heads_kv, HD)
    )
    query_low = rotate(query_raw, cos_four, sin_four).astype(jnp.bfloat16)
    key_low = rotate(key_raw, cos_three, sin_three).astype(jnp.bfloat16)
    key_all, value_all = (
        lax.all_gather(key_low, "ctx", axis=0, tiled=True),
        lax.all_gather(value_low, "ctx", axis=0, tiled=True),
    )
    row_top, row_total, out_low = attention_forward(
        query_low, key_all, value_all, segment_row, query_seg, positions
    )
    mixed_low = out_low.reshape(row_count, -1).astype(jnp.bfloat16)
    middle = inputs + head_sum(jnp.dot(mixed_low, w_out, preferred_element_type=jnp.float32))
    scale_second = lax.rsqrt(jnp.mean(middle * middle, axis=-1, keepdims=True) + epsilon)
    normal_second = middle * scale_second
    second = (normal_second * gain_second).astype(jnp.bfloat16)
    gate_part = jnp.dot(second, w_gate, preferred_element_type=jnp.float32)
    upward = jnp.dot(second, w_up, preferred_element_type=jnp.float32)
    sigmoid_gate = jax.nn.sigmoid(gate_part)
    silu_gate = gate_part * sigmoid_gate
    hidden = (silu_gate * upward).astype(jnp.bfloat16)
    result_rows = middle + head_sum(jnp.dot(hidden, w_down, preferred_element_type=jnp.float32))
    output_rows = result_rows.astype(jnp.bfloat16)
    grad_final = grad_in.astype(jnp.float32)
    grad_down = jnp.einsum("tf,td->fd", hidden, grad_in, preferred_element_type=jnp.float32)
    grad_hidden = jnp.einsum("td,fd->tf", grad_in, w_down, preferred_element_type=jnp.float32)
    grad_gate_low = (
        grad_hidden * upward * sigmoid_gate * (1.0 + gate_part * (1.0 - sigmoid_gate))
    ).astype(jnp.bfloat16)
    grad_up_low = (grad_hidden * silu_gate).astype(jnp.bfloat16)
    grad_gate = jnp.einsum("td,tf->df", second, grad_gate_low, preferred_element_type=jnp.float32)
    grad_up = jnp.einsum("td,tf->df", second, grad_up_low, preferred_element_type=jnp.float32)
    grad_second = head_sum(
        jnp.einsum("tf,df->td", grad_gate_low, w_gate, preferred_element_type=jnp.float32)
        + jnp.einsum("tf,df->td", grad_up_low, w_up, preferred_element_type=jnp.float32)
    )
    scaled_second = grad_second * gain_second
    grad_gain_mlp = jnp.sum(grad_second * normal_second, axis=0)
    grad_middle = grad_final + scale_second * (
        scaled_second
        - normal_second * jnp.mean(scaled_second * normal_second, axis=-1, keepdims=True)
    )
    grad_middle_low = grad_middle.astype(jnp.bfloat16)
    grad_out = jnp.einsum(
        "tk,td->kd", mixed_low, grad_middle_low, preferred_element_type=jnp.float32
    )
    grad_mixed = (
        jnp.einsum("td,kd->tk", grad_middle_low, w_out, preferred_element_type=jnp.float32)
        .astype(jnp.bfloat16)
        .reshape(row_count, heads_kv, GROUP, HD)
    )
    row_delta = jnp.transpose(jnp.sum(grad_mixed.astype(jnp.float32) * out_low, axis=-1), (1, 2, 0))
    grad_query_rot, grad_keys, grad_values = attention_backward(
        query_low,
        key_all,
        value_all,
        segment_row,
        query_seg,
        positions,
        row_top,
        row_total,
        grad_mixed,
        row_delta,
    )
    grad_key_mine, grad_value_mine = (
        lax.psum_scatter(
            grad_keys.astype(jnp.bfloat16), "ctx", scatter_dimension=0, tiled=True
        ).astype(jnp.float32),
        lax.psum_scatter(
            grad_values.astype(jnp.bfloat16), "ctx", scatter_dimension=0, tiled=True
        ).astype(jnp.float32),
    )
    grad_query_low = (
        rotate(grad_query_rot, cos_four, -sin_four).astype(jnp.bfloat16).reshape(row_count, -1)
    )
    grad_key_low = (
        rotate(grad_key_mine, cos_three, -sin_three).astype(jnp.bfloat16).reshape(row_count, -1)
    )
    grad_value_low = grad_value_mine.astype(jnp.bfloat16).reshape(row_count, -1)
    grad_query = jnp.einsum("td,tk->dk", normed, grad_query_low, preferred_element_type=jnp.float32)
    grad_key = jnp.einsum("td,tk->dk", normed, grad_key_low, preferred_element_type=jnp.float32)
    grad_value = jnp.einsum("td,tk->dk", normed, grad_value_low, preferred_element_type=jnp.float32)
    grad_normed = head_sum(
        jnp.einsum("tk,dk->td", grad_query_low, w_query, preferred_element_type=jnp.float32)
        + jnp.einsum("tk,dk->td", grad_key_low, w_key, preferred_element_type=jnp.float32)
        + jnp.einsum("tk,dk->td", grad_value_low, w_value, preferred_element_type=jnp.float32)
    )
    scaled_first = grad_normed * gain_first
    grad_gain_attn = jnp.sum(grad_normed * normal_first, axis=0)
    grad_tokens = grad_middle + scale_first * (
        scaled_first - normal_first * jnp.mean(scaled_first * normal_first, axis=-1, keepdims=True)
    )
    gradients = (
        grad_gain_attn,
        grad_query,
        grad_key,
        grad_value,
        grad_gain_mlp,
        grad_gate,
        grad_up,
        grad_out,
        grad_down,
    )
    return (output_rows, grad_tokens, gradients)


def body(
    tokens,
    segments,
    cotangent,
    gain_attn,
    w_query,
    w_key,
    w_value,
    w_out,
    gain_mlp,
    w_gate,
    w_up,
    w_down,
):
    micro_count = tokens.shape[0]
    row_count = tokens.shape[1]
    positions = lax.axis_index("ctx") * row_count + jnp.arange(row_count, dtype=jnp.int32)
    cosine_table, sine_table = rope_tables(positions)
    shards = (gain_attn, w_query, w_key, w_value, gain_mlp, w_gate, w_up, w_out, w_down)
    outputs = []
    token_grads = []
    gathered = weight_gather(shards)
    totals = None
    for micro_index in range(micro_count):
        output_rows, grad_rows, grads_now = micro_step(
            gathered,
            tokens[micro_index],
            segments[micro_index],
            cotangent[micro_index],
            positions,
            cosine_table,
            sine_table,
        )
        outputs.append(output_rows)
        token_grads.append(grad_rows)
        totals = (
            grads_now
            if totals is None
            else tuple(earlier + addend for earlier, addend in zip(totals, grads_now))
        )
    reduced = tuple(
        tensor_piece.astype(jnp.float32)
        for tensor_piece in grad_reduce(tuple(total.astype(jnp.bfloat16) for total in totals))
    )
    return (
        jnp.stack(outputs),
        jnp.stack(token_grads),
        reduced[0],
        reduced[1],
        reduced[2],
        reduced[3],
        reduced[7],
        reduced[4],
        reduced[5],
        reduced[6],
        reduced[8],
    )


def solution(mesh):
    placed = (
        P("fsdp", "ctx", None),
        P("fsdp", None),
        P("fsdp", "ctx", None),
        P(("fsdp", "ctx")),
        P(("fsdp", "ctx"), "tp"),
        P(("fsdp", "ctx"), "tp"),
        P(("fsdp", "ctx"), "tp"),
        P("tp", ("fsdp", "ctx")),
        P(("fsdp", "ctx")),
        P(("fsdp", "ctx"), "tp"),
        P(("fsdp", "ctx"), "tp"),
        P("tp", ("fsdp", "ctx")),
    )
    return jax.shard_map(
        body,
        mesh=mesh,
        in_specs=placed,
        out_specs=(
            P("fsdp", "ctx", None),
            P("fsdp", "ctx", None),
            P(("fsdp", "ctx")),
            P(("fsdp", "ctx"), "tp"),
            P(("fsdp", "ctx"), "tp"),
            P(("fsdp", "ctx"), "tp"),
            P("tp", ("fsdp", "ctx")),
            P(("fsdp", "ctx")),
            P(("fsdp", "ctx"), "tp"),
            P(("fsdp", "ctx"), "tp"),
            P("tp", ("fsdp", "ctx")),
        ),
        check_vma=False,
    )
```

```python
import math

import jax
import jax.numpy as jnp
from jax import lax
from jax.experimental import pallas as pl
from jax.experimental.pallas import tpu as pltpu
from jax.sharding import PartitionSpec as P

HD = 96
GROUP = 2


epsilon = 1e-05
rope_base = 100000.0
negative = -1e30


def rope_tables(positions):
    half_width = HD // 2
    frequency = rope_base ** (-(2.0 * jnp.arange(half_width, dtype=jnp.float32)) / HD)
    angles = positions.astype(jnp.float32)[:, None] * frequency[None, :]
    return (jnp.cos(angles), jnp.sin(angles))


def rotate(vectors, cosine_table, sine_table):
    half_width = vectors.shape[-1] // 2
    former = vectors[..., :half_width]
    latter = vectors[..., half_width:]
    return jnp.concatenate(
        [former * cosine_table - latter * sine_table, latter * cosine_table + former * sine_table],
        axis=-1,
    )


def head_sum(partial_rows):
    return lax.psum(partial_rows.astype(jnp.bfloat16), "tp").astype(jnp.float32)


def weight_gather(shards):
    row_parts = (
        lax.all_gather(shards[0], ("fsdp", "ctx"), axis=0, tiled=True),
        lax.all_gather(shards[1], ("fsdp", "ctx"), axis=0, tiled=True),
        lax.all_gather(shards[2], ("fsdp", "ctx"), axis=0, tiled=True),
        lax.all_gather(shards[3], ("fsdp", "ctx"), axis=0, tiled=True),
        lax.all_gather(shards[4], ("fsdp", "ctx"), axis=0, tiled=True),
        lax.all_gather(shards[5], ("fsdp", "ctx"), axis=0, tiled=True),
        lax.all_gather(shards[6], ("fsdp", "ctx"), axis=0, tiled=True),
    )
    column_parts = (
        lax.all_gather(shards[7], ("fsdp", "ctx"), axis=1, tiled=True),
        lax.all_gather(shards[8], ("fsdp", "ctx"), axis=1, tiled=True),
    )
    return tuple(row_parts) + tuple(column_parts)


def grad_reduce(gradients):
    row_parts = (
        lax.psum_scatter(gradients[0], ("fsdp", "ctx"), scatter_dimension=0, tiled=True),
        lax.psum_scatter(gradients[1], ("fsdp", "ctx"), scatter_dimension=0, tiled=True),
        lax.psum_scatter(gradients[2], ("fsdp", "ctx"), scatter_dimension=0, tiled=True),
        lax.psum_scatter(gradients[3], ("fsdp", "ctx"), scatter_dimension=0, tiled=True),
        lax.psum_scatter(gradients[4], ("fsdp", "ctx"), scatter_dimension=0, tiled=True),
        lax.psum_scatter(gradients[5], ("fsdp", "ctx"), scatter_dimension=0, tiled=True),
        lax.psum_scatter(gradients[6], ("fsdp", "ctx"), scatter_dimension=0, tiled=True),
    )
    column_parts = (
        lax.psum_scatter(gradients[7], ("fsdp", "ctx"), scatter_dimension=1, tiled=True),
        lax.psum_scatter(gradients[8], ("fsdp", "ctx"), scatter_dimension=1, tiled=True),
    )
    return tuple(row_parts) + tuple(column_parts)


def block_scores(queries, key_block, query_seg, positions, key_seg, key_start):
    score_scale = 1.0 / math.sqrt(queries.shape[-1])
    key_positions = key_start + jnp.arange(key_block.shape[0], dtype=jnp.int32)
    allowed = (query_seg[:, None] == key_seg[None, :]) & (
        positions[:, None] >= key_positions[None, :]
    )
    raw_scores = jnp.einsum(
        "qhgd,khd->hgqk", queries, key_block, preferred_element_type=jnp.float32
    )
    return (jnp.where(allowed, raw_scores * score_scale, negative), allowed)


def block_fetch(
    key_all, value_all, segment_row, block_index, block_keys, last_position, first_segment
):
    key_start = block_index * block_keys
    key_block = lax.dynamic_slice_in_dim(key_all, key_start, block_keys, 0)
    value_block = lax.dynamic_slice_in_dim(value_all, key_start, block_keys, 0)
    key_seg = lax.dynamic_slice_in_dim(segment_row, key_start, block_keys, 0)
    needed = (key_start <= last_position) & (key_seg[block_keys - 1] >= first_segment)
    return (key_start, key_block, value_block, key_seg, needed)


def attention_forward(queries, key_all, value_all, segment_row, query_seg, positions):
    row_count, heads_kv, group_size, head_dim = queries.shape
    length = key_all.shape[0]
    block_keys = math.gcd(512, length)
    block_total = length // block_keys
    last_position = positions[row_count - 1]
    first_segment = query_seg[0]

    def stats_step(block_index, state):
        key_start, key_block, value_block, key_seg, needed = block_fetch(
            key_all, value_all, segment_row, block_index, block_keys, last_position, first_segment
        )
        top_old, total_old = state
        scores, allowed = block_scores(queries, key_block, query_seg, positions, key_seg, key_start)
        top_new = jnp.maximum(top_old, jnp.max(scores, axis=-1))
        weights = jnp.where(allowed, jnp.exp(scores - top_new[..., None]), 0.0)
        return (top_new, total_old * jnp.exp(top_old - top_new) + jnp.sum(weights, axis=-1))

    start_top = jnp.full((heads_kv, group_size, row_count), negative, jnp.float32)
    row_top, row_total = lax.fori_loop(
        0, block_total, stats_step, (start_top, jnp.zeros_like(start_top))
    )

    def output_step(block_index, state):
        key_start, key_block, value_block, key_seg, needed = block_fetch(
            key_all, value_all, segment_row, block_index, block_keys, last_position, first_segment
        )
        scores, allowed = block_scores(queries, key_block, query_seg, positions, key_seg, key_start)
        probability = (
            jnp.where(allowed, jnp.exp(scores - row_top[..., None]), 0.0) / row_total[..., None]
        )
        return state + jnp.einsum(
            "hgqk,khd->qhgd",
            probability.astype(jnp.bfloat16),
            value_block,
            preferred_element_type=jnp.float32,
        )

    start_out = jnp.zeros((row_count, heads_kv, group_size, head_dim), jnp.float32)
    out_low = lax.fori_loop(0, block_total, output_step, start_out)
    return (row_top, row_total, out_low)


def attention_backward(
    queries,
    key_all,
    value_all,
    segment_row,
    query_seg,
    positions,
    row_top,
    row_total,
    grad_mixed,
    row_delta,
):
    row_count, heads_kv, group_size, head_dim = queries.shape
    length = key_all.shape[0]
    block_keys = math.gcd(512, length)
    block_total = length // block_keys
    last_position = positions[row_count - 1]
    first_segment = query_seg[0]
    score_scale = 1.0 / math.sqrt(head_dim)

    def grad_step(block_index, state):
        key_start, key_block, value_block, key_seg, needed = block_fetch(
            key_all, value_all, segment_row, block_index, block_keys, last_position, first_segment
        )
        grad_query, grad_keys, grad_values = state
        scores, allowed = block_scores(queries, key_block, query_seg, positions, key_seg, key_start)
        probability = (
            jnp.where(allowed, jnp.exp(scores - row_top[..., None]), 0.0) / row_total[..., None]
        )
        grad_prob = jnp.einsum(
            "qhgd,khd->hgqk", grad_mixed, value_block, preferred_element_type=jnp.float32
        )
        grad_score = (probability * (grad_prob - row_delta[..., None]) * score_scale).astype(
            jnp.bfloat16
        )
        grad_query = grad_query + jnp.einsum(
            "hgqk,khd->qhgd", grad_score, key_block, preferred_element_type=jnp.float32
        )
        key_part = jnp.einsum(
            "hgqk,qhgd->khd", grad_score, queries, preferred_element_type=jnp.float32
        )
        value_part = jnp.einsum(
            "hgqk,qhgd->khd",
            probability.astype(jnp.bfloat16),
            grad_mixed,
            preferred_element_type=jnp.float32,
        )
        grad_keys = lax.dynamic_update_slice_in_dim(grad_keys, key_part, key_start, 0)
        grad_values = lax.dynamic_update_slice_in_dim(grad_values, value_part, key_start, 0)
        return (grad_query, grad_keys, grad_values)

    start_query = jnp.zeros((row_count, heads_kv, group_size, head_dim), jnp.float32)
    start_keys = jnp.zeros((length, heads_kv, head_dim), jnp.float32)
    return lax.fori_loop(0, block_total, grad_step, (start_query, start_keys, start_keys))


def micro_step(gathered, token_rows, segment_row, grad_in, positions, cosine_table, sine_table):
    gain_attn, w_query, w_key, w_value, gain_mlp, w_gate, w_up, w_out, w_down = gathered
    row_count = token_rows.shape[0]
    heads_kv = w_key.shape[1] // HD
    cos_four = cosine_table[:, None, None, :]
    sin_four = sine_table[:, None, None, :]
    cos_three = cosine_table[:, None, :]
    sin_three = sine_table[:, None, :]
    query_seg = lax.dynamic_slice_in_dim(segment_row, positions[0], row_count, 0)
    gain_first = gain_attn.astype(jnp.float32)
    gain_second = gain_mlp.astype(jnp.float32)
    inputs = token_rows.astype(jnp.float32)
    scale_first = lax.rsqrt(jnp.mean(inputs * inputs, axis=-1, keepdims=True) + epsilon)
    normal_first = inputs * scale_first
    normed = (normal_first * gain_first).astype(jnp.bfloat16)
    query_raw = jnp.dot(normed, w_query, preferred_element_type=jnp.float32).reshape(
        row_count, heads_kv, GROUP, HD
    )
    key_raw = jnp.dot(normed, w_key, preferred_element_type=jnp.float32).reshape(
        row_count, heads_kv, HD
    )
    value_low = (
        jnp.dot(normed, w_value, preferred_element_type=jnp.float32)
        .astype(jnp.bfloat16)
        .reshape(row_count, heads_kv, HD)
    )
    query_low = rotate(query_raw, cos_four, sin_four).astype(jnp.bfloat16)
    key_low = rotate(key_raw, cos_three, sin_three).astype(jnp.bfloat16)
    key_all, value_all = (
        lax.all_gather(key_low, "ctx", axis=0, tiled=True),
        lax.all_gather(value_low, "ctx", axis=0, tiled=True),
    )
    row_top, row_total, out_low = attention_forward(
        query_low, key_all, value_all, segment_row, query_seg, positions
    )
    mixed_low = out_low.reshape(row_count, -1).astype(jnp.bfloat16)
    middle = inputs + head_sum(jnp.dot(mixed_low, w_out, preferred_element_type=jnp.float32))
    scale_second = lax.rsqrt(jnp.mean(middle * middle, axis=-1, keepdims=True) + epsilon)
    normal_second = middle * scale_second
    second = (normal_second * gain_second).astype(jnp.bfloat16)
    gate_part = jnp.dot(second, w_gate, preferred_element_type=jnp.float32)
    upward = jnp.dot(second, w_up, preferred_element_type=jnp.float32)
    sigmoid_gate = jax.nn.sigmoid(gate_part)
    silu_gate = gate_part * sigmoid_gate
    hidden = (silu_gate * upward).astype(jnp.bfloat16)
    result_rows = middle + head_sum(jnp.dot(hidden, w_down, preferred_element_type=jnp.float32))
    output_rows = result_rows.astype(jnp.bfloat16)
    grad_final = grad_in.astype(jnp.float32)
    grad_down = jnp.einsum("tf,td->fd", hidden, grad_in, preferred_element_type=jnp.float32)
    grad_hidden = jnp.einsum("td,fd->tf", grad_in, w_down, preferred_element_type=jnp.float32)
    grad_gate_low = (
        grad_hidden * upward * sigmoid_gate * (1.0 + gate_part * (1.0 - sigmoid_gate))
    ).astype(jnp.bfloat16)
    grad_up_low = (grad_hidden * silu_gate).astype(jnp.bfloat16)
    grad_gate = jnp.einsum("td,tf->df", second, grad_gate_low, preferred_element_type=jnp.float32)
    grad_up = jnp.einsum("td,tf->df", second, grad_up_low, preferred_element_type=jnp.float32)
    grad_second = head_sum(
        jnp.einsum("tf,df->td", grad_gate_low, w_gate, preferred_element_type=jnp.float32)
        + jnp.einsum("tf,df->td", grad_up_low, w_up, preferred_element_type=jnp.float32)
    )
    scaled_second = grad_second * gain_second
    grad_gain_mlp = jnp.sum(grad_second * normal_second, axis=0)
    grad_middle = grad_final + scale_second * (
        scaled_second
        - normal_second * jnp.mean(scaled_second * normal_second, axis=-1, keepdims=True)
    )
    grad_middle_low = grad_middle.astype(jnp.bfloat16)
    grad_out = jnp.einsum(
        "tk,td->kd", mixed_low, grad_middle_low, preferred_element_type=jnp.float32
    )
    grad_mixed = (
        jnp.einsum("td,kd->tk", grad_middle_low, w_out, preferred_element_type=jnp.float32)
        .astype(jnp.bfloat16)
        .reshape(row_count, heads_kv, GROUP, HD)
    )
    row_delta = jnp.transpose(jnp.sum(grad_mixed.astype(jnp.float32) * out_low, axis=-1), (1, 2, 0))
    grad_query_rot, grad_keys, grad_values = attention_backward(
        query_low,
        key_all,
        value_all,
        segment_row,
        query_seg,
        positions,
        row_top,
        row_total,
        grad_mixed,
        row_delta,
    )
    grad_key_mine, grad_value_mine = (
        lax.psum_scatter(
            grad_keys.astype(jnp.bfloat16), "ctx", scatter_dimension=0, tiled=True
        ).astype(jnp.float32),
        lax.psum_scatter(
            grad_values.astype(jnp.bfloat16), "ctx", scatter_dimension=0, tiled=True
        ).astype(jnp.float32),
    )
    grad_query_low = (
        rotate(grad_query_rot, cos_four, -sin_four).astype(jnp.bfloat16).reshape(row_count, -1)
    )
    grad_key_low = (
        rotate(grad_key_mine, cos_three, -sin_three).astype(jnp.bfloat16).reshape(row_count, -1)
    )
    grad_value_low = grad_value_mine.astype(jnp.bfloat16).reshape(row_count, -1)
    grad_query = jnp.einsum("td,tk->dk", normed, grad_query_low, preferred_element_type=jnp.float32)
    grad_key = jnp.einsum("td,tk->dk", normed, grad_key_low, preferred_element_type=jnp.float32)
    grad_value = jnp.einsum("td,tk->dk", normed, grad_value_low, preferred_element_type=jnp.float32)
    grad_normed = head_sum(
        jnp.einsum("tk,dk->td", grad_query_low, w_query, preferred_element_type=jnp.float32)
        + jnp.einsum("tk,dk->td", grad_key_low, w_key, preferred_element_type=jnp.float32)
        + jnp.einsum("tk,dk->td", grad_value_low, w_value, preferred_element_type=jnp.float32)
    )
    scaled_first = grad_normed * gain_first
    grad_gain_attn = jnp.sum(grad_normed * normal_first, axis=0)
    grad_tokens = grad_middle + scale_first * (
        scaled_first - normal_first * jnp.mean(scaled_first * normal_first, axis=-1, keepdims=True)
    )
    gradients = (
        grad_gain_attn,
        grad_query,
        grad_key,
        grad_value,
        grad_gain_mlp,
        grad_gate,
        grad_up,
        grad_out,
        grad_down,
    )
    return (output_rows, grad_tokens, gradients)


def body(
    tokens,
    segments,
    cotangent,
    gain_attn,
    w_query,
    w_key,
    w_value,
    w_out,
    gain_mlp,
    w_gate,
    w_up,
    w_down,
):
    micro_count = tokens.shape[0]
    row_count = tokens.shape[1]
    positions = lax.axis_index("ctx") * row_count + jnp.arange(row_count, dtype=jnp.int32)
    cosine_table, sine_table = rope_tables(positions)
    shards = (gain_attn, w_query, w_key, w_value, gain_mlp, w_gate, w_up, w_out, w_down)
    outputs = []
    token_grads = []
    gathered = weight_gather(shards)
    totals = None
    for micro_index in range(micro_count):
        output_rows, grad_rows, grads_now = micro_step(
            gathered,
            tokens[micro_index],
            segments[micro_index],
            cotangent[micro_index],
            positions,
            cosine_table,
            sine_table,
        )
        outputs.append(output_rows)
        token_grads.append(grad_rows)
        totals = (
            grads_now
            if totals is None
            else tuple(earlier + addend for earlier, addend in zip(totals, grads_now))
        )
    reduced = tuple(
        tensor_piece.astype(jnp.float32)
        for tensor_piece in grad_reduce(tuple(total.astype(jnp.bfloat16) for total in totals))
    )
    return (
        jnp.stack(outputs),
        jnp.stack(token_grads),
        reduced[0],
        reduced[1],
        reduced[2],
        reduced[3],
        reduced[7],
        reduced[4],
        reduced[5],
        reduced[6],
        reduced[8],
    )


MESH = pl.DeviceIdType.MESH
UNIT = 384
ROWS = 512
SPAN = 256
WIDE = 1536
F32 = jnp.float32
BF16 = jnp.bfloat16
NT = (((1,), (1,)), ((), ()))
TN = (((0,), (0,)), ((), ()))


def dot_nn(a, b):
    return jnp.dot(a, b, preferred_element_type=F32)


def dot_nt(a, b):
    return lax.dot_general(a, b, NT, preferred_element_type=F32)


def dot_tn(a, b):
    return lax.dot_general(a, b, TN, preferred_element_type=F32)


class Place:
    def __init__(self):
        f, c, t = (lax.axis_index(axis) for axis in ("fsdp", "ctx", "tp"))
        self.f, self.c, self.t = f, c, t
        self.y, self.k = lax.div(c, 2), lax.rem(c, 2)
        self.oy, self.ok = 1 - self.y, 1 - self.k
        self.half = lax.div(f, 2)
        self.inner = (f == 1) | (f == 2)
        self.edge = (f == 0) | (f == 3)
        self.near_f = f + 1 - 2 * lax.rem(f, 2)
        self.mid_f = 2 - self.half
        self.far_f = 3 - 3 * self.half
        self.near = (self.near_f, c, t)
        self.mid = (self.mid_f, c, t)
        self.far = (self.far_f, c, t)
        self.ypeer = (f, c + 2 - 4 * self.y, t)
        self.sib = (f, c + 1 - 2 * self.k, t)
        self.xpeer = (f, c, 1 - t)

    def barrier(self):
        sem = pltpu.get_barrier_semaphore()
        others = [(lax.rem(self.f + step, 4), self.c, self.t) for step in (1, 2, 3)]
        others += [self.ypeer, self.sib, self.xpeer]
        for other in others:
            pl.semaphore_signal(sem, inc=1, device_id=other, device_id_type=MESH)
        pl.semaphore_wait(sem, len(others))


def remote(src, dst, send, recv, device):
    return pltpu.make_async_remote_copy(
        src_ref=src,
        dst_ref=dst,
        send_sem=send,
        recv_sem=recv,
        device_id=device,
        device_id_type=MESH,
    )


def lanes(rows, columns):
    return lax.broadcasted_iota(jnp.int32, (rows, columns), 1)


def unpack_heads(x):
    lane = lanes(x.shape[0], 128)
    one, two, three = x[:, :128], x[:, 128:256], x[:, 256:]
    heads = (
        one,
        pltpu.roll(jnp.where(lane < 64, two, one), 32, 1),
        pltpu.roll(jnp.where(lane < 32, three, two), 64, 1),
        pltpu.roll(three, 96, 1),
    )
    return [jnp.where(lane < HD, head, 0.0) for head in heads]


def pack_heads(heads):
    lane = lanes(heads[0].shape[0], 128)
    second = pltpu.roll(heads[1], 96, 1)
    third = pltpu.roll(heads[2], 64, 1)
    fourth = pltpu.roll(heads[3], 32, 1)
    return jnp.concatenate(
        [
            jnp.where(lane < 96, heads[0], second),
            jnp.where(lane < 64, second, third),
            jnp.where(lane < 32, third, fourth),
        ],
        axis=1,
    )


def turn(x, cosine, sine):
    lane = lax.rem(lanes(x.shape[0], UNIT), HD)
    swapped = jnp.where(lane < HD // 2, pltpu.roll(x, UNIT - HD // 2, 1), pltpu.roll(x, HD // 2, 1))
    return x * cosine + swapped * sine


def transpose_into(dst, src):
    @pl.loop(0, WIDE // 128)
    def _(i):
        at = pl.multiple_of(i * 128, 128)
        dst[pl.ds(at, 128), :] = src[:, pl.ds(at, 128)].astype(F32).T.astype(BF16)


def weight(buf, slot, lo, hi):
    return buf[slot, :, :, :, :, lo:hi].reshape(WIDE, hi - lo)


def allowed_keys(low_row, high_row):
    row = lax.broadcasted_iota(jnp.int32, (4 * SPAN, SPAN), 0)
    return (row >= low_row) & (row <= high_row)


def forward_kernel(
    packed,
    gains,
    tokens,
    cot,
    cosine,
    sine,
    low,
    high,
    w_all,
    gain_rows,
    at_out,
    bt_out,
    et_out,
    qh,
    kh,
    vh,
    lse,
    ob,
    x2,
    gate,
    up,
    hidden,
    out_part,
    a_buf,
    gw,
    wbuf,
    kvx,
    oh,
    xs,
    xr,
    acc,
    z_send,
    z_recv,
    y_send,
    y_recv,
    c_send,
    c_recv,
    kv_send,
    kv_recv,
    x_send,
    x_recv,
    own_sem,
    load_sem,
):
    me = Place()
    f, y, k = me.f, me.y, me.k
    units = packed.shape[0]
    groups = gate.shape[0]
    scale = 1.0 / math.sqrt(HD)

    own = pltpu.make_async_copy(packed, w_all.at[:, f, y, k], own_sem.at[0])
    own.start()
    own_gain = pltpu.make_async_copy(gains, gw.at[0, f, y, k], own_sem.at[1])
    own_gain.start()
    me.barrier()

    def z_start(src, buf, j, s):
        for i, device in enumerate((me.near, me.mid)):
            remote(src, buf.at[j, f, y, k], z_send.at[s, i], z_recv.at[s], device).start()

    def hand_on(buf, j, s):
        part = buf.at[j, pl.ds(2 - 2 * me.half, 2), y, k]
        return remote(part, part, z_send.at[s, 2], z_recv.at[s], me.near)

    def y_copy(buf, j, s):
        part = buf.at[j, :, y, k]
        return remote(part, part, y_send.at[s], y_recv.at[s], me.ypeer)

    def core_copy(buf, j, s):
        part = buf.at[j, :, :, k]
        return remote(part, part, c_send.at[s], c_recv.at[s], me.sib)

    def stage_y(buf, j, s):
        three = buf.at[j, pl.ds(0, 3), y, k]
        remote(three, three, z_send.at[s, 0], z_recv.at[s], me.near).wait_recv()

        @pl.when(me.inner)
        def _():
            hand_on(buf, j, s).start()

        y_copy(buf, j, s).start()

    def stage_core(buf, j, s):
        y_copy(buf, j, s).wait_recv()
        core_copy(buf, j, s).start()

    def stage_done(buf, j, s):
        core_copy(buf, j, s).wait_recv()

    def sends_done(buf, j, s):
        for i, device in enumerate((me.near, me.mid)):
            remote(buf.at[j, f, y, k], buf.at[j, f, y, k], z_send.at[s, i], z_recv.at[s], device).wait_send()

        @pl.when(me.inner)
        def _():
            hand_on(buf, j, s).wait_send()

        y_copy(buf, j, s).wait_send()
        core_copy(buf, j, s).wait_send()

    ahead = 4

    def step(u):
        def guarded(low_ok, high_ok, act):
            if isinstance(u, int):
                if low_ok and high_ok:
                    act()
            else:
                pl.when(high_ok)(act)

        guarded(True, u + ahead < units, lambda: z_start(packed.at[u + ahead], w_all, u + ahead, u + ahead))
        guarded(True, u < units, lambda: stage_y(w_all, u, u))
        guarded(not isinstance(u, int) or u >= 1, u - 1 < units, lambda: stage_core(w_all, u - 1, u - 1))
        guarded(not isinstance(u, int) or u >= 2, u - 2 < units, lambda: stage_done(w_all, u - 2, u - 2))

    def load(u, slot, side):
        return pltpu.make_async_copy(
            w_all.at[u],
            wbuf.at[slot, :, :, :, :, pl.ds(side * UNIT, UNIT)],
            load_sem.at[slot, side],
        )

    z_start(gains, gw, 0, units)
    for u in range(ahead):
        z_start(packed.at[u], w_all, u, u)
    own.wait()
    own_gain.wait()
    stage_y(gw, 0, units)
    transpose_into(et_out, cot)
    stage_core(gw, 0, units)
    stage_done(gw, 0, units)
    gain_rows[...] = gw[0].reshape(WIDE, 128).astype(F32).T[:8, :]
    step(0)

    @pl.loop(0, ROWS // 64)
    def _(i):
        rows = pl.ds(pl.multiple_of(i * 64, 64), 64)
        x = tokens[rows, :].astype(F32)
        r = lax.rsqrt(jnp.mean(x * x, axis=-1, keepdims=True) + epsilon)
        a_buf[rows, :] = (x * r * gain_rows[0:1, :]).astype(BF16)

    step(1)
    transpose_into(at_out, a_buf)
    step(2)
    load(0, 0, 0).start()
    step(3)
    load(1, 0, 1).start()
    load(0, 0, 0).wait()
    for s in range(2):
        rows = pl.ds(s * SPAN, SPAN)
        key = turn(dot_nn(a_buf[rows, :], weight(wbuf, 0, 0, UNIT)), cosine[...], sine[...])
        kvx[y, k, rows, 0:UNIT] = key.astype(BF16)
    load(1, 0, 1).wait()
    kvx[y, k, :, UNIT:] = dot_nn(a_buf[...], weight(wbuf, 0, UNIT, 2 * UNIT)).astype(BF16)

    def kv_copy(stage):
        part = kvx.at[y, k] if stage == 0 else kvx.at[:, k]
        return remote(part, part, kv_send.at[stage], kv_recv.at[stage], me.ypeer if stage == 0 else me.sib)

    kv_copy(0).start()
    step(4)
    load(2, 1, 0).start()
    step(5)
    load(3, 1, 1).start()
    load(2, 1, 0).wait()
    load(3, 1, 1).wait()
    for side in range(2):
        for s in range(2):
            rows = pl.ds(s * SPAN, SPAN)
            columns = slice(side * UNIT, (side + 1) * UNIT)
            query = dot_nn(a_buf[rows, :], weight(wbuf, 1, side * UNIT, (side + 1) * UNIT))
            query = turn(query, cosine[...], sine[...])
            for i, head in enumerate(unpack_heads(query)):
                qh[s * 8 + side * 4 + i] = head.astype(BF16)
    kv_copy(0).wait_recv()
    kv_copy(1).start()
    step(6)
    load(4, 0, 0).start()
    step(7)
    load(5, 0, 1).start()
    kv_copy(1).wait_recv()

    @pl.loop(0, 8)
    def _(i):
        s, c = lax.div(i, 4), lax.rem(i, 4)
        block = kvx[lax.div(c, 2), lax.rem(c, 2), pl.ds(pl.multiple_of(s * SPAN, SPAN), SPAN), :]
        at = pl.ds(pl.multiple_of(c * SPAN, SPAN), SPAN)
        for g, head in enumerate(unpack_heads(block[:, :UNIT].astype(F32))):
            kh[s * 4 + g, at, :] = head.astype(BF16)
        for g, head in enumerate(unpack_heads(block[:, UNIT:].astype(F32))):
            vh[s * 4 + g, at, :] = head.astype(BF16)

    def attend(i):
        s, h = lax.div(i, 8), lax.rem(i, 8)
        g = s * 4 + lax.div(h, 2)
        scores = dot_nt(kh[g], qh[i]) * scale
        scores = jnp.where(allowed_keys(low[s], high[...]), scores, negative)
        top = jnp.max(scores, axis=0, keepdims=True)
        p = jnp.exp(scores - top)
        total = jnp.sum(p, axis=0, keepdims=True)
        lse[i] = jnp.broadcast_to(top + jnp.log(total), (8, SPAN))
        oh[h] = (dot_tn(vh[g], p.astype(BF16)) / total).T

    def gather_heads(s):
        for side in range(2):
            ob[s * SPAN : (s + 1) * SPAN, side * UNIT : (side + 1) * UNIT] = pack_heads(
                [oh[side * 4 + i] for i in range(4)]
            ).astype(BF16)

    pl.loop(0, 8)(attend)
    gather_heads(0)
    step(8)
    pl.loop(8, 16)(attend)
    gather_heads(1)
    load(4, 0, 0).wait()
    load(5, 0, 1).wait()

    def x_copy(r):
        rows = pl.ds(pl.multiple_of(r * 128, 128), 128)
        return remote(xs.at[rows], xr.at[rows], x_send.at[r], x_recv.at[r], me.xpeer)

    for r in range(4):
        rows = slice(r * 128, (r + 1) * 128)
        xs[rows, :] = dot_nt(ob[rows, :], weight(wbuf, 0, 0, 2 * UNIT)).astype(BF16)
        x_copy(r).start()
    for u in range(9, 13):
        step(u)

    @pl.loop(0, 4)
    def _(r):
        x_copy(r).wait()
        rows = pl.ds(pl.multiple_of(r * 128, 128), 128)
        x = tokens[rows, :].astype(F32) + (xs[rows, :].astype(F32) + xr[rows, :].astype(F32))
        x2[rows, :] = x
        r2 = lax.rsqrt(jnp.mean(x * x, axis=-1, keepdims=True) + epsilon)
        a_buf[rows, :] = (x * r2 * gain_rows[1:2, :]).astype(BF16)

    acc[...] = jnp.zeros_like(acc)

    def feed(n, slot):
        for side in range(2):
            load(6 + 2 * n + side, slot, side).wait()
        gate_n = dot_nn(a_buf[...], weight(wbuf, slot, 0, 256))
        up_n = dot_nn(a_buf[...], weight(wbuf, slot, 256, 512))
        hidden_n = (gate_n * jax.nn.sigmoid(gate_n) * up_n).astype(BF16)
        gate[n] = gate_n.astype(BF16)
        up[n] = up_n.astype(BF16)
        hidden[n] = hidden_n
        acc[...] += dot_nt(hidden_n, weight(wbuf, slot, 512, 768))

    @pl.loop(0, groups)
    def _(n):
        first = 6 + 2 * n
        slot = lax.rem(n, 2)

        @pl.when(n >= 3)
        def _():
            step(first + 2)
            step(first + 3)

        for side in range(2):
            load(first + side, slot, side).start()

        @pl.when(n == 0)
        def _():
            transpose_into(bt_out, a_buf)
            step(13)

        feed(n, slot)

    out_part[...] = acc[...].astype(BF16)
    kv_copy(0).wait_send()
    kv_copy(1).wait_send()
    sends_done(gw, 0, units)

    @pl.loop(0, units)
    def _(u):
        sends_done(w_all, u, u)


def rope_inputs(row_count):
    positions = lax.axis_index("ctx") * row_count + jnp.arange(row_count, dtype=jnp.int32)
    cosine_table, sine_table = rope_tables(positions)
    cosine = jnp.tile(cosine_table, (1, 2 * UNIT // HD))
    sine = jnp.tile(jnp.concatenate([-sine_table, sine_table], axis=1), (1, UNIT // HD))
    return positions, cosine, sine


def pack_weights(w_query, w_key, w_value, w_out, w_gate, w_up, w_down):
    depth = w_query.shape[0]
    groups = w_gate.shape[1] // 256
    fed = jnp.concatenate(
        [part.reshape(depth, groups, 256) for part in (w_gate, w_up, w_down.T)], axis=2
    ).reshape(depth, groups * 2 * UNIT)
    flat = jnp.concatenate([w_key, w_value, w_query, w_out.T, fed], axis=1)
    return jnp.transpose(flat.reshape(depth, flat.shape[1] // UNIT, UNIT), (1, 0, 2))


def pack_gains(gain_attn, gain_mlp):
    return jnp.pad(jnp.stack([gain_attn, gain_mlp], axis=1), ((0, 0), (0, 126)))


def vmem(shape, dtype):
    return pltpu.VMEM(shape, dtype)


def call_forward(packed, gains, tokens, cot, cosine, sine, low, high):
    units, depth = packed.shape[0], packed.shape[1]
    groups = (units - 6) // 2
    struct = jax.ShapeDtypeStruct
    any_spec = pl.BlockSpec(memory_space=pl.ANY)
    vmem_spec = pl.BlockSpec(memory_space=pltpu.VMEM)
    block = (4, 2, 2, depth)
    dma = pltpu.SemaphoreType.DMA
    return pl.pallas_call(
        forward_kernel,
        out_shape=(
            struct((units,) + block + (UNIT,), BF16),
            struct((8, WIDE), F32),
            struct((WIDE, ROWS), BF16),
            struct((WIDE, ROWS), BF16),
            struct((WIDE, ROWS), BF16),
            struct((16, SPAN, 128), BF16),
            struct((8, 4 * SPAN, 128), BF16),
            struct((8, 4 * SPAN, 128), BF16),
            struct((16, 8, SPAN), F32),
            struct((ROWS, 2 * UNIT), BF16),
            struct((ROWS, WIDE), F32),
            struct((groups, ROWS, 256), BF16),
            struct((groups, ROWS, 256), BF16),
            struct((groups, ROWS, 256), BF16),
            struct((ROWS, WIDE), BF16),
        ),
        in_specs=[any_spec, any_spec] + [vmem_spec] * 6,
        out_specs=(any_spec,) + (vmem_spec,) * 14,
        scratch_shapes=[
            vmem((ROWS, WIDE), BF16),
            vmem((1,) + block + (128,), BF16),
            vmem((2,) + block + (2 * UNIT,), BF16),
            vmem((2, 2, ROWS, 2 * UNIT), BF16),
            vmem((8, SPAN, 128), F32),
            vmem((ROWS, WIDE), BF16),
            vmem((ROWS, WIDE), BF16),
            vmem((ROWS, WIDE), F32),
            dma((units + 1, 3)),
            dma((units + 1,)),
            dma((units + 1,)),
            dma((units + 1,)),
            dma((units + 1,)),
            dma((units + 1,)),
            dma((2,)),
            dma((2,)),
            dma((4,)),
            dma((4,)),
            dma((2,)),
            dma((2, 2)),
        ],
        compiler_params=pltpu.CompilerParams(
            collective_id=1, has_side_effects=True, vmem_limit_bytes=60 << 20
        ),
        name="forward",
    )(packed, gains, tokens, cot, cosine, sine, low, high)


RING = 5


def backward_kernel(
    w_all,
    gain_rows,
    tokens,
    cot,
    at_in,
    bt_in,
    et_in,
    gate,
    up,
    hidden,
    out_part,
    qh,
    kh,
    vh,
    lse,
    ob,
    x2,
    cosine,
    sine,
    low,
    high,
    output,
    grad_tokens,
    grads,
    gain_grads,
    eb,
    et,
    bt,
    dxt,
    dg,
    du,
    gu,
    hbuf,
    wbuf,
    part,
    r1,
    r2,
    r3,
    acc,
    xs,
    xr,
    doh,
    dqh,
    dkh,
    dvh,
    dkv,
    rc,
    ry,
    dqb,
    dkvb,
    gacc,
    gp,
    g1,
    g2,
    g3,
    gs,
    c_send,
    c_recv,
    y_send,
    y_recv,
    za_send,
    za_recv,
    zb_send,
    zb_recv,
    c_cred,
    y_cred,
    z_cred,
    x_send,
    x_recv,
    x_cred,
    kv_send,
    kv_recv,
    g_send,
    g_recv,
    load_sem,
    w_sem,
    h_sem,
    gout,
    out_sem,
):
    me = Place()
    f, y, k = me.f, me.y, me.k
    units = grads.shape[0]
    groups = gate.shape[0]
    scale = 1.0 / math.sqrt(HD)

    def local(src, dst, i):
        return pltpu.make_async_copy(src, dst, load_sem.at[i])

    def load(u, slot, side):
        return pltpu.make_async_copy(
            w_all.at[u],
            wbuf.at[slot, :, :, :, :, pl.ds(side * UNIT, UNIT)],
            w_sem.at[slot, side],
        )

    def load_pair(u, slot):
        for side in range(2):
            load(u + side, slot, side).start()

    def wait_pair(u, slot):
        for side in range(2):
            load(u + side, slot, side).wait()

    def gu_copies(n, slot):
        return [
            pltpu.make_async_copy(src.at[n], gu.at[slot, i], h_sem.at[slot, i])
            for i, src in enumerate((gate, up))
        ]

    def h_copy(n, slot):
        return pltpu.make_async_copy(hidden.at[n], hbuf.at[slot], h_sem.at[slot, 2])

    load_pair(6, 0)
    for copy in gu_copies(0, 0):
        copy.start()
    local(cot, eb, 0).start()
    local(bt_in, bt, 1).start()
    local(et_in, et, 2).start()
    h_copy(0, 0).start()
    me.barrier()

    class Unit:
        def __init__(self, r):
            self.r = r
            self.ring = True
            self.s = lax.rem(r, RING)
            self.first = r < RING
            self.last = r + RING >= units
            slot = lax.rem(lax.div(r, 2), 2)
            columns = pl.ds(pl.multiple_of(lax.rem(r, 2) * UNIT, 128), UNIT)
            self.other = part.at[slot, :, :, me.ok, :, columns]
            self.mine = part.at[slot, :, :, k, :, columns]
            self.r1, self.r2, self.r3 = r1.at[self.s], r2.at[self.s], r3.at[self.s]

    class GainUnit:
        def __init__(self):
            self.r = units
            self.ring = False
            self.other = gp.at[:, :, me.ok]
            self.mine = gp.at[:, :, k]
            self.r1, self.r2, self.r3 = g1, g2, g3

    def credit(unit, sem):
        if unit.ring:

            @pl.when(jnp.logical_not(unit.first))
            def _():
                pl.semaphore_wait(sem, 1)

    def give(unit, sem, device):
        if unit.ring:

            @pl.when(jnp.logical_not(unit.last))
            def _():
                pl.semaphore_signal(sem, inc=1, device_id=device, device_id_type=MESH)

    def core_copy(unit):
        return remote(unit.other, unit.r1, c_send.at[unit.r], c_recv.at[unit.r], me.sib)

    def y_copy(unit):
        return remote(unit.r1.at[:, me.oy], unit.r2, y_send.at[unit.r], y_recv.at[unit.r], me.ypeer)

    def za_copy(unit):
        return remote(
            unit.r2.at[pl.ds(1 - me.half, 3)],
            unit.r3.at[pl.ds(0, 3)],
            za_send.at[unit.r],
            za_recv.at[unit.r],
            me.near,
        )

    def zb_copy(unit, i):
        owner, at, device = (
            (me.near_f, 0, me.near),
            (me.mid_f, 3, me.mid),
            (me.far_f, 1, me.far),
        )[i]
        return remote(
            unit.r2.at[owner],
            unit.r3.at[at],
            zb_send.at[unit.r, i],
            zb_recv.at[unit.r, min(i, 1)],
            device,
        )

    def stage_core(unit):
        credit(unit, c_cred)
        core_copy(unit).start()

    def stage_y(unit):
        core_copy(unit).wait_recv()
        unit.r1[...] = unit.r1[...] + unit.mine[...]
        core_copy(unit).wait_send()
        credit(unit, y_cred)
        y_copy(unit).start()

    def stage_z(unit):
        y_copy(unit).wait_recv()
        unit.r2[...] = unit.r2[...] + unit.r1[:, y]
        y_copy(unit).wait_send()
        give(unit, c_cred, me.sib)

        @pl.when(me.edge)
        def _():
            credit(unit, z_cred.at[0])
            za_copy(unit).start()

    def stage_zb(unit):
        @pl.when(me.inner)
        def _():
            za_copy(unit).wait_recv()
            for owner in (me.mid_f, me.far_f):
                unit.r2[owner] = unit.r2[owner] + unit.r3[owner - (1 - me.half)]
            for i in range(3):
                credit(unit, z_cred.at[i])
                zb_copy(unit, i).start()

    def stage_end(unit, store):
        zb_copy(unit, 1).wait_recv()

        @pl.when(me.edge)
        def _():
            zb_copy(unit, 0).wait_recv()

        one = jnp.where(me.edge, 0, f - (1 - me.half))
        two = jnp.where(me.edge, 1, 3)
        store(unit.r2[f].astype(F32) + unit.r3[one].astype(F32) + unit.r3[two].astype(F32))

        @pl.when(me.edge)
        def _():
            za_copy(unit).wait_send()
            give(unit, z_cred.at[0], me.near)
            give(unit, z_cred.at[2], me.mid)

        @pl.when(me.inner)
        def _():
            for i in range(3):
                zb_copy(unit, i).wait_send()
            give(unit, z_cred.at[0], me.near)
            give(unit, z_cred.at[1], me.mid)

        give(unit, y_cred, me.ypeer)

    def out_copy(i):
        slot = lax.rem(i, 2)
        return pltpu.make_async_copy(gout.at[slot], grads.at[i], out_sem.at[slot])

    def step(r):
        def guarded(lag, act):
            i = r - lag
            if isinstance(r, int):
                if 0 <= i < units:
                    act(i)
            else:
                pl.when((i >= 0) & (i < units))(lambda: act(i))

        def end(i):
            slot = lax.rem(i, 2)

            def store(total):
                @pl.when(i >= 2)
                def _():
                    out_copy(i - 2).wait()

                gout[slot] = total
                out_copy(i).start()

            stage_end(Unit(i), store)

        guarded(0, lambda i: stage_core(Unit(i)))
        guarded(1, lambda i: stage_y(Unit(i)))
        guarded(2, lambda i: stage_z(Unit(i)))
        guarded(3, lambda i: stage_zb(Unit(i)))
        guarded(4, end)

    depth = r2.shape[2]

    def put(pair, columns, value):
        part[lax.rem(pair, 2), :, :, :, :, columns] = value.astype(BF16).reshape(4, 2, 2, depth, 256)

    def feed_grads(n, pair):
        slot = lax.rem(n, 2)
        h_copy(n, slot).wait()
        put(pair, slice(0, 256), dot_nn(bt[...], dg[n]))
        put(pair, slice(256, 512), dot_nn(bt[...], du[n]))
        put(pair, slice(512, 768), dot_nn(et[...], hbuf[slot]))

        @pl.when(n + 1 < groups)
        def _():
            h_copy(n + 1, 1 - slot).start()

    local(cot, eb, 0).wait()
    local(bt_in, bt, 1).wait()
    local(et_in, et, 2).wait()
    acc[...] = jnp.zeros_like(acc)

    @pl.loop(0, groups)
    def _(n):
        slot = lax.rem(n, 2)

        @pl.when(n + 1 < groups)
        def _():
            load_pair(6 + 2 * (n + 1), 1 - slot)
            for copy in gu_copies(n + 1, 1 - slot):
                copy.start()

        wait_pair(6 + 2 * n, slot)
        for copy in gu_copies(n, slot):
            copy.wait()
        dh = dot_nn(eb[...], weight(wbuf, slot, 512, 768))
        g = gu[slot, 0].astype(F32)
        u = gu[slot, 1].astype(F32)
        sg = jax.nn.sigmoid(g)
        dg[n] = (dh * u * sg * (1.0 + g * (1.0 - sg))).astype(BF16)
        du[n] = (dh * g * sg).astype(BF16)

        @pl.loop(0, 4)
        def _(r):
            rows = pl.ds(pl.multiple_of(r * 128, 128), 128)
            acc[rows, :] += dot_nt(dg[n, rows, :], weight(wbuf, slot, 0, 256)) + dot_nt(
                du[n, rows, :], weight(wbuf, slot, 256, 512)
            )

        @pl.when((n == 0) | (n == 4))
        def _():
            pair = lax.div(n, 4)
            feed_grads(pair, pair)
            step(2 * pair)
            step(2 * pair + 1)

    load_pair(4, 0)

    def x_copy(e, r, src):
        rows = pl.ds(r * 128, 128)
        return remote(src.at[rows], xr.at[rows], x_send.at[e, r], x_recv.at[e, r], me.xpeer)

    for r in range(4):
        rows = slice(r * 128, (r + 1) * 128)
        xs[rows, :] = acc[rows, :].astype(BF16)
        x_copy(0, r, xs).start()

    @pl.loop(2, 4)
    def _(n):
        feed_grads(n, n)
        step(2 * n)
        step(2 * n + 1)

    gacc[...] = jnp.zeros_like(gacc)
    for r in range(4):
        rows = slice(r * 128, (r + 1) * 128)
        x_copy(0, r, xs).wait()
        own = xs[rows, :].astype(F32)
        db = own + xr[rows, :].astype(F32)
        x = x2[rows, :]
        r2_rows = lax.rsqrt(jnp.mean(x * x, axis=-1, keepdims=True) + epsilon)
        n2 = x * r2_rows
        gacc[1:2, :] += jnp.sum(own * n2, axis=0, keepdims=True)
        scaled = db * gain_rows[1:2, :]
        dx2 = eb[rows, :].astype(F32) + r2_rows * (
            scaled - n2 * jnp.mean(scaled * n2, axis=-1, keepdims=True)
        )
        acc[rows, :] = dx2
        eb[rows, :] = dx2.astype(BF16)

    def give_x():
        pl.semaphore_signal(x_cred, inc=1, device_id=me.xpeer, device_id_type=MESH)

    give_x()
    local(out_part, xs, 0).start()
    pl.semaphore_wait(x_cred, 1)
    for r in range(4):
        x_copy(1, r, out_part).start()

    transpose_into(dxt, eb)
    for i in range(3):
        put(4, slice(i * 256, (i + 1) * 256), dot_nn(dxt[...], ob[:, i * 256 : (i + 1) * 256]))
    step(8)
    wait_pair(4, 0)
    for s in range(2):
        rows = slice(s * SPAN, (s + 1) * SPAN)
        for side in range(2):
            columns = (side * UNIT, (side + 1) * UNIT)
            mixed = dot_nn(eb[rows, :], weight(wbuf, 0, *columns)).astype(BF16).astype(F32)
            for i, head in enumerate(unpack_heads(mixed)):
                doh[s * 8 + side * 4 + i] = head.astype(BF16)
    step(9)
    load_pair(2, 0)
    load_pair(0, 1)
    local(tokens, eb, 1).start()

    def attend_back(i):
        s, g = lax.div(i, 4), lax.rem(i, 4)
        mask = allowed_keys(low[s], high[...])
        dk = jnp.zeros((4 * SPAN, 128), F32)
        dv = jnp.zeros((4 * SPAN, 128), F32)
        for hh in range(2):
            h = s * 8 + 2 * g + hh
            scores = jnp.where(mask, dot_nt(kh[i], qh[h]) * scale, negative)
            p = jnp.exp(scores - lse[h][0:1, :])
            dp = dot_nt(vh[i], doh[h])
            delta = jnp.sum(p * dp, axis=0, keepdims=True)
            ds = (p * (dp - delta) * scale).astype(BF16)
            dv += dot_nn(p.astype(BF16), doh[h])
            dk += dot_nn(ds, qh[h])
            dqh[2 * g + hh] = dot_tn(kh[i], ds).T
        dkh[g] = dk.astype(BF16)
        dvh[g] = dv.astype(BF16)

    def kv_core(s):
        return remote(dkv.at[s, :, me.ok], rc.at[s], kv_send.at[0, s], kv_recv.at[0, s], me.sib)

    def kv_y(s):
        return remote(rc.at[s, me.oy], ry.at[s], kv_send.at[1, s], kv_recv.at[1, s], me.ypeer)

    @pl.loop(0, 4)
    def _(i):
        attend_back(2 * i)
        attend_back(2 * i + 1)
        feed_grads(4 + i, 5 + i)
        step(10 + 2 * i)

        @pl.when(lax.rem(i, 2) == 1)
        def _():
            s = lax.div(i, 2)
            for c in range(4):
                rows = slice(c * SPAN, (c + 1) * SPAN)
                for j, heads in enumerate((dkh, dvh)):
                    dkv[s, c // 2, c % 2, :, j * UNIT : (j + 1) * UNIT] = pack_heads(
                        [heads[g, rows, :].astype(F32) for g in range(4)]
                    ).astype(BF16)
            kv_core(s).start()
            rows = pl.ds(pl.multiple_of(s * SPAN, SPAN), SPAN)
            for side in range(2):
                dq = turn(pack_heads([dqh[side * 4 + j] for j in range(4)]), cosine[...], -sine[...])
                dqb[rows, side * UNIT : (side + 1) * UNIT] = dq.astype(BF16)

        step(11 + 2 * i)

    local(at_in, bt, 2).start()
    for s in range(2):
        kv_core(s).wait_recv()
        rc[s] = rc[s] + dkv[s, :, k]
        kv_y(s).start()
    local(at_in, bt, 2).wait()
    for i in range(3):
        put(9, slice(i * 256, (i + 1) * 256), dot_nn(bt[...], dqb[:, i * 256 : (i + 1) * 256]))
    step(18)

    local(out_part, xs, 0).wait()
    for r in range(4):
        rows = slice(r * 128, (r + 1) * 128)
        x_copy(1, r, out_part).wait()
        xs[rows, :] = (x2[rows, :] + (xs[rows, :].astype(F32) + xr[rows, :].astype(F32))).astype(BF16)
    give_x()
    local(xs, output, 0).start()
    step(19)
    wait_pair(2, 0)
    wait_pair(0, 1)
    local(tokens, eb, 1).wait()
    for s in range(2):
        rows = slice(s * SPAN, (s + 1) * SPAN)
        kv_y(s).wait_recv()
        total = rc[s, y].astype(F32) + ry[s].astype(F32)
        dkvb[rows, :UNIT] = turn(total[:, :UNIT], cosine[...], -sine[...]).astype(BF16)
        dkvb[rows, UNIT:] = total[:, UNIT:].astype(BF16)
    for i in range(3):
        put(10, slice(i * 256, (i + 1) * 256), dot_nn(bt[...], dkvb[:, i * 256 : (i + 1) * 256]))
    step(20)
    local(xs, output, 0).wait()
    pl.semaphore_wait(x_cred, 1)

    def first_norm(rows):
        x = eb[rows, :].astype(F32)
        r1_rows = lax.rsqrt(jnp.mean(x * x, axis=-1, keepdims=True) + epsilon)
        return r1_rows, x * r1_rows

    for r in range(4):
        rows = slice(r * 128, (r + 1) * 128)
        da = dot_nt(dqb[rows, :], weight(wbuf, 0, 0, 768)) + dot_nt(dkvb[rows, :], weight(wbuf, 1, 0, 768))
        xs[rows, :] = da.astype(BF16)
        x_copy(2, r, xs).start()
        gacc[0:1, :] += jnp.sum(xs[rows, :].astype(F32) * first_norm(rows)[1], axis=0, keepdims=True)
    step(21)
    gain_columns = jnp.concatenate([gacc[...], jnp.zeros((120, WIDE), F32)], axis=0).T
    gp[...] = gain_columns.astype(BF16).reshape(4, 2, 2, depth, 128)
    gain = GainUnit()
    stage_core(gain)
    step(22)
    stage_y(gain)
    step(23)
    stage_z(gain)

    for r in range(4):
        rows = slice(r * 128, (r + 1) * 128)
        x_copy(2, r, xs).wait()
        da = xs[rows, :].astype(F32) + xr[rows, :].astype(F32)
        r1_rows, n1 = first_norm(rows)
        scaled = da * gain_rows[0:1, :]
        acc[rows, :] += r1_rows * (scaled - n1 * jnp.mean(scaled * n1, axis=-1, keepdims=True))
    local(acc, grad_tokens, 0).start()
    stage_zb(gain)
    step(24)

    def store_gain(total):
        gs[0] = total

    stage_end(gain, store_gain)
    pair_copy = remote(gs.at[0], gs.at[1], g_send.at[0], g_recv.at[0], me.xpeer)
    pair_copy.start()
    step(25)
    pair_copy.wait()
    out_copy(units - 2).wait()
    out_copy(units - 1).wait()
    gain_grads[...] = gs[0] + gs[1]
    for s in range(2):
        kv_core(s).wait_send()
        kv_y(s).wait_send()
    local(acc, grad_tokens, 0).wait()


def call_backward(w_all, gain_rows, tokens, cot, at, bt, et, gate, up, hidden, out_part, *rest):
    units, depth = w_all.shape[0], w_all.shape[4]
    groups = gate.shape[0]
    struct = jax.ShapeDtypeStruct
    any_spec = pl.BlockSpec(memory_space=pl.ANY)
    vmem_spec = pl.BlockSpec(memory_space=pltpu.VMEM)
    dma = pltpu.SemaphoreType.DMA
    regular = pltpu.SemaphoreType.REGULAR
    return pl.pallas_call(
        backward_kernel,
        out_shape=(
            struct((ROWS, WIDE), BF16),
            struct((ROWS, WIDE), F32),
            struct((units, depth, UNIT), F32),
            struct((depth, 128), F32),
        ),
        in_specs=[any_spec, vmem_spec] + [any_spec] * 9 + [vmem_spec] * 10,
        out_specs=(any_spec, any_spec, any_spec, vmem_spec),
        scratch_shapes=[
            vmem((ROWS, WIDE), BF16),
            vmem((WIDE, ROWS), BF16),
            vmem((WIDE, ROWS), BF16),
            vmem((WIDE, ROWS), BF16),
            vmem((groups, ROWS, 256), BF16),
            vmem((groups, ROWS, 256), BF16),
            vmem((2, 2, ROWS, 256), BF16),
            vmem((2, ROWS, 256), BF16),
            vmem((2, 4, 2, 2, depth, 2 * UNIT), BF16),
            vmem((2, 4, 2, 2, depth, 2 * UNIT), BF16),
            vmem((RING, 4, 2, depth, UNIT), BF16),
            vmem((RING, 4, depth, UNIT), BF16),
            vmem((RING, 4, depth, UNIT), BF16),
            vmem((ROWS, WIDE), F32),
            vmem((ROWS, WIDE), BF16),
            vmem((ROWS, WIDE), BF16),
            vmem((16, SPAN, 128), BF16),
            vmem((8, SPAN, 128), F32),
            vmem((4, 4 * SPAN, 128), BF16),
            vmem((4, 4 * SPAN, 128), BF16),
            vmem((2, 2, 2, SPAN, 2 * UNIT), BF16),
            vmem((2, 2, SPAN, 2 * UNIT), BF16),
            vmem((2, SPAN, 2 * UNIT), BF16),
            vmem((ROWS, 2 * UNIT), BF16),
            vmem((ROWS, 2 * UNIT), BF16),
            vmem((8, WIDE), F32),
            vmem((4, 2, 2, depth, 128), BF16),
            vmem((4, 2, depth, 128), BF16),
            vmem((4, depth, 128), BF16),
            vmem((4, depth, 128), BF16),
            vmem((2, depth, 128), F32),
            dma((units + 1,)),
            dma((units + 1,)),
            dma((units + 1,)),
            dma((units + 1,)),
            dma((units + 1,)),
            dma((units + 1,)),
            dma((units + 1, 3)),
            dma((units + 1, 2)),
            regular,
            regular,
            regular((3,)),
            dma((3, 4)),
            dma((3, 4)),
            regular,
            dma((2, 2)),
            dma((2, 2)),
            dma((1,)),
            dma((1,)),
            dma((3,)),
            dma((2, 2)),
            dma((2, 3)),
            vmem((2, depth, UNIT), F32),
            dma((2,)),
        ],
        compiler_params=pltpu.CompilerParams(
            collective_id=2, has_side_effects=True, vmem_limit_bytes=64 << 20
        ),
        name="backward",
    )(w_all, gain_rows, tokens, cot, at, bt, et, gate, up, hidden, out_part, *rest)


def fast_body(
    tokens,
    segments,
    cotangent,
    gain_attn,
    w_query,
    w_key,
    w_value,
    w_out,
    gain_mlp,
    w_gate,
    w_up,
    w_down,
):
    positions, cosine, sine = rope_inputs(SPAN)
    mine = lax.dynamic_slice_in_dim(segments, positions[0], SPAN, 1)
    low = jnp.sum((segments[:, None, :] < mine[:, :, None]).astype(jnp.int32), axis=-1)[:, None, :]
    high = positions[None, :]
    packed = pack_weights(w_query, w_key, w_value, w_out, w_gate, w_up, w_down)
    gains = pack_gains(gain_attn, gain_mlp)
    flat_tokens = tokens.reshape(ROWS, WIDE)
    flat_cot = cotangent.reshape(ROWS, WIDE)
    (
        w_all,
        gain_rows,
        at,
        bt,
        et,
        qh,
        kh,
        vh,
        lse,
        ob,
        x2,
        gate,
        up,
        hidden,
        out_part,
    ) = call_forward(packed, gains, flat_tokens, flat_cot, cosine, sine, low, high)
    output, grad_tokens, grads, gain_grads = call_backward(
        w_all,
        gain_rows,
        flat_tokens,
        flat_cot,
        at,
        bt,
        et,
        gate,
        up,
        hidden,
        out_part,
        qh,
        kh,
        vh,
        lse,
        ob,
        x2,
        cosine,
        sine,
        low,
        high,
    )

    def span(lo, hi):
        return jnp.concatenate([grads[i] for i in range(lo, hi)], axis=1)

    fed = [span(2 * i, 2 * i + 2) for i in (0, 1, 2, 3, 5, 6, 7, 8)]
    gate_grad, up_grad, down_grad = (
        jnp.concatenate([group[:, i * 256 : (i + 1) * 256] for group in fed], axis=1) for i in range(3)
    )
    return (
        output.reshape(tokens.shape),
        grad_tokens.reshape(tokens.shape),
        gain_grads[:, 0],
        span(18, 20),
        grads[20],
        grads[21],
        span(8, 10).T,
        gain_grads[:, 1],
        gate_grad,
        up_grad,
        down_grad.T,
    )


def fits(mesh):
    return mesh.shape["fsdp"] == 4 and mesh.shape["ctx"] == 4 and mesh.shape["tp"] == 2


def solution(mesh):
    placed = (
        P("fsdp", "ctx", None),
        P("fsdp", None),
        P("fsdp", "ctx", None),
        P(("fsdp", "ctx")),
        P(("fsdp", "ctx"), "tp"),
        P(("fsdp", "ctx"), "tp"),
        P(("fsdp", "ctx"), "tp"),
        P("tp", ("fsdp", "ctx")),
        P(("fsdp", "ctx")),
        P(("fsdp", "ctx"), "tp"),
        P(("fsdp", "ctx"), "tp"),
        P("tp", ("fsdp", "ctx")),
    )
    return jax.shard_map(
        fast_body if fits(mesh) else body,
        mesh=mesh,
        in_specs=placed,
        out_specs=(
            P("fsdp", "ctx", None),
            P("fsdp", "ctx", None),
            P(("fsdp", "ctx")),
            P(("fsdp", "ctx"), "tp"),
            P(("fsdp", "ctx"), "tp"),
            P(("fsdp", "ctx"), "tp"),
            P("tp", ("fsdp", "ctx")),
            P(("fsdp", "ctx")),
            P(("fsdp", "ctx"), "tp"),
            P(("fsdp", "ctx"), "tp"),
            P("tp", ("fsdp", "ctx")),
        ),
        check_vma=False,
    )
```

```python
import math

import jax
import jax.numpy as jnp
from jax import lax
from jax.experimental import pallas as pl
from jax.experimental.pallas import tpu as pltpu
from jax.sharding import PartitionSpec as P

HD = 96
GROUP = 2


epsilon = 1e-05
rope_base = 100000.0
negative = -1e30


def rope_tables(positions):
    half_width = HD // 2
    frequency = rope_base ** (-(2.0 * jnp.arange(half_width, dtype=jnp.float32)) / HD)
    angles = positions.astype(jnp.float32)[:, None] * frequency[None, :]
    return (jnp.cos(angles), jnp.sin(angles))


def rotate(vectors, cosine_table, sine_table):
    half_width = vectors.shape[-1] // 2
    former = vectors[..., :half_width]
    latter = vectors[..., half_width:]
    return jnp.concatenate(
        [former * cosine_table - latter * sine_table, latter * cosine_table + former * sine_table],
        axis=-1,
    )


def head_sum(partial_rows):
    return lax.psum(partial_rows.astype(jnp.bfloat16), "tp").astype(jnp.float32)


def weight_gather(shards):
    row_parts = (
        lax.all_gather(shards[0], ("fsdp", "ctx"), axis=0, tiled=True),
        lax.all_gather(shards[1], ("fsdp", "ctx"), axis=0, tiled=True),
        lax.all_gather(shards[2], ("fsdp", "ctx"), axis=0, tiled=True),
        lax.all_gather(shards[3], ("fsdp", "ctx"), axis=0, tiled=True),
        lax.all_gather(shards[4], ("fsdp", "ctx"), axis=0, tiled=True),
        lax.all_gather(shards[5], ("fsdp", "ctx"), axis=0, tiled=True),
        lax.all_gather(shards[6], ("fsdp", "ctx"), axis=0, tiled=True),
    )
    column_parts = (
        lax.all_gather(shards[7], ("fsdp", "ctx"), axis=1, tiled=True),
        lax.all_gather(shards[8], ("fsdp", "ctx"), axis=1, tiled=True),
    )
    return tuple(row_parts) + tuple(column_parts)


def grad_reduce(gradients):
    row_parts = (
        lax.psum_scatter(gradients[0], ("fsdp", "ctx"), scatter_dimension=0, tiled=True),
        lax.psum_scatter(gradients[1], ("fsdp", "ctx"), scatter_dimension=0, tiled=True),
        lax.psum_scatter(gradients[2], ("fsdp", "ctx"), scatter_dimension=0, tiled=True),
        lax.psum_scatter(gradients[3], ("fsdp", "ctx"), scatter_dimension=0, tiled=True),
        lax.psum_scatter(gradients[4], ("fsdp", "ctx"), scatter_dimension=0, tiled=True),
        lax.psum_scatter(gradients[5], ("fsdp", "ctx"), scatter_dimension=0, tiled=True),
        lax.psum_scatter(gradients[6], ("fsdp", "ctx"), scatter_dimension=0, tiled=True),
    )
    column_parts = (
        lax.psum_scatter(gradients[7], ("fsdp", "ctx"), scatter_dimension=1, tiled=True),
        lax.psum_scatter(gradients[8], ("fsdp", "ctx"), scatter_dimension=1, tiled=True),
    )
    return tuple(row_parts) + tuple(column_parts)


def block_scores(queries, key_block, query_seg, positions, key_seg, key_start):
    score_scale = 1.0 / math.sqrt(queries.shape[-1])
    key_positions = key_start + jnp.arange(key_block.shape[0], dtype=jnp.int32)
    allowed = (query_seg[:, None] == key_seg[None, :]) & (
        positions[:, None] >= key_positions[None, :]
    )
    raw_scores = jnp.einsum(
        "qhgd,khd->hgqk", queries, key_block, preferred_element_type=jnp.float32
    )
    return (jnp.where(allowed, raw_scores * score_scale, negative), allowed)


def block_fetch(
    key_all, value_all, segment_row, block_index, block_keys, last_position, first_segment
):
    key_start = block_index * block_keys
    key_block = lax.dynamic_slice_in_dim(key_all, key_start, block_keys, 0)
    value_block = lax.dynamic_slice_in_dim(value_all, key_start, block_keys, 0)
    key_seg = lax.dynamic_slice_in_dim(segment_row, key_start, block_keys, 0)
    needed = (key_start <= last_position) & (key_seg[block_keys - 1] >= first_segment)
    return (key_start, key_block, value_block, key_seg, needed)


def attention_forward(queries, key_all, value_all, segment_row, query_seg, positions):
    row_count, heads_kv, group_size, head_dim = queries.shape
    length = key_all.shape[0]
    block_keys = math.gcd(512, length)
    block_total = length // block_keys
    last_position = positions[row_count - 1]
    first_segment = query_seg[0]

    def stats_step(block_index, state):
        key_start, key_block, value_block, key_seg, needed = block_fetch(
            key_all, value_all, segment_row, block_index, block_keys, last_position, first_segment
        )
        top_old, total_old = state
        scores, allowed = block_scores(queries, key_block, query_seg, positions, key_seg, key_start)
        top_new = jnp.maximum(top_old, jnp.max(scores, axis=-1))
        weights = jnp.where(allowed, jnp.exp(scores - top_new[..., None]), 0.0)
        return (top_new, total_old * jnp.exp(top_old - top_new) + jnp.sum(weights, axis=-1))

    start_top = jnp.full((heads_kv, group_size, row_count), negative, jnp.float32)
    row_top, row_total = lax.fori_loop(
        0, block_total, stats_step, (start_top, jnp.zeros_like(start_top))
    )

    def output_step(block_index, state):
        key_start, key_block, value_block, key_seg, needed = block_fetch(
            key_all, value_all, segment_row, block_index, block_keys, last_position, first_segment
        )
        scores, allowed = block_scores(queries, key_block, query_seg, positions, key_seg, key_start)
        probability = (
            jnp.where(allowed, jnp.exp(scores - row_top[..., None]), 0.0) / row_total[..., None]
        )
        return state + jnp.einsum(
            "hgqk,khd->qhgd",
            probability.astype(jnp.bfloat16),
            value_block,
            preferred_element_type=jnp.float32,
        )

    start_out = jnp.zeros((row_count, heads_kv, group_size, head_dim), jnp.float32)
    out_low = lax.fori_loop(0, block_total, output_step, start_out)
    return (row_top, row_total, out_low)


def attention_backward(
    queries,
    key_all,
    value_all,
    segment_row,
    query_seg,
    positions,
    row_top,
    row_total,
    grad_mixed,
    row_delta,
):
    row_count, heads_kv, group_size, head_dim = queries.shape
    length = key_all.shape[0]
    block_keys = math.gcd(512, length)
    block_total = length // block_keys
    last_position = positions[row_count - 1]
    first_segment = query_seg[0]
    score_scale = 1.0 / math.sqrt(head_dim)

    def grad_step(block_index, state):
        key_start, key_block, value_block, key_seg, needed = block_fetch(
            key_all, value_all, segment_row, block_index, block_keys, last_position, first_segment
        )
        grad_query, grad_keys, grad_values = state
        scores, allowed = block_scores(queries, key_block, query_seg, positions, key_seg, key_start)
        probability = (
            jnp.where(allowed, jnp.exp(scores - row_top[..., None]), 0.0) / row_total[..., None]
        )
        grad_prob = jnp.einsum(
            "qhgd,khd->hgqk", grad_mixed, value_block, preferred_element_type=jnp.float32
        )
        grad_score = (probability * (grad_prob - row_delta[..., None]) * score_scale).astype(
            jnp.bfloat16
        )
        grad_query = grad_query + jnp.einsum(
            "hgqk,khd->qhgd", grad_score, key_block, preferred_element_type=jnp.float32
        )
        key_part = jnp.einsum(
            "hgqk,qhgd->khd", grad_score, queries, preferred_element_type=jnp.float32
        )
        value_part = jnp.einsum(
            "hgqk,qhgd->khd",
            probability.astype(jnp.bfloat16),
            grad_mixed,
            preferred_element_type=jnp.float32,
        )
        grad_keys = lax.dynamic_update_slice_in_dim(grad_keys, key_part, key_start, 0)
        grad_values = lax.dynamic_update_slice_in_dim(grad_values, value_part, key_start, 0)
        return (grad_query, grad_keys, grad_values)

    start_query = jnp.zeros((row_count, heads_kv, group_size, head_dim), jnp.float32)
    start_keys = jnp.zeros((length, heads_kv, head_dim), jnp.float32)
    return lax.fori_loop(0, block_total, grad_step, (start_query, start_keys, start_keys))


def micro_step(gathered, token_rows, segment_row, grad_in, positions, cosine_table, sine_table):
    gain_attn, w_query, w_key, w_value, gain_mlp, w_gate, w_up, w_out, w_down = gathered
    row_count = token_rows.shape[0]
    heads_kv = w_key.shape[1] // HD
    cos_four = cosine_table[:, None, None, :]
    sin_four = sine_table[:, None, None, :]
    cos_three = cosine_table[:, None, :]
    sin_three = sine_table[:, None, :]
    query_seg = lax.dynamic_slice_in_dim(segment_row, positions[0], row_count, 0)
    gain_first = gain_attn.astype(jnp.float32)
    gain_second = gain_mlp.astype(jnp.float32)
    inputs = token_rows.astype(jnp.float32)
    scale_first = lax.rsqrt(jnp.mean(inputs * inputs, axis=-1, keepdims=True) + epsilon)
    normal_first = inputs * scale_first
    normed = (normal_first * gain_first).astype(jnp.bfloat16)
    query_raw = jnp.dot(normed, w_query, preferred_element_type=jnp.float32).reshape(
        row_count, heads_kv, GROUP, HD
    )
    key_raw = jnp.dot(normed, w_key, preferred_element_type=jnp.float32).reshape(
        row_count, heads_kv, HD
    )
    value_low = (
        jnp.dot(normed, w_value, preferred_element_type=jnp.float32)
        .astype(jnp.bfloat16)
        .reshape(row_count, heads_kv, HD)
    )
    query_low = rotate(query_raw, cos_four, sin_four).astype(jnp.bfloat16)
    key_low = rotate(key_raw, cos_three, sin_three).astype(jnp.bfloat16)
    key_all, value_all = (
        lax.all_gather(key_low, "ctx", axis=0, tiled=True),
        lax.all_gather(value_low, "ctx", axis=0, tiled=True),
    )
    row_top, row_total, out_low = attention_forward(
        query_low, key_all, value_all, segment_row, query_seg, positions
    )
    mixed_low = out_low.reshape(row_count, -1).astype(jnp.bfloat16)
    middle = inputs + head_sum(jnp.dot(mixed_low, w_out, preferred_element_type=jnp.float32))
    scale_second = lax.rsqrt(jnp.mean(middle * middle, axis=-1, keepdims=True) + epsilon)
    normal_second = middle * scale_second
    second = (normal_second * gain_second).astype(jnp.bfloat16)
    gate_part = jnp.dot(second, w_gate, preferred_element_type=jnp.float32)
    upward = jnp.dot(second, w_up, preferred_element_type=jnp.float32)
    sigmoid_gate = jax.nn.sigmoid(gate_part)
    silu_gate = gate_part * sigmoid_gate
    hidden = (silu_gate * upward).astype(jnp.bfloat16)
    result_rows = middle + head_sum(jnp.dot(hidden, w_down, preferred_element_type=jnp.float32))
    output_rows = result_rows.astype(jnp.bfloat16)
    grad_final = grad_in.astype(jnp.float32)
    grad_down = jnp.einsum("tf,td->fd", hidden, grad_in, preferred_element_type=jnp.float32)
    grad_hidden = jnp.einsum("td,fd->tf", grad_in, w_down, preferred_element_type=jnp.float32)
    grad_gate_low = (
        grad_hidden * upward * sigmoid_gate * (1.0 + gate_part * (1.0 - sigmoid_gate))
    ).astype(jnp.bfloat16)
    grad_up_low = (grad_hidden * silu_gate).astype(jnp.bfloat16)
    grad_gate = jnp.einsum("td,tf->df", second, grad_gate_low, preferred_element_type=jnp.float32)
    grad_up = jnp.einsum("td,tf->df", second, grad_up_low, preferred_element_type=jnp.float32)
    grad_second = head_sum(
        jnp.einsum("tf,df->td", grad_gate_low, w_gate, preferred_element_type=jnp.float32)
        + jnp.einsum("tf,df->td", grad_up_low, w_up, preferred_element_type=jnp.float32)
    )
    scaled_second = grad_second * gain_second
    grad_gain_mlp = jnp.sum(grad_second * normal_second, axis=0)
    grad_middle = grad_final + scale_second * (
        scaled_second
        - normal_second * jnp.mean(scaled_second * normal_second, axis=-1, keepdims=True)
    )
    grad_middle_low = grad_middle.astype(jnp.bfloat16)
    grad_out = jnp.einsum(
        "tk,td->kd", mixed_low, grad_middle_low, preferred_element_type=jnp.float32
    )
    grad_mixed = (
        jnp.einsum("td,kd->tk", grad_middle_low, w_out, preferred_element_type=jnp.float32)
        .astype(jnp.bfloat16)
        .reshape(row_count, heads_kv, GROUP, HD)
    )
    row_delta = jnp.transpose(jnp.sum(grad_mixed.astype(jnp.float32) * out_low, axis=-1), (1, 2, 0))
    grad_query_rot, grad_keys, grad_values = attention_backward(
        query_low,
        key_all,
        value_all,
        segment_row,
        query_seg,
        positions,
        row_top,
        row_total,
        grad_mixed,
        row_delta,
    )
    grad_key_mine, grad_value_mine = (
        lax.psum_scatter(
            grad_keys.astype(jnp.bfloat16), "ctx", scatter_dimension=0, tiled=True
        ).astype(jnp.float32),
        lax.psum_scatter(
            grad_values.astype(jnp.bfloat16), "ctx", scatter_dimension=0, tiled=True
        ).astype(jnp.float32),
    )
    grad_query_low = (
        rotate(grad_query_rot, cos_four, -sin_four).astype(jnp.bfloat16).reshape(row_count, -1)
    )
    grad_key_low = (
        rotate(grad_key_mine, cos_three, -sin_three).astype(jnp.bfloat16).reshape(row_count, -1)
    )
    grad_value_low = grad_value_mine.astype(jnp.bfloat16).reshape(row_count, -1)
    grad_query = jnp.einsum("td,tk->dk", normed, grad_query_low, preferred_element_type=jnp.float32)
    grad_key = jnp.einsum("td,tk->dk", normed, grad_key_low, preferred_element_type=jnp.float32)
    grad_value = jnp.einsum("td,tk->dk", normed, grad_value_low, preferred_element_type=jnp.float32)
    grad_normed = head_sum(
        jnp.einsum("tk,dk->td", grad_query_low, w_query, preferred_element_type=jnp.float32)
        + jnp.einsum("tk,dk->td", grad_key_low, w_key, preferred_element_type=jnp.float32)
        + jnp.einsum("tk,dk->td", grad_value_low, w_value, preferred_element_type=jnp.float32)
    )
    scaled_first = grad_normed * gain_first
    grad_gain_attn = jnp.sum(grad_normed * normal_first, axis=0)
    grad_tokens = grad_middle + scale_first * (
        scaled_first - normal_first * jnp.mean(scaled_first * normal_first, axis=-1, keepdims=True)
    )
    gradients = (
        grad_gain_attn,
        grad_query,
        grad_key,
        grad_value,
        grad_gain_mlp,
        grad_gate,
        grad_up,
        grad_out,
        grad_down,
    )
    return (output_rows, grad_tokens, gradients)


def body(
    tokens,
    segments,
    cotangent,
    gain_attn,
    w_query,
    w_key,
    w_value,
    w_out,
    gain_mlp,
    w_gate,
    w_up,
    w_down,
):
    micro_count = tokens.shape[0]
    row_count = tokens.shape[1]
    positions = lax.axis_index("ctx") * row_count + jnp.arange(row_count, dtype=jnp.int32)
    cosine_table, sine_table = rope_tables(positions)
    shards = (gain_attn, w_query, w_key, w_value, gain_mlp, w_gate, w_up, w_out, w_down)
    outputs = []
    token_grads = []
    gathered = weight_gather(shards)
    totals = None
    for micro_index in range(micro_count):
        output_rows, grad_rows, grads_now = micro_step(
            gathered,
            tokens[micro_index],
            segments[micro_index],
            cotangent[micro_index],
            positions,
            cosine_table,
            sine_table,
        )
        outputs.append(output_rows)
        token_grads.append(grad_rows)
        totals = (
            grads_now
            if totals is None
            else tuple(earlier + addend for earlier, addend in zip(totals, grads_now))
        )
    reduced = tuple(
        tensor_piece.astype(jnp.float32)
        for tensor_piece in grad_reduce(tuple(total.astype(jnp.bfloat16) for total in totals))
    )
    return (
        jnp.stack(outputs),
        jnp.stack(token_grads),
        reduced[0],
        reduced[1],
        reduced[2],
        reduced[3],
        reduced[7],
        reduced[4],
        reduced[5],
        reduced[6],
        reduced[8],
    )


MESH = pl.DeviceIdType.MESH
UNIT = 384
ROWS = 512
SPAN = 256
WIDE = 1536
F32 = jnp.float32
BF16 = jnp.bfloat16
NT = (((1,), (1,)), ((), ()))
TN = (((0,), (0,)), ((), ()))


def dot_nn(a, b):
    return jnp.dot(a, b, preferred_element_type=F32)


def dot_nt(a, b):
    return lax.dot_general(a, b, NT, preferred_element_type=F32)


def dot_tn(a, b):
    return lax.dot_general(a, b, TN, preferred_element_type=F32)


class Place:
    def __init__(self):
        f, c, t = (lax.axis_index(axis) for axis in ("fsdp", "ctx", "tp"))
        self.f, self.c, self.t = f, c, t
        self.y, self.k = lax.div(c, 2), lax.rem(c, 2)
        self.oy, self.ok = 1 - self.y, 1 - self.k
        self.half = lax.div(f, 2)
        self.inner = (f == 1) | (f == 2)
        self.edge = (f == 0) | (f == 3)
        self.near_f = f + 1 - 2 * lax.rem(f, 2)
        self.mid_f = 2 - self.half
        self.far_f = 3 - 3 * self.half
        self.near = (self.near_f, c, t)
        self.mid = (self.mid_f, c, t)
        self.far = (self.far_f, c, t)
        self.ypeer = (f, c + 2 - 4 * self.y, t)
        self.sib = (f, c + 1 - 2 * self.k, t)
        self.xpeer = (f, c, 1 - t)

    def barrier(self):
        sem = pltpu.get_barrier_semaphore()
        others = [(lax.rem(self.f + step, 4), self.c, self.t) for step in (1, 2, 3)]
        others += [self.ypeer, self.sib, self.xpeer]
        for other in others:
            pl.semaphore_signal(sem, inc=1, device_id=other, device_id_type=MESH)
        pl.semaphore_wait(sem, len(others))


def remote(src, dst, send, recv, device):
    return pltpu.make_async_remote_copy(
        src_ref=src,
        dst_ref=dst,
        send_sem=send,
        recv_sem=recv,
        device_id=device,
        device_id_type=MESH,
    )


def lanes(rows, columns):
    return lax.broadcasted_iota(jnp.int32, (rows, columns), 1)


def unpack_heads(x):
    lane = lanes(x.shape[0], 128)
    one, two, three = x[:, :128], x[:, 128:256], x[:, 256:]
    heads = (
        one,
        pltpu.roll(jnp.where(lane < 64, two, one), 32, 1),
        pltpu.roll(jnp.where(lane < 32, three, two), 64, 1),
        pltpu.roll(three, 96, 1),
    )
    return [jnp.where(lane < HD, head, 0.0) for head in heads]


def pack_heads(heads):
    lane = lanes(heads[0].shape[0], 128)
    second = pltpu.roll(heads[1], 96, 1)
    third = pltpu.roll(heads[2], 64, 1)
    fourth = pltpu.roll(heads[3], 32, 1)
    return jnp.concatenate(
        [
            jnp.where(lane < 96, heads[0], second),
            jnp.where(lane < 64, second, third),
            jnp.where(lane < 32, third, fourth),
        ],
        axis=1,
    )


def turn(x, cosine, sine):
    lane = lax.rem(lanes(x.shape[0], UNIT), HD)
    swapped = jnp.where(lane < HD // 2, pltpu.roll(x, UNIT - HD // 2, 1), pltpu.roll(x, HD // 2, 1))
    return x * cosine + swapped * sine


def transpose_into(dst, src):
    @pl.loop(0, WIDE // 128)
    def _(i):
        at = pl.multiple_of(i * 128, 128)
        dst[pl.ds(at, 128), :] = src[:, pl.ds(at, 128)].astype(F32).T.astype(BF16)


def weight(buf, slot, lo, hi):
    return buf[slot, :, :, :, :, lo:hi].reshape(WIDE, hi - lo)


def allowed_keys(low_row, high_row):
    row = lax.broadcasted_iota(jnp.int32, (4 * SPAN, SPAN), 0)
    return (row >= low_row) & (row <= high_row)


RING = 5
WIDE_A = 256
WIDE_B = 128


class GatherA:
    def __init__(self, me, buf, source, sems):
        self.me, self.buf, self.source = me, buf, source
        self.z_send, self.z_recv, self.y_send, self.y_recv, self.c_send, self.c_recv = sems

    def z_copy(self, j, i):
        me = self.me
        dst = self.buf.at[j, me.f, me.y, me.k]
        return remote(self.source.at[j], dst, self.z_send.at[j, i], self.z_recv.at[j], (me.near, me.mid)[i])

    def hand_copy(self, j):
        me = self.me
        part = self.buf.at[j, pl.ds(2 - 2 * me.half, 2), me.y, me.k]
        return remote(part, part, self.z_send.at[j, 2], self.z_recv.at[j], me.near)

    def y_copy(self, j):
        me = self.me
        part = self.buf.at[j, :, me.y, me.k]
        return remote(part, part, self.y_send.at[j], self.y_recv.at[j], me.ypeer)

    def core_copy(self, j):
        me = self.me
        part = self.buf.at[j, :, :, me.k]
        return remote(part, part, self.c_send.at[j], self.c_recv.at[j], me.sib)

    def z_wait(self, j):
        me = self.me
        three = self.buf.at[j, pl.ds(0, 3), me.y, me.k]
        remote(three, three, self.z_send.at[j, 0], self.z_recv.at[j], me.near).wait_recv()

    def start(self, j):
        for i in range(2):
            self.z_copy(j, i).start()

    def spread(self, j):
        pass

    def hand(self, j):
        @pl.when(self.me.inner)
        def _():
            self.z_wait(j)
            self.hand_copy(j).start()

    def turn(self, j):
        @pl.when(self.me.edge)
        def _():
            self.z_wait(j)

        self.y_copy(j).start()

    def core(self, j):
        self.y_copy(j).wait_recv()
        self.core_copy(j).start()

    def done(self, j):
        self.core_copy(j).wait_recv()

    def sent(self, j):
        for i in range(2):
            self.z_copy(j, i).wait_send()

        @pl.when(self.me.inner)
        def _():
            self.hand_copy(j).wait_send()

        self.y_copy(j).wait_send()
        self.core_copy(j).wait_send()


class GatherB(GatherA):
    def z_copy(self, j, i):
        me = self.me
        part = self.buf.at[j, me.f, :, me.k]
        return remote(part, part, self.z_send.at[j, i], self.z_recv.at[j], (me.near, me.mid)[i])

    def hand_copy(self, j):
        me = self.me
        part = self.buf.at[j, pl.ds(2 - 2 * me.half, 2), :, me.k]
        return remote(part, part, self.z_send.at[j, 2], self.z_recv.at[j], me.near)

    def y_copy(self, j):
        me = self.me
        dst = self.buf.at[j, me.f, me.y, me.k]
        return remote(self.source.at[j], dst, self.y_send.at[j], self.y_recv.at[j], me.ypeer)

    def z_wait(self, j):
        me = self.me
        three = self.buf.at[j, pl.ds(0, 3), :, me.k]
        remote(three, three, self.z_send.at[j, 0], self.z_recv.at[j], me.near).wait_recv()

    def start(self, j):
        self.y_copy(j).start()

    def spread(self, j):
        self.y_copy(j).wait_recv()
        for i in range(2):
            self.z_copy(j, i).start()

    def turn(self, j):
        pass

    def core(self, j):
        @pl.when(self.me.edge)
        def _():
            self.z_wait(j)

        self.core_copy(j).start()


class ReduceA:
    def __init__(self, me, r, other, mine, bufs, sems):
        self.me, self.r, self.other, self.mine = me, r, other, mine
        self.r1, self.r2, self.r3 = bufs
        (
            self.c_send,
            self.c_recv,
            self.y_send,
            self.y_recv,
            self.za_send,
            self.za_recv,
            self.zb_send,
            self.zb_recv,
        ) = sems
        self.zed = self.r2

    def core_copy(self):
        return remote(self.other, self.r1, self.c_send.at[self.r], self.c_recv.at[self.r], self.me.sib)

    def y_copy(self):
        src = self.r1.at[:, self.me.oy]
        return remote(src, self.r2, self.y_send.at[self.r], self.y_recv.at[self.r], self.me.ypeer)

    def za_copy(self):
        src = self.zed.at[pl.ds(1 - self.me.half, 3)]
        dst = self.r3.at[pl.ds(0, 3)]
        return remote(src, dst, self.za_send.at[self.r], self.za_recv.at[self.r], self.me.near)

    def zb_copy(self, i):
        me = self.me
        owner, at, device = ((me.near_f, 0, me.near), (me.mid_f, 3, me.mid), (me.far_f, 1, me.far))[i]
        recv = self.zb_recv.at[self.r, min(i, 1)]
        return remote(self.zed.at[owner], self.r3.at[at], self.zb_send.at[self.r, i], recv, device)

    def core(self):
        self.core_copy().start()

    def add_core(self):
        self.core_copy().wait_recv()
        self.r1[...] = self.r1[...] + self.mine[...]
        self.core_copy().wait_send()

    def z_first(self):
        @pl.when(self.me.edge)
        def _():
            self.za_copy().start()

    def z_second(self, before=None):
        me = self.me

        @pl.when(me.inner)
        def _():
            self.za_copy().wait_recv()
            for owner in (me.mid_f, me.far_f):
                self.zed[owner] = self.zed[owner] + self.r3[owner - (1 - me.half)]
            if before is not None:
                before()
            for i in range(3):
                self.zb_copy(i).start()

    def z_total(self):
        me = self.me
        self.zb_copy(1).wait_recv()

        @pl.when(me.edge)
        def _():
            self.zb_copy(0).wait_recv()

        one = jnp.where(me.edge, 0, me.f - (1 - me.half))
        two = jnp.where(me.edge, 1, 3)
        return self.zed[me.f].astype(F32) + self.r3[one].astype(F32) + self.r3[two].astype(F32)

    def z_sent(self):
        @pl.when(self.me.edge)
        def _():
            self.za_copy().wait_send()

        @pl.when(self.me.inner)
        def _():
            for i in range(3):
                self.zb_copy(i).wait_send()

    def y_start(self):
        self.y_copy().start()

    def y_add(self):
        self.y_copy().wait_recv()
        self.r2[...] = self.r2[...] + self.r1[:, self.me.y]
        self.y_copy().wait_send()


class ReduceB(ReduceA):
    def __init__(self, *args):
        super().__init__(*args)
        self.zed = self.r1

    def y_copy(self):
        src = self.r1.at[self.me.f, self.me.oy]
        return remote(src, self.r2, self.y_send.at[self.r], self.y_recv.at[self.r], self.me.ypeer)

    def z_end(self):
        self.r1[self.me.f] = self.z_total().astype(BF16)
        self.z_sent()
        self.y_copy().start()

    def total(self):
        self.y_copy().wait_recv()
        out = self.r1[self.me.f, self.me.y].astype(F32) + self.r2[...].astype(F32)
        self.y_copy().wait_send()
        return out


def layer_kernel(
    packed_a,
    packed_b,
    gains,
    tokens,
    cot,
    cosine,
    sine,
    low,
    high,
    output,
    grad_tokens,
    grads,
    gain_grads,
    wa,
    wb,
    fed,
    gw,
    gain_rows,
    a_buf,
    at,
    bt,
    et,
    eb,
    kvx,
    qh,
    kh,
    vh,
    lse,
    ob,
    x2,
    acc,
    out_acc,
    wbuf,
    part,
    stage,
    back,
    ra1,
    ra2,
    ra3,
    rb1,
    rb2,
    rb3,
    gout,
    xs,
    xr,
    doh,
    heads,
    dkh,
    dvh,
    rc,
    ry,
    dqb,
    dkvb,
    gacc,
    gp,
    g1,
    g2,
    g3,
    gs,
    ga_sems,
    gb_sems,
    gg_sems,
    ra_sems,
    rb_sems,
    rg_sems,
    c_cred,
    y_cred,
    z_cred,
    x_cred,
    x_send,
    x_recv,
    kv_send,
    kv_recv,
    g_sems,
    load_sem,
    w_sem,
    stage_sem,
    back_sem,
    out_sem,
):
    me = Place()
    f, y, k = me.f, me.y, me.k
    units, depth = packed_a.shape[0], packed_a.shape[1]
    groups = fed.shape[0]
    scale = 1.0 / math.sqrt(HD)

    def local(src, dst, i):
        return pltpu.make_async_copy(src, dst, load_sem.at[i])

    own = (
        local(packed_a, wa.at[:, f, y, k], 0),
        local(packed_b, wb.at[:, f, y, k], 1),
        local(gains.at[0], gw.at[0, f, y, k], 2),
    )
    for copy in own:
        copy.start()
    local(cot, eb, 3).start()
    me.barrier()

    gather_a = GatherA(me, wa, packed_a, ga_sems)
    gather_b = GatherB(me, wb, packed_b, gb_sems)
    gather_g = GatherA(me, gw, gains, gg_sems)

    def within(i, count, act):
        if isinstance(i, int):
            if 0 <= i < count:
                act(i)
        else:
            pl.when((i >= 0) & (i < count))(lambda: act(i))

    def ag(t):
        def both(name):
            def act(j):
                getattr(gather_b, name)(j)
                getattr(gather_a, name)(j)

            return act

        within(t + 5, units, both("start"))
        within(t + 3, units, both("spread"))
        within(t + 1, units, both("hand"))
        within(t, units, both("turn"))
        within(t - 1, units, both("core"))
        within(t - 2, units, both("done"))

    def load(u, slot, side):
        at_b = side * UNIT + WIDE_A
        return (
            pltpu.make_async_copy(
                wa.at[u], wbuf.at[slot, :, :, :, :, pl.ds(side * UNIT, WIDE_A)], w_sem.at[slot, side, 0]
            ),
            pltpu.make_async_copy(
                wb.at[u], wbuf.at[slot, :, :, :, :, pl.ds(at_b, WIDE_B)], w_sem.at[slot, side, 1]
            ),
        )

    def load_start(u, slot, side):
        for copy in load(u, slot, side):
            copy.start()

    def load_wait(u, slot, side):
        for copy in load(u, slot, side):
            copy.wait()

    def ring(r):
        s = lax.rem(r, RING)
        slot = lax.rem(lax.div(r, 2), 2)
        start = lax.rem(r, 2) * UNIT
        cols_a = pl.ds(pl.multiple_of(start, 128), WIDE_A)
        cols_b = pl.ds(pl.multiple_of(start + WIDE_A, 128), WIDE_B)
        one = ReduceA(
            me,
            r,
            part.at[slot, :, :, me.ok, :, cols_a],
            part.at[slot, :, :, k, :, cols_a],
            (ra1.at[s], ra2.at[s], ra3.at[s]),
            ra_sems,
        )
        two = ReduceB(
            me,
            r,
            part.at[slot, :, :, me.ok, :, cols_b],
            part.at[slot, :, :, k, :, cols_b],
            (rb1.at[s], rb2.at[s], rb3.at[s]),
            rb_sems,
        )
        return one, two

    def credit(r, sem):
        within(r - RING, units, lambda i: pl.semaphore_wait(sem, 1))

    def give(r, sem, device):
        def act(i):
            pl.semaphore_signal(sem, inc=1, device_id=device, device_id_type=MESH)

        within(r + RING, units, act)

    def out_copy(i):
        slot = lax.rem(i, 2)
        return pltpu.make_async_copy(gout.at[slot], grads.at[i], out_sem.at[slot])

    def rs(r):
        def first(i):
            credit(i, c_cred)
            for unit in ring(i):
                unit.core()

        def second(i):
            one, two = ring(i)
            two.add_core()

            @pl.when(me.edge)
            def _():
                credit(i, z_cred.at[0])

            two.z_first()
            one.add_core()
            credit(i, y_cred)
            one.y_start()

        def third(i):
            one, two = ring(i)

            def take():
                for j in range(3):
                    credit(i, z_cred.at[j])

            two.z_second(take)
            one.y_add()
            one.z_first()

        def fourth(i):
            one, two = ring(i)
            one.z_second()
            two.z_end()

        def fifth(i):
            one, two = ring(i)
            slot = lax.rem(i, 2)
            within(i - 2, units, lambda j: out_copy(j).wait())
            gout[slot, :, 0:WIDE_A] = one.z_total()
            one.z_sent()
            gout[slot, :, WIDE_A:] = two.total()
            out_copy(i).start()
            give(i, c_cred, me.sib)
            give(i, y_cred, me.ypeer)

            @pl.when(me.edge)
            def _():
                give(i, z_cred.at[0], me.near)
                give(i, z_cred.at[2], me.mid)

            @pl.when(me.inner)
            def _():
                give(i, z_cred.at[0], me.near)
                give(i, z_cred.at[1], me.mid)

        within(r, units, first)
        within(r - 1, units, second)
        within(r - 2, units, third)
        within(r - 3, units, fourth)
        within(r - 4, units, fifth)

    def put(pair, i, value):
        columns = slice(i * 256, (i + 1) * 256)
        part[lax.rem(pair, 2), :, :, :, :, columns] = value.astype(BF16).reshape(4, 2, 2, depth, 256)

    def x_copy(e, r):
        rows = pl.ds(pl.multiple_of(r * 128, 128), 128)
        return remote(xs.at[rows], xr.at[rows], x_send.at[e, r], x_recv.at[e, r], me.xpeer)

    def give_x():
        pl.semaphore_signal(x_cred, inc=1, device_id=me.xpeer, device_id_type=MESH)

    def take_x():
        pl.semaphore_wait(x_cred, 1)

    for copy in own:
        copy.wait()
    gather_g.start(0)
    ag(-5)
    ag(-4)
    gather_g.hand(0)
    gather_g.turn(0)
    ag(-3)
    local(cot, eb, 3).wait()
    transpose_into(et, eb)
    gather_g.core(0)
    ag(-2)
    gather_g.done(0)
    gain_rows[...] = gw[0].reshape(WIDE, 128).astype(F32).T[:8, :]
    ag(-1)

    @pl.loop(0, ROWS // 64)
    def _(i):
        rows = pl.ds(pl.multiple_of(i * 64, 64), 64)
        x = tokens[rows, :].astype(F32)
        r = lax.rsqrt(jnp.mean(x * x, axis=-1, keepdims=True) + epsilon)
        a_buf[rows, :] = (x * r * gain_rows[0:1, :]).astype(BF16)

    ag(0)
    transpose_into(at, a_buf)
    ag(1)
    ag(2)
    load_start(0, 0, 0)
    ag(3)
    load_start(1, 0, 1)
    load_wait(0, 0, 0)
    for s in range(2):
        rows = pl.ds(s * SPAN, SPAN)
        key = turn(dot_nn(a_buf[rows, :], weight(wbuf, 0, 0, UNIT)), cosine[...], sine[...])
        kvx[y, k, rows, 0:UNIT] = key.astype(BF16)
    load_wait(1, 0, 1)
    kvx[y, k, :, UNIT:] = dot_nn(a_buf[...], weight(wbuf, 0, UNIT, 2 * UNIT)).astype(BF16)

    def kv_copy(i):
        part_kv = kvx.at[y, k] if i == 0 else kvx.at[:, k]
        return remote(part_kv, part_kv, kv_send.at[0, i], kv_recv.at[0, i], me.ypeer if i == 0 else me.sib)

    kv_copy(0).start()
    ag(4)
    load_start(2, 1, 0)
    ag(5)
    load_start(3, 1, 1)
    load_wait(2, 1, 0)
    load_wait(3, 1, 1)
    for side in range(2):
        for s in range(2):
            rows = pl.ds(s * SPAN, SPAN)
            query = dot_nn(a_buf[rows, :], weight(wbuf, 1, side * UNIT, (side + 1) * UNIT))
            query = turn(query, cosine[...], sine[...])
            for i, head in enumerate(unpack_heads(query)):
                qh[s * 8 + side * 4 + i] = head.astype(BF16)
    kv_copy(0).wait_recv()
    kv_copy(1).start()
    ag(6)
    load_start(4, 0, 0)
    ag(7)
    load_start(5, 0, 1)
    kv_copy(1).wait_recv()

    @pl.loop(0, 8)
    def _(i):
        s, c = lax.div(i, 4), lax.rem(i, 4)
        block = kvx[lax.div(c, 2), lax.rem(c, 2), pl.ds(pl.multiple_of(s * SPAN, SPAN), SPAN), :]
        rows = pl.ds(pl.multiple_of(c * SPAN, SPAN), SPAN)
        for g, head in enumerate(unpack_heads(block[:, :UNIT].astype(F32))):
            kh[s * 4 + g, rows, :] = head.astype(BF16)
        for g, head in enumerate(unpack_heads(block[:, UNIT:].astype(F32))):
            vh[s * 4 + g, rows, :] = head.astype(BF16)

    def attend(i):
        s, h = lax.div(i, 8), lax.rem(i, 8)
        g = s * 4 + lax.div(h, 2)
        scores = dot_nt(kh[g], qh[i]) * scale
        scores = jnp.where(allowed_keys(low[s], high[...]), scores, negative)
        top = jnp.max(scores, axis=0, keepdims=True)
        p = jnp.exp(scores - top)
        total = jnp.sum(p, axis=0, keepdims=True)
        lse[i] = jnp.broadcast_to(top + jnp.log(total), (8, SPAN))
        heads[h] = (dot_tn(vh[g], p.astype(BF16)) / total).T

    for s in range(2):
        pl.loop(8 * s, 8 * s + 8)(attend)
        rows = slice(s * SPAN, (s + 1) * SPAN)
        for side in range(2):
            mixed = pack_heads([heads[side * 4 + i] for i in range(4)])
            ob[rows, side * UNIT : (side + 1) * UNIT] = mixed.astype(BF16)
        if s == 0:
            load_wait(4, 0, 0)
            load_wait(5, 0, 1)
        xs[rows, :] = dot_nt(ob[rows, :], weight(wbuf, 0, 0, 2 * UNIT)).astype(BF16)
        x_copy(0, 2 * s).start()
        x_copy(0, 2 * s + 1).start()
        ag(8 + s)

    for s in range(2):
        ag(10 + 2 * s)

        @pl.loop(2 * s, 2 * s + 2)
        def _(r):
            x_copy(0, r).wait()
            rows = pl.ds(pl.multiple_of(r * 128, 128), 128)
            x = tokens[rows, :].astype(F32) + (xs[rows, :].astype(F32) + xr[rows, :].astype(F32))
            x2[rows, :] = x
            r2 = lax.rsqrt(jnp.mean(x * x, axis=-1, keepdims=True) + epsilon)
            a_buf[rows, :] = (x * r2 * gain_rows[1:2, :]).astype(BF16)

        ag(11 + 2 * s)
    give_x()
    transpose_into(bt, a_buf)
    acc[...] = jnp.zeros_like(acc)
    out_acc[...] = jnp.zeros_like(out_acc)

    def stage_copy(n):
        slot = lax.rem(n, 2)
        return pltpu.make_async_copy(stage.at[slot], fed.at[n], stage_sem.at[slot])

    def back_copy(n):
        slot = lax.rem(n, 2)
        return pltpu.make_async_copy(fed.at[n], back.at[slot], back_sem.at[slot])

    def feed_grads(n, pair, ready):
        slot = lax.rem(n, 2)
        back_copy(n).wait()
        put(pair, 0, dot_nn(bt[...], back[slot, 0]))
        put(pair, 1, dot_nn(bt[...], back[slot, 1]))
        put(pair, 2, dot_nn(et[...], back[slot, 2]))
        if ready:
            within(n + 1, groups, lambda i: back_copy(i).start())

    @pl.loop(0, groups)
    def _(n):
        slot = lax.rem(n, 2)
        ag(14 + n + jnp.maximum(n - 5, 0))

        @pl.when((n == 5) | (n == 6))
        def _():
            ag(15 + n + jnp.maximum(n - 5, 0))

        for side in range(2):
            load_start(6 + 2 * n + side, slot, side)

        @pl.when((n == 2) | (n == 4) | (n == 6))
        def _():
            pair = lax.div(n, 2) - 1
            feed_grads(pair, pair, False)

        @pl.when(n >= 2)
        def _():
            rs(n - 2)

        @pl.when(n >= 1)
        def _():
            stage_copy(n - 1).wait()

        @pl.when(lax.rem(n, 2) == 1)
        def _():
            back_copy(lax.div(n, 2)).start()

        for side in range(2):
            load_wait(6 + 2 * n + side, slot, side)
        gate = dot_nn(a_buf[...], weight(wbuf, slot, 0, 256))
        up = dot_nn(a_buf[...], weight(wbuf, slot, 256, 512))
        sg = jax.nn.sigmoid(gate)
        silu = gate * sg
        stage[slot, 2] = (silu * up).astype(BF16)
        dh = dot_nn(eb[...], weight(wbuf, slot, 512, 768))
        stage[slot, 0] = (dh * up * sg * (1.0 + gate * (1.0 - sg))).astype(BF16)
        stage[slot, 1] = (dh * silu).astype(BF16)
        stage_copy(n).start()

        @pl.loop(0, 4)
        def _(i):
            columns = pl.ds(pl.multiple_of(i * 4 * depth, 128), 4 * depth)

            def rows_of(lo):
                return wbuf[slot, i, :, :, :, lo : lo + 256].reshape(4 * depth, 256)

            out_acc[:, columns] += dot_nt(stage[slot, 2], rows_of(512))
            acc[:, columns] += dot_nt(stage[slot, 0], rows_of(0)) + dot_nt(stage[slot, 1], rows_of(256))

    load_start(4, 0, 0)
    load_start(5, 0, 1)
    take_x()
    for r in range(4):
        rows = slice(r * 128, (r + 1) * 128)
        xs[rows, :] = acc[rows, :].astype(BF16)
        x_copy(1, r).start()
    stage_copy(groups - 1).wait()

    gacc[...] = jnp.zeros_like(gacc)

    def norm_back(r):
        x_copy(1, r).wait()
        rows = pl.ds(pl.multiple_of(r * 128, 128), 128)
        mine = xs[rows, :].astype(F32)
        db = mine + xr[rows, :].astype(F32)
        x = x2[rows, :]
        r2 = lax.rsqrt(jnp.mean(x * x, axis=-1, keepdims=True) + epsilon)
        n2 = x * r2
        gacc[1:2, :] += jnp.sum(mine * n2, axis=0, keepdims=True)
        scaled = db * gain_rows[1:2, :]
        dx2 = eb[rows, :].astype(F32) + r2 * (scaled - n2 * jnp.mean(scaled * n2, axis=-1, keepdims=True))
        acc[rows, :] = dx2
        eb[rows, :] = dx2.astype(BF16)

    feed_grads(3, 3, True)
    rs(6)
    rs(7)
    pl.loop(0, 2)(norm_back)
    feed_grads(4, 4, True)
    rs(8)
    rs(9)
    pl.loop(2, 4)(norm_back)

    give_x()
    xs[...] = out_acc[...].astype(BF16)
    take_x()
    for r in range(4):
        x_copy(2, r).start()

    load_wait(4, 0, 0)
    load_wait(5, 0, 1)
    for s in range(2):
        rows = slice(s * SPAN, (s + 1) * SPAN)
        for side in range(2):
            mixed = dot_nn(eb[rows, :], weight(wbuf, 0, side * UNIT, (side + 1) * UNIT)).astype(BF16)
            for i, head in enumerate(unpack_heads(mixed.astype(F32))):
                doh[s * 8 + side * 4 + i] = head.astype(BF16)
    feed_grads(5, 5, True)
    rs(10)
    for side in range(2):
        load_start(2 + side, 0, side)
        load_start(side, 1, side)

    def attend_back(i):
        s, g = lax.div(i, 4), lax.rem(i, 4)
        mask = allowed_keys(low[s], high[...])
        dk = jnp.zeros((4 * SPAN, 128), F32)
        dv = jnp.zeros((4 * SPAN, 128), F32)
        for hh in range(2):
            h = s * 8 + 2 * g + hh
            scores = jnp.where(mask, dot_nt(kh[i], qh[h]) * scale, negative)
            p = jnp.exp(scores - lse[h][0:1, :])
            dp = dot_nt(vh[i], doh[h])
            delta = jnp.sum(p * dp, axis=0, keepdims=True)
            ds = (p * (dp - delta) * scale).astype(BF16)
            dv += dot_nn(p.astype(BF16), doh[h])
            dk += dot_nn(ds, qh[h])
            heads[2 * g + hh] = dot_tn(kh[i], ds).T
        dkh[g] = dk.astype(BF16)
        dvh[g] = dv.astype(BF16)

    def dkv_mine(s, core):
        return kvx.at[:, core, pl.ds(pl.multiple_of(s * SPAN, SPAN), SPAN)]

    def kv_core(s):
        return remote(dkv_mine(s, me.ok), rc.at[s], kv_send.at[1, s], kv_recv.at[1, s], me.sib)

    def kv_y(s):
        return remote(rc.at[s, me.oy], ry.at[s], kv_send.at[2, s], kv_recv.at[2, s], me.ypeer)

    def kv_add(s):
        kv_core(s).wait_recv()
        rc[s] = rc[s] + dkv_mine(s, k)[...]
        kv_y(s).start()

    kv_copy(0).wait_send()
    kv_copy(1).wait_send()

    @pl.loop(0, 2)
    def _(s):
        attend_back(4 * s)
        attend_back(4 * s + 1)
        rs(11 + 2 * s)
        attend_back(4 * s + 2)
        attend_back(4 * s + 3)
        rows = pl.ds(pl.multiple_of(s * SPAN, SPAN), SPAN)
        for c in range(4):
            at_c = slice(c * SPAN, (c + 1) * SPAN)
            for j, src in enumerate((dkh, dvh)):
                kvx[c // 2, c % 2, rows, j * UNIT : (j + 1) * UNIT] = pack_heads(
                    [src[g, at_c, :].astype(F32) for g in range(4)]
                ).astype(BF16)
        kv_core(s).start()
        for side in range(2):
            dq = turn(pack_heads([heads[side * 4 + j] for j in range(4)]), cosine[...], -sine[...])
            dqb[rows, side * UNIT : (side + 1) * UNIT] = dq.astype(BF16)
        feed_grads(6 + s, 6 + s, True)
        rs(12 + 2 * s)
        kv_add(s)

    transpose_into(bt, eb)
    for i in range(3):
        put(8, i, dot_nn(bt[...], ob[:, i * 256 : (i + 1) * 256]))
    rs(15)
    rs(16)

    for r in range(4):
        rows = slice(r * 128, (r + 1) * 128)
        x_copy(2, r).wait()
        xs[rows, :] = (x2[rows, :] + (xs[rows, :].astype(F32) + xr[rows, :].astype(F32))).astype(BF16)
    give_x()
    local(xs, output, 0).start()
    for i in range(3):
        put(9, i, dot_nn(at[...], dqb[:, i * 256 : (i + 1) * 256]))
    rs(17)
    rs(18)
    for side in range(2):
        load_wait(2 + side, 0, side)
        load_wait(side, 1, side)
    for s in range(2):
        rows = slice(s * SPAN, (s + 1) * SPAN)
        kv_y(s).wait_recv()
        total = rc[s, y].astype(F32) + ry[s].astype(F32)
        dkvb[rows, :UNIT] = turn(total[:, :UNIT], cosine[...], -sine[...]).astype(BF16)
        dkvb[rows, UNIT:] = total[:, UNIT:].astype(BF16)
    for i in range(3):
        put(10, i, dot_nn(at[...], dkvb[:, i * 256 : (i + 1) * 256]))
    rs(19)
    rs(20)
    local(xs, output, 0).wait()
    take_x()

    def first_norm(rows):
        x = tokens[rows, :].astype(F32)
        r1 = lax.rsqrt(jnp.mean(x * x, axis=-1, keepdims=True) + epsilon)
        return r1, x * r1

    for s in range(2):
        rows = slice(s * SPAN, (s + 1) * SPAN)
        da = dot_nt(dqb[rows, :], weight(wbuf, 0, 0, 768)) + dot_nt(dkvb[rows, :], weight(wbuf, 1, 0, 768))
        xs[rows, :] = da.astype(BF16)
        x_copy(3, 2 * s).start()
        x_copy(3, 2 * s + 1).start()
    rs(21)

    @pl.loop(0, 4)
    def _(r):
        rows = pl.ds(pl.multiple_of(r * 128, 128), 128)
        gacc[0:1, :] += jnp.sum(xs[rows, :].astype(F32) * first_norm(rows)[1], axis=0, keepdims=True)

    gain_columns = jnp.concatenate([gacc[...], jnp.zeros((120, WIDE), F32)], axis=0).T
    gp[...] = gain_columns.astype(BF16).reshape(4, 2, 2, depth, 128)
    gain = ReduceA(me, 0, gp.at[:, :, me.ok], gp.at[:, :, k], (g1, g2, g3), rg_sems)
    gain.core()
    rs(22)
    gain.add_core()
    gain.y_start()
    rs(23)
    gain.y_add()
    gain.z_first()

    @pl.loop(0, 4)
    def _(r):
        x_copy(3, r).wait()
        rows = pl.ds(pl.multiple_of(r * 128, 128), 128)
        da = xs[rows, :].astype(F32) + xr[rows, :].astype(F32)
        r1, n1 = first_norm(rows)
        scaled = da * gain_rows[0:1, :]
        acc[rows, :] += r1 * (scaled - n1 * jnp.mean(scaled * n1, axis=-1, keepdims=True))

    local(acc, grad_tokens, 0).start()
    gain.z_second()
    rs(24)
    gs[0] = gain.z_total()
    gain.z_sent()
    pair_copy = remote(gs.at[0], gs.at[1], g_sems.at[0], g_sems.at[1], me.xpeer)
    pair_copy.start()
    rs(25)
    pair_copy.wait()
    gain_grads[...] = gs[0] + gs[1]
    for s in range(2):
        kv_core(s).wait_send()
        kv_y(s).wait_send()
    gather_g.sent(0)

    @pl.loop(0, units)
    def _(u):
        gather_a.sent(u)
        gather_b.sent(u)

    out_copy(units - 2).wait()
    out_copy(units - 1).wait()
    local(acc, grad_tokens, 0).wait()


def rope_inputs(row_count):
    positions = lax.axis_index("ctx") * row_count + jnp.arange(row_count, dtype=jnp.int32)
    cosine_table, sine_table = rope_tables(positions)
    cosine = jnp.tile(cosine_table, (1, 2 * UNIT // HD))
    sine = jnp.tile(jnp.concatenate([-sine_table, sine_table], axis=1), (1, UNIT // HD))
    return positions, cosine, sine


def pack_weights(w_query, w_key, w_value, w_out, w_gate, w_up, w_down):
    depth = w_query.shape[0]
    groups = w_gate.shape[1] // 256
    fed = jnp.concatenate(
        [part.reshape(depth, groups, 256) for part in (w_gate, w_up, w_down.T)], axis=2
    ).reshape(depth, groups * 2 * UNIT)
    flat = jnp.concatenate([w_key, w_value, w_query, w_out.T, fed], axis=1)
    cut = jnp.transpose(flat.reshape(depth, flat.shape[1] // UNIT, UNIT), (1, 0, 2))
    return cut[:, :, :WIDE_A], cut[:, :, WIDE_A:]


def pack_gains(gain_attn, gain_mlp):
    return jnp.pad(jnp.stack([gain_attn, gain_mlp], axis=1), ((0, 0), (0, 126)))[None]


def call_layer(packed_a, packed_b, gains, tokens, cot, cosine, sine, low, high):
    units, depth = packed_a.shape[0], packed_a.shape[1]
    groups = (units - 6) // 2
    struct = jax.ShapeDtypeStruct
    vmem = pltpu.VMEM
    any_spec = pl.BlockSpec(memory_space=pl.ANY)
    vmem_spec = pl.BlockSpec(memory_space=pltpu.VMEM)
    block = (4, 2, 2, depth)
    dma = pltpu.SemaphoreType.DMA
    regular = pltpu.SemaphoreType.REGULAR

    def gather_sems(count):
        return (dma((count, 3)),) + tuple(dma((count,)) for _ in range(5))

    def reduce_sems(count):
        return tuple(dma((count,)) for _ in range(6)) + (dma((count, 3)), dma((count, 2)))

    return pl.pallas_call(
        layer_kernel,
        out_shape=(
            struct((ROWS, WIDE), BF16),
            struct((ROWS, WIDE), F32),
            struct((units, depth, UNIT), F32),
            struct((depth, 128), F32),
            struct((units,) + block + (WIDE_A,), BF16),
            struct((units,) + block + (WIDE_B,), BF16),
            struct((groups, 3, ROWS, 256), BF16),
        ),
        in_specs=[any_spec] * 3 + [vmem_spec, any_spec] + [vmem_spec] * 4,
        out_specs=(any_spec,) * 3 + (vmem_spec,) + (any_spec,) * 3,
        scratch_shapes=[
            vmem((1,) + block + (128,), BF16),
            vmem((8, WIDE), F32),
            vmem((ROWS, WIDE), BF16),
            vmem((WIDE, ROWS), BF16),
            vmem((WIDE, ROWS), BF16),
            vmem((WIDE, ROWS), BF16),
            vmem((ROWS, WIDE), BF16),
            vmem((2, 2, ROWS, 2 * UNIT), BF16),
            vmem((16, SPAN, 128), BF16),
            vmem((8, 4 * SPAN, 128), BF16),
            vmem((8, 4 * SPAN, 128), BF16),
            vmem((16, 8, SPAN), F32),
            vmem((ROWS, 2 * UNIT), BF16),
            vmem((ROWS, WIDE), F32),
            vmem((ROWS, WIDE), F32),
            vmem((ROWS, WIDE), F32),
            vmem((2,) + block + (2 * UNIT,), BF16),
            vmem((2,) + block + (2 * UNIT,), BF16),
            vmem((2, 3, ROWS, 256), BF16),
            vmem((2, 3, ROWS, 256), BF16),
            vmem((RING, 4, 2, depth, WIDE_A), BF16),
            vmem((RING, 4, depth, WIDE_A), BF16),
            vmem((RING, 4, depth, WIDE_A), BF16),
            vmem((RING, 4, 2, depth, WIDE_B), BF16),
            vmem((RING, depth, WIDE_B), BF16),
            vmem((RING, 4, 2, depth, WIDE_B), BF16),
            vmem((2, depth, UNIT), F32),
            vmem((ROWS, WIDE), BF16),
            vmem((ROWS, WIDE), BF16),
            vmem((16, SPAN, 128), BF16),
            vmem((8, SPAN, 128), F32),
            vmem((4, 4 * SPAN, 128), BF16),
            vmem((4, 4 * SPAN, 128), BF16),
            vmem((2, 2, SPAN, 2 * UNIT), BF16),
            vmem((2, SPAN, 2 * UNIT), BF16),
            vmem((ROWS, 2 * UNIT), BF16),
            vmem((ROWS, 2 * UNIT), BF16),
            vmem((8, WIDE), F32),
            vmem(block + (128,), BF16),
            vmem((4, 2, depth, 128), BF16),
            vmem((4, depth, 128), BF16),
            vmem((4, depth, 128), BF16),
            vmem((2, depth, 128), F32),
            gather_sems(units),
            gather_sems(units),
            gather_sems(1),
            reduce_sems(units),
            reduce_sems(units),
            reduce_sems(1),
            regular,
            regular,
            regular((3,)),
            regular,
            dma((4, 4)),
            dma((4, 4)),
            dma((3, 2)),
            dma((3, 2)),
            dma((2,)),
            dma((4,)),
            dma((2, 2, 2)),
            dma((2,)),
            dma((2,)),
            dma((2,)),
        ],
        compiler_params=pltpu.CompilerParams(
            collective_id=1, has_side_effects=True, vmem_limit_bytes=64 << 20
        ),
        name="layer",
    )(packed_a, packed_b, gains, tokens, cot, cosine, sine, low, high)


def fast_body(
    tokens,
    segments,
    cotangent,
    gain_attn,
    w_query,
    w_key,
    w_value,
    w_out,
    gain_mlp,
    w_gate,
    w_up,
    w_down,
):
    positions, cosine, sine = rope_inputs(SPAN)
    mine = lax.dynamic_slice_in_dim(segments, positions[0], SPAN, 1)
    low = jnp.sum((segments[:, None, :] < mine[:, :, None]).astype(jnp.int32), axis=-1)[:, None, :]
    high = positions[None, :]
    packed_a, packed_b = pack_weights(w_query, w_key, w_value, w_out, w_gate, w_up, w_down)
    output, grad_tokens, grads, gain_grads = call_layer(
        packed_a,
        packed_b,
        pack_gains(gain_attn, gain_mlp),
        tokens.reshape(ROWS, WIDE),
        cotangent.reshape(ROWS, WIDE),
        cosine,
        sine,
        low,
        high,
    )[:4]

    def span(lo, hi):
        return jnp.concatenate([grads[i] for i in range(lo, hi)], axis=1)

    fed = [span(2 * i, 2 * i + 2) for i in range(8)]
    gate_grad, up_grad, down_grad = (
        jnp.concatenate([group[:, i * 256 : (i + 1) * 256] for group in fed], axis=1) for i in range(3)
    )
    return (
        output.reshape(tokens.shape),
        grad_tokens.reshape(tokens.shape),
        gain_grads[:, 0],
        span(18, 20),
        grads[20],
        grads[21],
        span(16, 18).T,
        gain_grads[:, 1],
        gate_grad,
        up_grad,
        down_grad.T,
    )


def fits(mesh):
    return mesh.shape["fsdp"] == 4 and mesh.shape["ctx"] == 4 and mesh.shape["tp"] == 2


def solution(mesh):
    placed = (
        P("fsdp", "ctx", None),
        P("fsdp", None),
        P("fsdp", "ctx", None),
        P(("fsdp", "ctx")),
        P(("fsdp", "ctx"), "tp"),
        P(("fsdp", "ctx"), "tp"),
        P(("fsdp", "ctx"), "tp"),
        P("tp", ("fsdp", "ctx")),
        P(("fsdp", "ctx")),
        P(("fsdp", "ctx"), "tp"),
        P(("fsdp", "ctx"), "tp"),
        P("tp", ("fsdp", "ctx")),
    )
    return jax.shard_map(
        fast_body if fits(mesh) else body,
        mesh=mesh,
        in_specs=placed,
        out_specs=(
            P("fsdp", "ctx", None),
            P("fsdp", "ctx", None),
            P(("fsdp", "ctx")),
            P(("fsdp", "ctx"), "tp"),
            P(("fsdp", "ctx"), "tp"),
            P(("fsdp", "ctx"), "tp"),
            P("tp", ("fsdp", "ctx")),
            P(("fsdp", "ctx")),
            P(("fsdp", "ctx"), "tp"),
            P(("fsdp", "ctx"), "tp"),
            P("tp", ("fsdp", "ctx")),
        ),
        check_vma=False,
    )
```

```python
import math

import jax
import jax.numpy as jnp
from jax import lax
from jax.experimental import pallas as pl
from jax.experimental.pallas import tpu as pltpu
from jax.sharding import PartitionSpec as P

HD = 96
GROUP = 2


epsilon = 1e-05
rope_base = 100000.0
negative = -1e30


def rope_tables(positions):
    half_width = HD // 2
    frequency = rope_base ** (-(2.0 * jnp.arange(half_width, dtype=jnp.float32)) / HD)
    angles = positions.astype(jnp.float32)[:, None] * frequency[None, :]
    return (jnp.cos(angles), jnp.sin(angles))


def rotate(vectors, cosine_table, sine_table):
    half_width = vectors.shape[-1] // 2
    former = vectors[..., :half_width]
    latter = vectors[..., half_width:]
    return jnp.concatenate(
        [former * cosine_table - latter * sine_table, latter * cosine_table + former * sine_table],
        axis=-1,
    )


def head_sum(partial_rows):
    return lax.psum(partial_rows.astype(jnp.bfloat16), "tp").astype(jnp.float32)


def weight_gather(shards):
    row_parts = (
        lax.all_gather(shards[0], ("fsdp", "ctx"), axis=0, tiled=True),
        lax.all_gather(shards[1], ("fsdp", "ctx"), axis=0, tiled=True),
        lax.all_gather(shards[2], ("fsdp", "ctx"), axis=0, tiled=True),
        lax.all_gather(shards[3], ("fsdp", "ctx"), axis=0, tiled=True),
        lax.all_gather(shards[4], ("fsdp", "ctx"), axis=0, tiled=True),
        lax.all_gather(shards[5], ("fsdp", "ctx"), axis=0, tiled=True),
        lax.all_gather(shards[6], ("fsdp", "ctx"), axis=0, tiled=True),
    )
    column_parts = (
        lax.all_gather(shards[7], ("fsdp", "ctx"), axis=1, tiled=True),
        lax.all_gather(shards[8], ("fsdp", "ctx"), axis=1, tiled=True),
    )
    return tuple(row_parts) + tuple(column_parts)


def grad_reduce(gradients):
    row_parts = (
        lax.psum_scatter(gradients[0], ("fsdp", "ctx"), scatter_dimension=0, tiled=True),
        lax.psum_scatter(gradients[1], ("fsdp", "ctx"), scatter_dimension=0, tiled=True),
        lax.psum_scatter(gradients[2], ("fsdp", "ctx"), scatter_dimension=0, tiled=True),
        lax.psum_scatter(gradients[3], ("fsdp", "ctx"), scatter_dimension=0, tiled=True),
        lax.psum_scatter(gradients[4], ("fsdp", "ctx"), scatter_dimension=0, tiled=True),
        lax.psum_scatter(gradients[5], ("fsdp", "ctx"), scatter_dimension=0, tiled=True),
        lax.psum_scatter(gradients[6], ("fsdp", "ctx"), scatter_dimension=0, tiled=True),
    )
    column_parts = (
        lax.psum_scatter(gradients[7], ("fsdp", "ctx"), scatter_dimension=1, tiled=True),
        lax.psum_scatter(gradients[8], ("fsdp", "ctx"), scatter_dimension=1, tiled=True),
    )
    return tuple(row_parts) + tuple(column_parts)


def block_scores(queries, key_block, query_seg, positions, key_seg, key_start):
    score_scale = 1.0 / math.sqrt(queries.shape[-1])
    key_positions = key_start + jnp.arange(key_block.shape[0], dtype=jnp.int32)
    allowed = (query_seg[:, None] == key_seg[None, :]) & (
        positions[:, None] >= key_positions[None, :]
    )
    raw_scores = jnp.einsum(
        "qhgd,khd->hgqk", queries, key_block, preferred_element_type=jnp.float32
    )
    return (jnp.where(allowed, raw_scores * score_scale, negative), allowed)


def block_fetch(
    key_all, value_all, segment_row, block_index, block_keys, last_position, first_segment
):
    key_start = block_index * block_keys
    key_block = lax.dynamic_slice_in_dim(key_all, key_start, block_keys, 0)
    value_block = lax.dynamic_slice_in_dim(value_all, key_start, block_keys, 0)
    key_seg = lax.dynamic_slice_in_dim(segment_row, key_start, block_keys, 0)
    needed = (key_start <= last_position) & (key_seg[block_keys - 1] >= first_segment)
    return (key_start, key_block, value_block, key_seg, needed)


def attention_forward(queries, key_all, value_all, segment_row, query_seg, positions):
    row_count, heads_kv, group_size, head_dim = queries.shape
    length = key_all.shape[0]
    block_keys = math.gcd(512, length)
    block_total = length // block_keys
    last_position = positions[row_count - 1]
    first_segment = query_seg[0]

    def stats_step(block_index, state):
        key_start, key_block, value_block, key_seg, needed = block_fetch(
            key_all, value_all, segment_row, block_index, block_keys, last_position, first_segment
        )
        top_old, total_old = state
        scores, allowed = block_scores(queries, key_block, query_seg, positions, key_seg, key_start)
        top_new = jnp.maximum(top_old, jnp.max(scores, axis=-1))
        weights = jnp.where(allowed, jnp.exp(scores - top_new[..., None]), 0.0)
        return (top_new, total_old * jnp.exp(top_old - top_new) + jnp.sum(weights, axis=-1))

    start_top = jnp.full((heads_kv, group_size, row_count), negative, jnp.float32)
    row_top, row_total = lax.fori_loop(
        0, block_total, stats_step, (start_top, jnp.zeros_like(start_top))
    )

    def output_step(block_index, state):
        key_start, key_block, value_block, key_seg, needed = block_fetch(
            key_all, value_all, segment_row, block_index, block_keys, last_position, first_segment
        )
        scores, allowed = block_scores(queries, key_block, query_seg, positions, key_seg, key_start)
        probability = (
            jnp.where(allowed, jnp.exp(scores - row_top[..., None]), 0.0) / row_total[..., None]
        )
        return state + jnp.einsum(
            "hgqk,khd->qhgd",
            probability.astype(jnp.bfloat16),
            value_block,
            preferred_element_type=jnp.float32,
        )

    start_out = jnp.zeros((row_count, heads_kv, group_size, head_dim), jnp.float32)
    out_low = lax.fori_loop(0, block_total, output_step, start_out)
    return (row_top, row_total, out_low)


def attention_backward(
    queries,
    key_all,
    value_all,
    segment_row,
    query_seg,
    positions,
    row_top,
    row_total,
    grad_mixed,
    row_delta,
):
    row_count, heads_kv, group_size, head_dim = queries.shape
    length = key_all.shape[0]
    block_keys = math.gcd(512, length)
    block_total = length // block_keys
    last_position = positions[row_count - 1]
    first_segment = query_seg[0]
    score_scale = 1.0 / math.sqrt(head_dim)

    def grad_step(block_index, state):
        key_start, key_block, value_block, key_seg, needed = block_fetch(
            key_all, value_all, segment_row, block_index, block_keys, last_position, first_segment
        )
        grad_query, grad_keys, grad_values = state
        scores, allowed = block_scores(queries, key_block, query_seg, positions, key_seg, key_start)
        probability = (
            jnp.where(allowed, jnp.exp(scores - row_top[..., None]), 0.0) / row_total[..., None]
        )
        grad_prob = jnp.einsum(
            "qhgd,khd->hgqk", grad_mixed, value_block, preferred_element_type=jnp.float32
        )
        grad_score = (probability * (grad_prob - row_delta[..., None]) * score_scale).astype(
            jnp.bfloat16
        )
        grad_query = grad_query + jnp.einsum(
            "hgqk,khd->qhgd", grad_score, key_block, preferred_element_type=jnp.float32
        )
        key_part = jnp.einsum(
            "hgqk,qhgd->khd", grad_score, queries, preferred_element_type=jnp.float32
        )
        value_part = jnp.einsum(
            "hgqk,qhgd->khd",
            probability.astype(jnp.bfloat16),
            grad_mixed,
            preferred_element_type=jnp.float32,
        )
        grad_keys = lax.dynamic_update_slice_in_dim(grad_keys, key_part, key_start, 0)
        grad_values = lax.dynamic_update_slice_in_dim(grad_values, value_part, key_start, 0)
        return (grad_query, grad_keys, grad_values)

    start_query = jnp.zeros((row_count, heads_kv, group_size, head_dim), jnp.float32)
    start_keys = jnp.zeros((length, heads_kv, head_dim), jnp.float32)
    return lax.fori_loop(0, block_total, grad_step, (start_query, start_keys, start_keys))


def micro_step(gathered, token_rows, segment_row, grad_in, positions, cosine_table, sine_table):
    gain_attn, w_query, w_key, w_value, gain_mlp, w_gate, w_up, w_out, w_down = gathered
    row_count = token_rows.shape[0]
    heads_kv = w_key.shape[1] // HD
    cos_four = cosine_table[:, None, None, :]
    sin_four = sine_table[:, None, None, :]
    cos_three = cosine_table[:, None, :]
    sin_three = sine_table[:, None, :]
    query_seg = lax.dynamic_slice_in_dim(segment_row, positions[0], row_count, 0)
    gain_first = gain_attn.astype(jnp.float32)
    gain_second = gain_mlp.astype(jnp.float32)
    inputs = token_rows.astype(jnp.float32)
    scale_first = lax.rsqrt(jnp.mean(inputs * inputs, axis=-1, keepdims=True) + epsilon)
    normal_first = inputs * scale_first
    normed = (normal_first * gain_first).astype(jnp.bfloat16)
    query_raw = jnp.dot(normed, w_query, preferred_element_type=jnp.float32).reshape(
        row_count, heads_kv, GROUP, HD
    )
    key_raw = jnp.dot(normed, w_key, preferred_element_type=jnp.float32).reshape(
        row_count, heads_kv, HD
    )
    value_low = (
        jnp.dot(normed, w_value, preferred_element_type=jnp.float32)
        .astype(jnp.bfloat16)
        .reshape(row_count, heads_kv, HD)
    )
    query_low = rotate(query_raw, cos_four, sin_four).astype(jnp.bfloat16)
    key_low = rotate(key_raw, cos_three, sin_three).astype(jnp.bfloat16)
    key_all, value_all = (
        lax.all_gather(key_low, "ctx", axis=0, tiled=True),
        lax.all_gather(value_low, "ctx", axis=0, tiled=True),
    )
    row_top, row_total, out_low = attention_forward(
        query_low, key_all, value_all, segment_row, query_seg, positions
    )
    mixed_low = out_low.reshape(row_count, -1).astype(jnp.bfloat16)
    middle = inputs + head_sum(jnp.dot(mixed_low, w_out, preferred_element_type=jnp.float32))
    scale_second = lax.rsqrt(jnp.mean(middle * middle, axis=-1, keepdims=True) + epsilon)
    normal_second = middle * scale_second
    second = (normal_second * gain_second).astype(jnp.bfloat16)
    gate_part = jnp.dot(second, w_gate, preferred_element_type=jnp.float32)
    upward = jnp.dot(second, w_up, preferred_element_type=jnp.float32)
    sigmoid_gate = jax.nn.sigmoid(gate_part)
    silu_gate = gate_part * sigmoid_gate
    hidden = (silu_gate * upward).astype(jnp.bfloat16)
    result_rows = middle + head_sum(jnp.dot(hidden, w_down, preferred_element_type=jnp.float32))
    output_rows = result_rows.astype(jnp.bfloat16)
    grad_final = grad_in.astype(jnp.float32)
    grad_down = jnp.einsum("tf,td->fd", hidden, grad_in, preferred_element_type=jnp.float32)
    grad_hidden = jnp.einsum("td,fd->tf", grad_in, w_down, preferred_element_type=jnp.float32)
    grad_gate_low = (
        grad_hidden * upward * sigmoid_gate * (1.0 + gate_part * (1.0 - sigmoid_gate))
    ).astype(jnp.bfloat16)
    grad_up_low = (grad_hidden * silu_gate).astype(jnp.bfloat16)
    grad_gate = jnp.einsum("td,tf->df", second, grad_gate_low, preferred_element_type=jnp.float32)
    grad_up = jnp.einsum("td,tf->df", second, grad_up_low, preferred_element_type=jnp.float32)
    grad_second = head_sum(
        jnp.einsum("tf,df->td", grad_gate_low, w_gate, preferred_element_type=jnp.float32)
        + jnp.einsum("tf,df->td", grad_up_low, w_up, preferred_element_type=jnp.float32)
    )
    scaled_second = grad_second * gain_second
    grad_gain_mlp = jnp.sum(grad_second * normal_second, axis=0)
    grad_middle = grad_final + scale_second * (
        scaled_second
        - normal_second * jnp.mean(scaled_second * normal_second, axis=-1, keepdims=True)
    )
    grad_middle_low = grad_middle.astype(jnp.bfloat16)
    grad_out = jnp.einsum(
        "tk,td->kd", mixed_low, grad_middle_low, preferred_element_type=jnp.float32
    )
    grad_mixed = (
        jnp.einsum("td,kd->tk", grad_middle_low, w_out, preferred_element_type=jnp.float32)
        .astype(jnp.bfloat16)
        .reshape(row_count, heads_kv, GROUP, HD)
    )
    row_delta = jnp.transpose(jnp.sum(grad_mixed.astype(jnp.float32) * out_low, axis=-1), (1, 2, 0))
    grad_query_rot, grad_keys, grad_values = attention_backward(
        query_low,
        key_all,
        value_all,
        segment_row,
        query_seg,
        positions,
        row_top,
        row_total,
        grad_mixed,
        row_delta,
    )
    grad_key_mine, grad_value_mine = (
        lax.psum_scatter(
            grad_keys.astype(jnp.bfloat16), "ctx", scatter_dimension=0, tiled=True
        ).astype(jnp.float32),
        lax.psum_scatter(
            grad_values.astype(jnp.bfloat16), "ctx", scatter_dimension=0, tiled=True
        ).astype(jnp.float32),
    )
    grad_query_low = (
        rotate(grad_query_rot, cos_four, -sin_four).astype(jnp.bfloat16).reshape(row_count, -1)
    )
    grad_key_low = (
        rotate(grad_key_mine, cos_three, -sin_three).astype(jnp.bfloat16).reshape(row_count, -1)
    )
    grad_value_low = grad_value_mine.astype(jnp.bfloat16).reshape(row_count, -1)
    grad_query = jnp.einsum("td,tk->dk", normed, grad_query_low, preferred_element_type=jnp.float32)
    grad_key = jnp.einsum("td,tk->dk", normed, grad_key_low, preferred_element_type=jnp.float32)
    grad_value = jnp.einsum("td,tk->dk", normed, grad_value_low, preferred_element_type=jnp.float32)
    grad_normed = head_sum(
        jnp.einsum("tk,dk->td", grad_query_low, w_query, preferred_element_type=jnp.float32)
        + jnp.einsum("tk,dk->td", grad_key_low, w_key, preferred_element_type=jnp.float32)
        + jnp.einsum("tk,dk->td", grad_value_low, w_value, preferred_element_type=jnp.float32)
    )
    scaled_first = grad_normed * gain_first
    grad_gain_attn = jnp.sum(grad_normed * normal_first, axis=0)
    grad_tokens = grad_middle + scale_first * (
        scaled_first - normal_first * jnp.mean(scaled_first * normal_first, axis=-1, keepdims=True)
    )
    gradients = (
        grad_gain_attn,
        grad_query,
        grad_key,
        grad_value,
        grad_gain_mlp,
        grad_gate,
        grad_up,
        grad_out,
        grad_down,
    )
    return (output_rows, grad_tokens, gradients)


def body(
    tokens,
    segments,
    cotangent,
    gain_attn,
    w_query,
    w_key,
    w_value,
    w_out,
    gain_mlp,
    w_gate,
    w_up,
    w_down,
):
    micro_count = tokens.shape[0]
    row_count = tokens.shape[1]
    positions = lax.axis_index("ctx") * row_count + jnp.arange(row_count, dtype=jnp.int32)
    cosine_table, sine_table = rope_tables(positions)
    shards = (gain_attn, w_query, w_key, w_value, gain_mlp, w_gate, w_up, w_out, w_down)
    outputs = []
    token_grads = []
    gathered = weight_gather(shards)
    totals = None
    for micro_index in range(micro_count):
        output_rows, grad_rows, grads_now = micro_step(
            gathered,
            tokens[micro_index],
            segments[micro_index],
            cotangent[micro_index],
            positions,
            cosine_table,
            sine_table,
        )
        outputs.append(output_rows)
        token_grads.append(grad_rows)
        totals = (
            grads_now
            if totals is None
            else tuple(earlier + addend for earlier, addend in zip(totals, grads_now))
        )
    reduced = tuple(
        tensor_piece.astype(jnp.float32)
        for tensor_piece in grad_reduce(tuple(total.astype(jnp.bfloat16) for total in totals))
    )
    return (
        jnp.stack(outputs),
        jnp.stack(token_grads),
        reduced[0],
        reduced[1],
        reduced[2],
        reduced[3],
        reduced[7],
        reduced[4],
        reduced[5],
        reduced[6],
        reduced[8],
    )


MESH = pl.DeviceIdType.MESH
UNIT = 384
ROWS = 512
SPAN = 256
WIDE = 1536
F32 = jnp.float32
BF16 = jnp.bfloat16
NT = (((1,), (1,)), ((), ()))
TN = (((0,), (0,)), ((), ()))


def dot_nn(a, b):
    return jnp.dot(a, b, preferred_element_type=F32)


def dot_nt(a, b):
    return lax.dot_general(a, b, NT, preferred_element_type=F32)


def dot_tn(a, b):
    return lax.dot_general(a, b, TN, preferred_element_type=F32)


class Place:
    def __init__(self):
        f, c, t = (lax.axis_index(axis) for axis in ("fsdp", "ctx", "tp"))
        self.f, self.c, self.t = f, c, t
        self.y, self.k = lax.div(c, 2), lax.rem(c, 2)
        self.oy, self.ok = 1 - self.y, 1 - self.k
        self.half = lax.div(f, 2)
        self.inner = (f == 1) | (f == 2)
        self.edge = (f == 0) | (f == 3)
        self.near_f = f + 1 - 2 * lax.rem(f, 2)
        self.mid_f = 2 - self.half
        self.far_f = 3 - 3 * self.half
        self.near = (self.near_f, c, t)
        self.mid = (self.mid_f, c, t)
        self.far = (self.far_f, c, t)
        self.ypeer = (f, c + 2 - 4 * self.y, t)
        self.sib = (f, c + 1 - 2 * self.k, t)
        self.xpeer = (f, c, 1 - t)

    def barrier(self):
        sem = pltpu.get_barrier_semaphore()
        others = [(lax.rem(self.f + step, 4), self.c, self.t) for step in (1, 2, 3)]
        others += [self.ypeer, self.sib, self.xpeer]
        for other in others:
            pl.semaphore_signal(sem, inc=1, device_id=other, device_id_type=MESH)
        pl.semaphore_wait(sem, len(others))


def remote(src, dst, send, recv, device):
    return pltpu.make_async_remote_copy(
        src_ref=src,
        dst_ref=dst,
        send_sem=send,
        recv_sem=recv,
        device_id=device,
        device_id_type=MESH,
    )


def lanes(rows, columns):
    return lax.broadcasted_iota(jnp.int32, (rows, columns), 1)


def unpack_heads(x):
    lane = lanes(x.shape[0], 128)
    one, two, three = x[:, :128], x[:, 128:256], x[:, 256:]
    heads = (
        one,
        pltpu.roll(jnp.where(lane < 64, two, one), 32, 1),
        pltpu.roll(jnp.where(lane < 32, three, two), 64, 1),
        pltpu.roll(three, 96, 1),
    )
    return [jnp.where(lane < HD, head, 0.0) for head in heads]


def pack_heads(heads):
    lane = lanes(heads[0].shape[0], 128)
    second = pltpu.roll(heads[1], 96, 1)
    third = pltpu.roll(heads[2], 64, 1)
    fourth = pltpu.roll(heads[3], 32, 1)
    return jnp.concatenate(
        [
            jnp.where(lane < 96, heads[0], second),
            jnp.where(lane < 64, second, third),
            jnp.where(lane < 32, third, fourth),
        ],
        axis=1,
    )


def turn(x, cosine, sine):
    lane = lax.rem(lanes(x.shape[0], UNIT), HD)
    swapped = jnp.where(lane < HD // 2, pltpu.roll(x, UNIT - HD // 2, 1), pltpu.roll(x, HD // 2, 1))
    return x * cosine + swapped * sine


def transpose_into(dst, src):
    @pl.loop(0, WIDE // 128)
    def _(i):
        at = pl.multiple_of(i * 128, 128)
        dst[pl.ds(at, 128), :] = src[:, pl.ds(at, 128)].astype(F32).T.astype(BF16)


def weight(buf, slot, lo, hi):
    return buf[slot, :, :, :, :, lo:hi].reshape(WIDE, hi - lo)


def allowed_keys(low_row, high_row):
    row = lax.broadcasted_iota(jnp.int32, (4 * SPAN, SPAN), 0)
    return (row >= low_row) & (row <= high_row)


RING = 5
SPLIT_ALL = True
WIDE_A = 256
WIDE_B = 128


class GatherA:
    def __init__(self, me, buf, source, sems):
        self.me, self.buf, self.source = me, buf, source
        self.z_send, self.z_recv, self.y_send, self.y_recv, self.c_send, self.c_recv = sems

    def z_copy(self, j, i):
        me = self.me
        dst = self.buf.at[j, me.f, me.y, me.k]
        return remote(self.source.at[j], dst, self.z_send.at[j, i], self.z_recv.at[j], (me.near, me.mid)[i])

    def hand_copy(self, j):
        me = self.me
        part = self.buf.at[j, pl.ds(2 - 2 * me.half, 2), me.y, me.k]
        return remote(part, part, self.z_send.at[j, 2], self.z_recv.at[j], me.near)

    def y_copy(self, j):
        me = self.me
        part = self.buf.at[j, :, me.y, me.k]
        return remote(part, part, self.y_send.at[j], self.y_recv.at[j], me.ypeer)

    def core_copy(self, j):
        me = self.me
        part = self.buf.at[j, :, :, me.k]
        return remote(part, part, self.c_send.at[j], self.c_recv.at[j], me.sib)

    def z_wait(self, j):
        me = self.me
        three = self.buf.at[j, pl.ds(0, 3), me.y, me.k]
        remote(three, three, self.z_send.at[j, 0], self.z_recv.at[j], me.near).wait_recv()

    def start(self, j):
        for i in range(2):
            self.z_copy(j, i).start()

    def spread(self, j):
        pass

    def hand(self, j):
        @pl.when(self.me.inner)
        def _():
            self.z_wait(j)
            self.hand_copy(j).start()

    def turn(self, j):
        @pl.when(self.me.edge)
        def _():
            self.z_wait(j)

        self.y_copy(j).start()

    def core(self, j):
        self.y_copy(j).wait_recv()
        self.core_copy(j).start()

    def done(self, j):
        self.core_copy(j).wait_recv()

    def sent(self, j):
        for i in range(2):
            self.z_copy(j, i).wait_send()

        @pl.when(self.me.inner)
        def _():
            self.hand_copy(j).wait_send()

        self.y_copy(j).wait_send()
        self.core_copy(j).wait_send()


class GatherB(GatherA):
    def z_copy(self, j, i):
        me = self.me
        part = self.buf.at[j, me.f, :, me.k]
        return remote(part, part, self.z_send.at[j, i], self.z_recv.at[j], (me.near, me.mid)[i])

    def hand_copy(self, j):
        me = self.me
        part = self.buf.at[j, pl.ds(2 - 2 * me.half, 2), :, me.k]
        return remote(part, part, self.z_send.at[j, 2], self.z_recv.at[j], me.near)

    def y_copy(self, j):
        me = self.me
        dst = self.buf.at[j, me.f, me.y, me.k]
        return remote(self.source.at[j], dst, self.y_send.at[j], self.y_recv.at[j], me.ypeer)

    def z_wait(self, j):
        me = self.me
        three = self.buf.at[j, pl.ds(0, 3), :, me.k]
        remote(three, three, self.z_send.at[j, 0], self.z_recv.at[j], me.near).wait_recv()

    def start(self, j):
        self.y_copy(j).start()

    def spread(self, j):
        self.y_copy(j).wait_recv()
        for i in range(2):
            self.z_copy(j, i).start()

    def turn(self, j):
        pass

    def core(self, j):
        @pl.when(self.me.edge)
        def _():
            self.z_wait(j)

        self.core_copy(j).start()


class ReduceA:
    def __init__(self, me, r, other, mine, bufs, sems):
        self.me, self.r, self.other, self.mine = me, r, other, mine
        self.r1, self.r2, self.r3 = bufs
        (
            self.c_send,
            self.c_recv,
            self.y_send,
            self.y_recv,
            self.za_send,
            self.za_recv,
            self.zb_send,
            self.zb_recv,
        ) = sems
        self.zed = self.r2

    def core_copy(self):
        return remote(self.other, self.r1, self.c_send.at[self.r], self.c_recv.at[self.r], self.me.sib)

    def y_copy(self):
        src = self.r1.at[:, self.me.oy]
        return remote(src, self.r2, self.y_send.at[self.r], self.y_recv.at[self.r], self.me.ypeer)

    def za_copy(self):
        src = self.zed.at[pl.ds(1 - self.me.half, 3)]
        dst = self.r3.at[pl.ds(0, 3)]
        return remote(src, dst, self.za_send.at[self.r], self.za_recv.at[self.r], self.me.near)

    def zb_copy(self, i):
        me = self.me
        owner, at, device = ((me.near_f, 0, me.near), (me.mid_f, 3, me.mid), (me.far_f, 1, me.far))[i]
        recv = self.zb_recv.at[self.r, min(i, 1)]
        return remote(self.zed.at[owner], self.r3.at[at], self.zb_send.at[self.r, i], recv, device)

    def core(self):
        self.core_copy().start()

    def add_core(self):
        self.core_copy().wait_recv()
        self.r1[...] = self.r1[...] + self.mine[...]
        self.core_copy().wait_send()

    def z_first(self):
        @pl.when(self.me.edge)
        def _():
            self.za_copy().start()

    def z_second(self, before=None):
        me = self.me

        @pl.when(me.inner)
        def _():
            self.za_copy().wait_recv()
            for owner in (me.mid_f, me.far_f):
                self.zed[owner] = self.zed[owner] + self.r3[owner - (1 - me.half)]
            if before is not None:
                before()
            for i in range(3):
                self.zb_copy(i).start()

    def z_total(self):
        me = self.me
        self.zb_copy(1).wait_recv()

        @pl.when(me.edge)
        def _():
            self.zb_copy(0).wait_recv()

        one = jnp.where(me.edge, 0, me.f - (1 - me.half))
        two = jnp.where(me.edge, 1, 3)
        return self.zed[me.f].astype(F32) + self.r3[one].astype(F32) + self.r3[two].astype(F32)

    def z_sent(self):
        @pl.when(self.me.edge)
        def _():
            self.za_copy().wait_send()

        @pl.when(self.me.inner)
        def _():
            for i in range(3):
                self.zb_copy(i).wait_send()

    def y_start(self):
        self.y_copy().start()

    def y_add(self):
        self.y_copy().wait_recv()
        self.r2[...] = self.r2[...] + self.r1[:, self.me.y]
        self.y_copy().wait_send()


class ReduceB(ReduceA):
    def __init__(self, *args):
        super().__init__(*args)
        self.zed = self.r1

    def y_copy(self):
        src = self.r1.at[self.me.f, self.me.oy]
        return remote(src, self.r2, self.y_send.at[self.r], self.y_recv.at[self.r], self.me.ypeer)

    def z_end(self):
        self.r1[self.me.f] = self.z_total().astype(BF16)
        self.z_sent()
        self.y_copy().start()

    def total(self):
        self.y_copy().wait_recv()
        out = self.r1[self.me.f, self.me.y].astype(F32) + self.r2[...].astype(F32)
        self.y_copy().wait_send()
        return out


def layer_kernel(
    packed_a,
    packed_b,
    gains,
    tokens,
    cot,
    cosine,
    sine,
    low,
    high,
    output,
    grad_tokens,
    grads,
    gain_grads,
    wa,
    wb,
    fed,
    gw,
    gain_rows,
    a_buf,
    at,
    bt,
    et,
    eb,
    kvx,
    qh,
    kh,
    vh,
    lse,
    ob,
    x2,
    acc,
    out_acc,
    wbuf,
    part,
    stage,
    back,
    ra1,
    ra2,
    ra3,
    rb1,
    rb2,
    rb3,
    gout,
    xs,
    xr,
    doh,
    heads,
    dkh,
    dvh,
    rc,
    ry,
    dqb,
    gacc,
    g1,
    g2,
    g3,
    gs,
    ga_sems,
    gb_sems,
    gg_sems,
    ra_sems,
    rb_sems,
    rg_sems,
    c_cred,
    y_cred,
    z_cred,
    x_cred,
    x_send,
    x_recv,
    kv_send,
    kv_recv,
    g_sems,
    load_sem,
    w_sem,
    stage_sem,
    back_sem,
    out_sem,
):
    me = Place()
    f, y, k = me.f, me.y, me.k
    units, depth = packed_a.shape[0], packed_a.shape[1]
    groups = fed.shape[0]
    scale = 1.0 / math.sqrt(HD)

    def local(src, dst, i):
        return pltpu.make_async_copy(src, dst, load_sem.at[i])

    own = (
        local(packed_a, wa.at[:, f, y, k], 0),
        local(packed_b, wb.at[:, f, y, k], 1),
        local(gains.at[0], gw.at[0, f, y, k], 2),
    )
    for copy in own:
        copy.start()
    local(cot, eb, 3).start()
    me.barrier()

    gather_a = GatherA(me, wa, packed_a, ga_sems)
    gather_b = (GatherA(me, wb, packed_b, gb_sems), GatherB(me, wb, packed_b, gb_sems))
    gather_g = GatherA(me, gw, gains, gg_sems)

    def within(i, count, act):
        if isinstance(i, int):
            if 0 <= i < count:
                act(i)
        else:
            pl.when((i >= 0) & (i < count))(lambda: act(i))

    def is_even(i):
        return jnp.array(False) if SPLIT_ALL else lax.rem(i, 2) == 0

    def by_parity(i, count, act):
        def both(j):
            if SPLIT_ALL:
                act(j, 1)
            elif isinstance(j, int):
                act(j, j % 2)
            else:
                pl.when(lax.rem(j, 2) == 0)(lambda: act(j, 0))
                pl.when(lax.rem(j, 2) == 1)(lambda: act(j, 1))

        within(i, count, both)

    def ag(t):
        def run(lag, gather, name):
            within(t + lag, units, getattr(gather, name))

        def split(lag, name):
            by_parity(t + lag, units, lambda j, kind: getattr(gather_b[kind], name)(j))

        def even(j, kind):
            if kind == 0:
                gather_b[0].start(j)

        def odd(j, kind):
            if kind == 1:
                gather_b[1].start(j)

        by_parity(t + 6, units, odd)
        run(4, gather_a, "start")
        by_parity(t + 4, units, even)
        split(4, "spread")
        run(2, gather_a, "hand")
        split(2, "hand")
        run(0, gather_a, "turn")
        split(0, "turn")
        run(-1, gather_a, "core")
        split(-1, "core")
        run(-2, gather_a, "done")
        run(-2, gather_b[0], "done")

    def load(u, slot, side):
        at_b = side * UNIT + WIDE_A
        return (
            pltpu.make_async_copy(
                wa.at[u], wbuf.at[slot, :, :, :, :, pl.ds(side * UNIT, WIDE_A)], w_sem.at[slot, side, 0]
            ),
            pltpu.make_async_copy(
                wb.at[u], wbuf.at[slot, :, :, :, :, pl.ds(at_b, WIDE_B)], w_sem.at[slot, side, 1]
            ),
        )

    def load_start(u, slot, side):
        for copy in load(u, slot, side):
            copy.start()

    def load_wait(u, slot, side):
        for copy in load(u, slot, side):
            copy.wait()

    def ring(r):
        s = lax.rem(r, RING)
        slot = lax.rem(lax.div(r, 2), 2)
        start = lax.rem(r, 2) * UNIT
        cols_a = pl.ds(pl.multiple_of(start, 128), WIDE_A)
        cols_b = pl.ds(pl.multiple_of(start + WIDE_A, 128), WIDE_B)
        one = ReduceA(
            me,
            r,
            part.at[slot, :, :, me.ok, :, cols_a],
            part.at[slot, :, :, k, :, cols_a],
            (ra1.at[s], ra2.at[s], ra3.at[s]),
            ra_sems,
        )
        other, mine = part.at[slot, :, :, me.ok, :, cols_b], part.at[slot, :, :, k, :, cols_b]
        two = (
            ReduceA(me, r, other, mine, (rb1.at[s], rb2.at[s], rb3.at[s, :, 0]), rb_sems),
            ReduceB(me, r, other, mine, (rb1.at[s], rb2.at[s, 0], rb3.at[s]), rb_sems),
        )
        return one, two

    def credit(r, sem):
        within(r - RING, units, lambda i: pl.semaphore_wait(sem, 1))

    def give(r, sem, device):
        def act(i):
            pl.semaphore_signal(sem, inc=1, device_id=device, device_id_type=MESH)

        within(r + RING, units, act)

    def out_copy(i):
        slot = lax.rem(i, 2)
        return pltpu.make_async_copy(gout.at[slot], grads.at[i], out_sem.at[slot])

    def rs(r):
        def credit_near(i):
            @pl.when(me.edge)
            def _():
                credit(i, z_cred.at[0])

        def credit_inner(i):
            for j in range(3):
                credit(i, z_cred.at[j])

        def first_a(i):
            credit(i, c_cred)
            ring(i)[0].core()

        def second_a(i):
            one = ring(i)[0]
            one.add_core()
            credit(i, y_cred)
            one.y_start()

        def third_a(i):
            one = ring(i)[0]
            one.y_add()

            @pl.when(is_even(i))
            def _():
                credit_near(i)

            one.z_first()

        def fourth_a(i):
            ring(i)[0].z_second(lambda: pl.when(is_even(i))(lambda: credit_inner(i)))

        def fifth_a(i):
            one = ring(i)[0]
            within(i - 2, units, lambda j: out_copy(j).wait())
            gout[lax.rem(i, 2), :, 0:WIDE_A] = one.z_total()
            one.z_sent()

        def first_b(i):
            ring(i)[1][0].core()

        def second_b(i, kind):
            two = ring(i)[1][kind]
            two.add_core()
            if kind == 0:
                two.y_start()
            else:
                credit_near(i)
                two.z_first()

        def third_b(i, kind):
            two = ring(i)[1][kind]
            if kind == 0:
                two.y_add()
                two.z_first()
            else:
                two.z_second(lambda: credit_inner(i))

        def fourth_b(i, kind):
            two = ring(i)[1][kind]
            if kind == 0:
                two.z_second()
            else:
                two.z_end()

        def fifth_b(i, kind):
            two = ring(i)[1][kind]
            if kind == 0:
                gout[lax.rem(i, 2), :, WIDE_A:] = two.z_total()
                two.z_sent()
            else:
                gout[lax.rem(i, 2), :, WIDE_A:] = two.total()

        def last(i):
            out_copy(i).start()
            give(i, c_cred, me.sib)
            give(i, y_cred, me.ypeer)

            @pl.when(me.edge)
            def _():
                give(i, z_cred.at[0], me.near)
                give(i, z_cred.at[2], me.mid)

            @pl.when(me.inner)
            def _():
                give(i, z_cred.at[0], me.near)
                give(i, z_cred.at[1], me.mid)

        within(r, units, first_a)
        within(r - 1, units, second_a)
        within(r - 2, units, third_a)
        within(r - 3, units, fourth_a)
        within(r - 4, units, fifth_a)
        within(r, units, first_b)
        by_parity(r - 1, units, second_b)
        by_parity(r - 2, units, third_b)
        by_parity(r - 3, units, fourth_b)
        by_parity(r - 4, units, fifth_b)
        within(r - 4, units, last)

    def put(pair, i, value):
        columns = slice(i * 256, (i + 1) * 256)
        part[lax.rem(pair, 2), :, :, :, :, columns] = value.astype(BF16).reshape(4, 2, 2, depth, 256)

    def x_copy(e, r, src):
        rows = pl.ds(pl.multiple_of(r * 128, 128), 128)
        return remote(src.at[rows], xr.at[rows], x_send.at[e, r], x_recv.at[e, r], me.xpeer)

    def give_x():
        pl.semaphore_signal(x_cred, inc=1, device_id=me.xpeer, device_id_type=MESH)

    def take_x():
        pl.semaphore_wait(x_cred, 1)

    for copy in own:
        copy.wait()
    gather_g.start(0)
    ag(-6)
    ag(-5)
    gather_g.hand(0)
    gather_g.turn(0)
    ag(-4)
    local(cot, eb, 3).wait()
    transpose_into(et, eb)
    gather_g.core(0)
    ag(-3)
    gather_g.done(0)
    gain_rows[...] = gw[0].reshape(WIDE, 128).astype(F32).T[:8, :]
    ag(-2)
    ag(-1)

    @pl.loop(0, ROWS // 64)
    def _(i):
        rows = pl.ds(pl.multiple_of(i * 64, 64), 64)
        x = tokens[rows, :].astype(F32)
        r = lax.rsqrt(jnp.mean(x * x, axis=-1, keepdims=True) + epsilon)
        a_buf[rows, :] = (x * r * gain_rows[0:1, :]).astype(BF16)

    ag(0)
    transpose_into(at, a_buf)
    ag(1)
    ag(2)
    load_start(0, 0, 0)
    ag(3)
    load_start(1, 0, 1)
    load_wait(0, 0, 0)
    load_wait(1, 0, 1)

    def kv_copy(i, s):
        core = (y, k) if i == 0 else (slice(None), k)
        half = kvx.at[core[0], core[1], pl.ds(s * SPAN, SPAN)]
        return remote(half, half, kv_send.at[i, s], kv_recv.at[i, s], me.sib if i else me.ypeer)

    for s in range(2):
        rows = pl.ds(s * SPAN, SPAN)
        pair = dot_nn(a_buf[rows, :], weight(wbuf, 0, 0, 2 * UNIT))
        kvx[y, k, rows, :UNIT] = turn(pair[:, :UNIT], cosine[...], sine[...]).astype(BF16)
        kvx[y, k, rows, UNIT:] = pair[:, UNIT:].astype(BF16)
        kv_copy(0, s).start()
    ag(4)
    load_start(2, 1, 0)
    ag(5)
    load_start(3, 1, 1)
    load_wait(2, 1, 0)
    load_wait(3, 1, 1)
    for side in range(2):
        for s in range(2):
            rows = pl.ds(s * SPAN, SPAN)
            query = dot_nn(a_buf[rows, :], weight(wbuf, 1, side * UNIT, (side + 1) * UNIT))
            query = turn(query, cosine[...], sine[...])
            for i, head in enumerate(unpack_heads(query)):
                qh[s * 8 + side * 4 + i] = head.astype(BF16)
    kv_copy(0, 0).wait_recv()
    kv_copy(1, 0).start()
    ag(6)
    load_start(4, 0, 0)
    kv_copy(0, 1).wait_recv()
    kv_copy(1, 1).start()
    ag(7)
    load_start(5, 0, 1)

    def spread_heads(i):
        s, c = lax.div(i, 4), lax.rem(i, 4)
        block = kvx[lax.div(c, 2), lax.rem(c, 2), pl.ds(pl.multiple_of(s * SPAN, SPAN), SPAN), :]
        rows = pl.ds(pl.multiple_of(c * SPAN, SPAN), SPAN)
        for g, head in enumerate(unpack_heads(block[:, :UNIT].astype(F32))):
            kh[s * 4 + g, rows, :] = head.astype(BF16)
        for g, head in enumerate(unpack_heads(block[:, UNIT:].astype(F32))):
            vh[s * 4 + g, rows, :] = head.astype(BF16)

    def attend(i):
        s, h = lax.div(i, 8), lax.rem(i, 8)
        g = s * 4 + lax.div(h, 2)
        scores = dot_nt(kh[g], qh[i]) * scale
        scores = jnp.where(allowed_keys(low[s], high[...]), scores, negative)
        top = jnp.max(scores, axis=0, keepdims=True)
        p = jnp.exp(scores - top)
        total = jnp.sum(p, axis=0, keepdims=True)
        lse[i] = jnp.broadcast_to(top + jnp.log(total), (8, SPAN))
        heads[h] = (dot_tn(vh[g], p.astype(BF16)) / total).T

    for s in range(2):
        kv_copy(1, s).wait_recv()
        pl.loop(4 * s, 4 * s + 4)(spread_heads)
        pl.loop(8 * s, 8 * s + 4)(attend)
        ag(8 + 2 * s)
        pl.loop(8 * s + 4, 8 * s + 8)(attend)
        rows = slice(s * SPAN, (s + 1) * SPAN)
        for side in range(2):
            mixed = pack_heads([heads[side * 4 + i] for i in range(4)])
            ob[rows, side * UNIT : (side + 1) * UNIT] = mixed.astype(BF16)
        if s == 0:
            load_wait(4, 0, 0)
            load_wait(5, 0, 1)
        xs[rows, :] = dot_nt(ob[rows, :], weight(wbuf, 0, 0, 2 * UNIT)).astype(BF16)
        x_copy(0, 2 * s, xs).start()
        x_copy(0, 2 * s + 1, xs).start()
        ag(9 + 2 * s)

    def norm_second(r):
        x_copy(0, r, xs).wait()
        rows = pl.ds(pl.multiple_of(r * 128, 128), 128)
        x = tokens[rows, :].astype(F32) + (xs[rows, :].astype(F32) + xr[rows, :].astype(F32))
        x2[rows, :] = x
        r2 = lax.rsqrt(jnp.mean(x * x, axis=-1, keepdims=True) + epsilon)
        a_buf[rows, :] = (x * r2 * gain_rows[1:2, :]).astype(BF16)

    acc[...] = jnp.zeros_like(acc)
    out_acc[...] = jnp.zeros_like(out_acc)
    pl.loop(0, 2)(norm_second)
    ag(12)
    ag(13)
    ag(14)
    pl.loop(2, 4)(norm_second)
    give_x()
    ag(15)
    transpose_into(bt, a_buf)
    ag(16)

    def stage_copy(n):
        slot = lax.rem(n, 2)
        return pltpu.make_async_copy(stage.at[slot], fed.at[n], stage_sem.at[slot])

    def back_copy(n):
        slot = lax.rem(n, 2)
        return pltpu.make_async_copy(fed.at[n], back.at[slot], back_sem.at[slot])

    def feed_grads(n, pair, ready):
        slot = lax.rem(n, 2)
        back_copy(n).wait()
        put(pair, 0, dot_nn(bt[...], back[slot, 0]))
        put(pair, 1, dot_nn(bt[...], back[slot, 1]))
        put(pair, 2, dot_nn(et[...], back[slot, 2]))
        if ready:
            within(n + 1, groups, lambda i: back_copy(i).start())

    @pl.loop(0, groups)
    def _(n):
        slot = lax.rem(n, 2)
        for side in range(2):
            load_start(6 + 2 * n + side, slot, side)

        @pl.when(n >= 1)
        def _():
            stage_copy(n - 1).wait()

        @pl.when(n == 1)
        def _():
            back_copy(0).start()

        @pl.when((lax.rem(n, 2) == 0) & (n >= 2))
        def _():
            back_copy(lax.div(n, 2)).start()

        @pl.when(n < groups - 1)
        def _():
            ag(17 + n)

        @pl.when(lax.rem(n, 2) == 1)
        def _():
            feed_grads(lax.div(n, 2), lax.div(n, 2), False)

        @pl.when(n >= 1)
        def _():
            rs(n - 1)

        for side in range(2):
            load_wait(6 + 2 * n + side, slot, side)
        gate = dot_nn(a_buf[...], weight(wbuf, slot, 0, 256))
        up = dot_nn(a_buf[...], weight(wbuf, slot, 256, 512))
        sg = jax.nn.sigmoid(gate)
        silu = gate * sg
        stage[slot, 2] = (silu * up).astype(BF16)
        dh = dot_nn(eb[...], weight(wbuf, slot, 512, 768))
        stage[slot, 0] = (dh * up * sg * (1.0 + gate * (1.0 - sg))).astype(BF16)
        stage[slot, 1] = (dh * silu).astype(BF16)
        stage_copy(n).start()

        @pl.loop(0, 4)
        def _(i):
            columns = pl.ds(pl.multiple_of(i * 4 * depth, 128), 4 * depth)

            def rows_of(lo):
                return wbuf[slot, i, :, :, :, lo : lo + 256].reshape(4 * depth, 256)

            out_acc[:, columns] += dot_nt(stage[slot, 2], rows_of(512))
            acc[:, columns] += dot_nt(stage[slot, 0], rows_of(0)) + dot_nt(stage[slot, 1], rows_of(256))

    load_start(4, 0, 0)
    load_start(5, 0, 1)
    take_x()
    for r in range(4):
        rows = slice(r * 128, (r + 1) * 128)
        xs[rows, :] = acc[rows, :].astype(BF16)
        x_copy(1, r, xs).start()
    stage_copy(groups - 1).wait()
    back_copy(4).start()
    rs(7)

    gacc[...] = jnp.zeros_like(gacc)

    def norm_back(r):
        x_copy(1, r, xs).wait()
        rows = pl.ds(pl.multiple_of(r * 128, 128), 128)
        mine = xs[rows, :].astype(F32)
        db = mine + xr[rows, :].astype(F32)
        x = x2[rows, :]
        r2 = lax.rsqrt(jnp.mean(x * x, axis=-1, keepdims=True) + epsilon)
        n2 = x * r2
        gacc[1:2, :] += jnp.sum(mine * n2, axis=0, keepdims=True)
        scaled = db * gain_rows[1:2, :]
        dx2 = eb[rows, :].astype(F32) + r2 * (scaled - n2 * jnp.mean(scaled * n2, axis=-1, keepdims=True))
        acc[rows, :] = dx2
        eb[rows, :] = dx2.astype(BF16)

    def attend_back(i):
        s, g = lax.div(i, 4), lax.rem(i, 4)
        mask = allowed_keys(low[s], high[...])
        dk = jnp.zeros((4 * SPAN, 128), F32)
        dv = jnp.zeros((4 * SPAN, 128), F32)
        for hh in range(2):
            h = s * 8 + 2 * g + hh
            scores = jnp.where(mask, dot_nt(kh[i], qh[h]) * scale, negative)
            p = jnp.exp(scores - lse[h][0:1, :])
            dp = dot_nt(vh[i], doh[h])
            delta = jnp.sum(p * dp, axis=0, keepdims=True)
            ds = (p * (dp - delta) * scale).astype(BF16)
            dv += dot_nn(p.astype(BF16), doh[h])
            dk += dot_nn(ds, qh[h])
            heads[2 * g + hh] = dot_tn(kh[i], ds).T
        dkh[g] = dk.astype(BF16)
        dvh[g] = dv.astype(BF16)

    def dkv_mine(s, core):
        return kvx.at[:, core, pl.ds(pl.multiple_of(s * SPAN, SPAN), SPAN)]

    def kv_core(s):
        return remote(dkv_mine(s, me.ok), rc.at[s], kv_send.at[2, s], kv_recv.at[2, s], me.sib)

    def kv_y(s):
        return remote(rc.at[s, me.oy], ry.at[s], kv_send.at[3, s], kv_recv.at[3, s], me.ypeer)

    def kv_add(s):
        kv_core(s).wait_recv()
        rc[s] = rc[s] + dkv_mine(s, k)[...]
        kv_y(s).start()

    for s in range(2):
        kv_copy(0, s).wait_send()
        kv_copy(1, s).wait_send()
    load_wait(4, 0, 0)
    load_wait(5, 0, 1)

    @pl.loop(0, 2)
    def _(s):
        rows = pl.ds(pl.multiple_of(s * SPAN, SPAN), SPAN)
        norm_back(2 * s)
        norm_back(2 * s + 1)

        @pl.when(s == 1)
        def _():
            give_x()
            xs[...] = out_acc[...].astype(BF16)
            take_x()
            for r in range(4):
                x_copy(2, r, xs).start()

        feed_grads(4 + 2 * s, 4 + 2 * s, True)
        rs(8 + 4 * s)
        for side in range(2):
            mixed = dot_nn(eb[rows, :], weight(wbuf, 0, side * UNIT, (side + 1) * UNIT)).astype(BF16)
            for i, head in enumerate(unpack_heads(mixed.astype(F32))):
                doh[s * 8 + side * 4 + i] = head.astype(BF16)
        attend_back(4 * s)
        attend_back(4 * s + 1)
        rs(9 + 4 * s)
        attend_back(4 * s + 2)
        attend_back(4 * s + 3)
        feed_grads(5 + 2 * s, 5 + 2 * s, True)
        rs(10 + 4 * s)
        for c in range(4):
            at_c = slice(c * SPAN, (c + 1) * SPAN)
            for j, src in enumerate((dkh, dvh)):
                kvx[c // 2, c % 2, rows, j * UNIT : (j + 1) * UNIT] = pack_heads(
                    [src[g, at_c, :].astype(F32) for g in range(4)]
                ).astype(BF16)
        kv_core(s).start()
        for side in range(2):
            dq = turn(pack_heads([heads[side * 4 + j] for j in range(4)]), cosine[...], -sine[...])
            dqb[rows, side * UNIT : (side + 1) * UNIT] = dq.astype(BF16)
        rs(11 + 4 * s)
        kv_add(s)

    for side in range(2):
        load_start(2 + side, 0, side)
        load_start(side, 1, side)
    transpose_into(bt, eb)
    for i in range(3):
        put(8, i, dot_nn(bt[...], ob[:, i * 256 : (i + 1) * 256]))
    rs(16)
    for i in range(3):
        put(9, i, dot_nn(at[...], dqb[:, i * 256 : (i + 1) * 256]))
    rs(17)
    for side in range(2):
        load_wait(2 + side, 0, side)
        load_wait(side, 1, side)

    def norm_grad(s):
        rows = slice(s * SPAN, (s + 1) * SPAN)
        kv_y(s).wait_recv()
        total = rc[s, y].astype(F32) + ry[s].astype(F32)
        ob[rows, :UNIT] = turn(total[:, :UNIT], cosine[...], -sine[...]).astype(BF16)
        ob[rows, UNIT:] = total[:, UNIT:].astype(BF16)
        da = dot_nt(dqb[rows, :], weight(wbuf, 0, 0, 768)) + dot_nt(ob[rows, :], weight(wbuf, 1, 0, 768))
        a_buf[rows, :] = da.astype(BF16)

    norm_grad(0)
    rs(18)

    for r in range(4):
        rows = slice(r * 128, (r + 1) * 128)
        x_copy(2, r, xs).wait()
        xs[rows, :] = (x2[rows, :] + (xs[rows, :].astype(F32) + xr[rows, :].astype(F32))).astype(BF16)
    give_x()
    local(xs, output, 0).start()
    take_x()
    x_copy(3, 0, a_buf).start()
    x_copy(3, 1, a_buf).start()
    norm_grad(1)
    x_copy(3, 2, a_buf).start()
    x_copy(3, 3, a_buf).start()
    rs(19)
    for i in range(3):
        put(10, i, dot_nn(at[...], ob[:, i * 256 : (i + 1) * 256]))
    rs(20)

    def first_norm(rows):
        x = tokens[rows, :].astype(F32)
        r1 = lax.rsqrt(jnp.mean(x * x, axis=-1, keepdims=True) + epsilon)
        return r1, x * r1

    rs(21)

    @pl.loop(0, 4)
    def _(r):
        rows = pl.ds(pl.multiple_of(r * 128, 128), 128)
        gacc[0:1, :] += jnp.sum(a_buf[rows, :].astype(F32) * first_norm(rows)[1], axis=0, keepdims=True)

    gain_columns = jnp.concatenate([gacc[...], jnp.zeros((120, WIDE), F32)], axis=0).T
    gather_g.sent(0)
    gw[0] = gain_columns.astype(BF16).reshape(4, 2, 2, depth, 128)
    gain = ReduceA(me, 0, gw.at[0, :, :, me.ok], gw.at[0, :, :, k], (g1, g2, g3), rg_sems)
    gain.core()
    rs(22)
    gain.add_core()
    gain.y_start()
    rs(23)
    gain.y_add()
    gain.z_first()

    @pl.loop(0, 4)
    def _(r):
        x_copy(3, r, a_buf).wait()
        rows = pl.ds(pl.multiple_of(r * 128, 128), 128)
        da = a_buf[rows, :].astype(F32) + xr[rows, :].astype(F32)
        r1, n1 = first_norm(rows)
        scaled = da * gain_rows[0:1, :]
        acc[rows, :] += r1 * (scaled - n1 * jnp.mean(scaled * n1, axis=-1, keepdims=True))

    local(acc, grad_tokens, 1).start()
    gain.z_second()
    rs(24)
    gs[0] = gain.z_total()
    gain.z_sent()
    pair_copy = remote(gs.at[0], gs.at[1], g_sems.at[0], g_sems.at[1], me.xpeer)
    pair_copy.start()
    rs(25)
    pair_copy.wait()
    gain_grads[...] = gs[0] + gs[1]
    for s in range(2):
        kv_core(s).wait_send()
        kv_y(s).wait_send()

    @pl.loop(0, units)
    def _(u):
        gather_a.sent(u)
        by_parity(u, units, lambda j, kind: gather_b[kind].sent(j))

    out_copy(units - 2).wait()
    out_copy(units - 1).wait()
    local(acc, grad_tokens, 1).wait()
    local(xs, output, 0).wait()


def rope_inputs(row_count):
    positions = lax.axis_index("ctx") * row_count + jnp.arange(row_count, dtype=jnp.int32)
    lane = jnp.arange(UNIT, dtype=jnp.int32) % HD
    half_lane = (lane % (HD // 2)).astype(jnp.float32)
    angles = positions.astype(jnp.float32)[:, None] * (rope_base ** (-(2.0 * half_lane) / HD))[None, :]
    cosine = jnp.cos(angles)
    sine = jnp.where(lane[None, :] < HD // 2, -jnp.sin(angles), jnp.sin(angles))
    return positions, cosine, sine


def pack_weights(w_query, w_key, w_value, w_out, w_gate, w_up, w_down):
    depth = w_query.shape[0]
    groups = w_gate.shape[1] // 256
    fed = jnp.concatenate(
        [part.reshape(depth, groups, 256) for part in (w_gate, w_up, w_down.T)], axis=2
    ).reshape(depth, groups * 2 * UNIT)
    flat = jnp.concatenate([w_key, w_value, w_query, w_out.T, fed], axis=1)
    cut = jnp.transpose(flat.reshape(depth, flat.shape[1] // UNIT, UNIT), (1, 0, 2))
    return cut[:, :, :WIDE_A], cut[:, :, WIDE_A:]


def pack_gains(gain_attn, gain_mlp):
    return jnp.pad(jnp.stack([gain_attn, gain_mlp], axis=1), ((0, 0), (0, 126)))[None]


def call_layer(packed_a, packed_b, gains, tokens, cot, cosine, sine, low, high):
    units, depth = packed_a.shape[0], packed_a.shape[1]
    groups = (units - 6) // 2
    struct = jax.ShapeDtypeStruct
    vmem = pltpu.VMEM
    any_spec = pl.BlockSpec(memory_space=pl.ANY)
    vmem_spec = pl.BlockSpec(memory_space=pltpu.VMEM)
    block = (4, 2, 2, depth)
    dma = pltpu.SemaphoreType.DMA
    regular = pltpu.SemaphoreType.REGULAR

    def gather_sems(count):
        return (dma((count, 3)),) + tuple(dma((count,)) for _ in range(5))

    def reduce_sems(count):
        return tuple(dma((count,)) for _ in range(6)) + (dma((count, 3)), dma((count, 2)))

    return pl.pallas_call(
        layer_kernel,
        out_shape=(
            struct((ROWS, WIDE), BF16),
            struct((ROWS, WIDE), F32),
            struct((units, depth, UNIT), F32),
            struct((depth, 128), F32),
            struct((units,) + block + (WIDE_A,), BF16),
            struct((units,) + block + (WIDE_B,), BF16),
            struct((groups, 3, ROWS, 256), BF16),
        ),
        in_specs=[vmem_spec] * 4 + [any_spec] + [vmem_spec] * 4,
        out_specs=(any_spec,) * 3 + (vmem_spec,) + (any_spec,) * 3,
        scratch_shapes=[
            vmem((1,) + block + (128,), BF16),
            vmem((8, WIDE), F32),
            vmem((ROWS, WIDE), BF16),
            vmem((WIDE, ROWS), BF16),
            vmem((WIDE, ROWS), BF16),
            vmem((WIDE, ROWS), BF16),
            vmem((ROWS, WIDE), BF16),
            vmem((2, 2, ROWS, 2 * UNIT), BF16),
            vmem((16, SPAN, 128), BF16),
            vmem((8, 4 * SPAN, 128), BF16),
            vmem((8, 4 * SPAN, 128), BF16),
            vmem((16, 8, SPAN), F32),
            vmem((ROWS, 2 * UNIT), BF16),
            vmem((ROWS, WIDE), F32),
            vmem((ROWS, WIDE), F32),
            vmem((ROWS, WIDE), F32),
            vmem((2,) + block + (2 * UNIT,), BF16),
            vmem((2,) + block + (2 * UNIT,), BF16),
            vmem((2, 3, ROWS, 256), BF16),
            vmem((2, 3, ROWS, 256), BF16),
            vmem((RING, 4, 2, depth, WIDE_A), BF16),
            vmem((RING, 4, depth, WIDE_A), BF16),
            vmem((RING, 4, depth, WIDE_A), BF16),
            vmem((RING, 4, 2, depth, WIDE_B), BF16),
            vmem((RING, 4, depth, WIDE_B), BF16),
            vmem((RING, 4, 2, depth, WIDE_B), BF16),
            vmem((2, depth, UNIT), F32),
            vmem((ROWS, WIDE), BF16),
            vmem((ROWS, WIDE), BF16),
            vmem((16, SPAN, 128), BF16),
            vmem((8, SPAN, 128), F32),
            vmem((4, 4 * SPAN, 128), BF16),
            vmem((4, 4 * SPAN, 128), BF16),
            vmem((2, 2, SPAN, 2 * UNIT), BF16),
            vmem((2, SPAN, 2 * UNIT), BF16),
            vmem((ROWS, 2 * UNIT), BF16),
            vmem((8, WIDE), F32),
            vmem((4, 2, depth, 128), BF16),
            vmem((4, depth, 128), BF16),
            vmem((4, depth, 128), BF16),
            vmem((2, depth, 128), F32),
            gather_sems(units),
            gather_sems(units),
            gather_sems(1),
            reduce_sems(units),
            reduce_sems(units),
            reduce_sems(1),
            regular,
            regular,
            regular((3,)),
            regular,
            dma((4, 4)),
            dma((4, 4)),
            dma((4, 2)),
            dma((4, 2)),
            dma((2,)),
            dma((4,)),
            dma((2, 2, 2)),
            dma((2,)),
            dma((2,)),
            dma((2,)),
        ],
        compiler_params=pltpu.CompilerParams(
            collective_id=1, has_side_effects=True, vmem_limit_bytes=64 << 20
        ),
        name="layer",
    )(packed_a, packed_b, gains, tokens, cot, cosine, sine, low, high)


def fast_body(
    tokens,
    segments,
    cotangent,
    gain_attn,
    w_query,
    w_key,
    w_value,
    w_out,
    gain_mlp,
    w_gate,
    w_up,
    w_down,
):
    positions, cosine, sine = rope_inputs(SPAN)
    mine = lax.dynamic_slice_in_dim(segments, positions[0], SPAN, 1)
    low = jnp.sum((segments[:, None, :] < mine[:, :, None]).astype(jnp.int32), axis=-1)[:, None, :]
    high = positions[None, :]
    packed_a, packed_b = pack_weights(w_query, w_key, w_value, w_out, w_gate, w_up, w_down)
    output, grad_tokens, grads, gain_grads = call_layer(
        packed_a,
        packed_b,
        pack_gains(gain_attn, gain_mlp),
        tokens.reshape(ROWS, WIDE),
        cotangent.reshape(ROWS, WIDE),
        cosine,
        sine,
        low,
        high,
    )[:4]

    def span(lo, hi):
        return jnp.concatenate([grads[i] for i in range(lo, hi)], axis=1)

    fed = [span(2 * i, 2 * i + 2) for i in range(8)]
    gate_grad, up_grad, down_grad = (
        jnp.concatenate([group[:, i * 256 : (i + 1) * 256] for group in fed], axis=1) for i in range(3)
    )
    return (
        output.reshape(tokens.shape),
        grad_tokens.reshape(tokens.shape),
        gain_grads[:, 0],
        span(18, 20),
        grads[20],
        grads[21],
        span(16, 18).T,
        gain_grads[:, 1],
        gate_grad,
        up_grad,
        down_grad.T,
    )


def fits(mesh):
    return mesh.shape["fsdp"] == 4 and mesh.shape["ctx"] == 4 and mesh.shape["tp"] == 2


def solution(mesh):
    placed = (
        P("fsdp", "ctx", None),
        P("fsdp", None),
        P("fsdp", "ctx", None),
        P(("fsdp", "ctx")),
        P(("fsdp", "ctx"), "tp"),
        P(("fsdp", "ctx"), "tp"),
        P(("fsdp", "ctx"), "tp"),
        P("tp", ("fsdp", "ctx")),
        P(("fsdp", "ctx")),
        P(("fsdp", "ctx"), "tp"),
        P(("fsdp", "ctx"), "tp"),
        P("tp", ("fsdp", "ctx")),
    )
    return jax.shard_map(
        fast_body if fits(mesh) else body,
        mesh=mesh,
        in_specs=placed,
        out_specs=(
            P("fsdp", "ctx", None),
            P("fsdp", "ctx", None),
            P(("fsdp", "ctx")),
            P(("fsdp", "ctx"), "tp"),
            P(("fsdp", "ctx"), "tp"),
            P(("fsdp", "ctx"), "tp"),
            P("tp", ("fsdp", "ctx")),
            P(("fsdp", "ctx")),
            P(("fsdp", "ctx"), "tp"),
            P(("fsdp", "ctx"), "tp"),
            P("tp", ("fsdp", "ctx")),
        ),
        check_vma=False,
    )
```

```python
import math

import jax
import jax.numpy as jnp
from jax import lax
from jax.experimental import pallas as pl
from jax.experimental.pallas import tpu as pltpu
from jax.sharding import PartitionSpec as P

HD = 96
GROUP = 2


epsilon = 1e-05
rope_base = 100000.0
negative = -1e30


def rope_tables(positions):
    half_width = HD // 2
    frequency = rope_base ** (-(2.0 * jnp.arange(half_width, dtype=jnp.float32)) / HD)
    angles = positions.astype(jnp.float32)[:, None] * frequency[None, :]
    return (jnp.cos(angles), jnp.sin(angles))


def rotate(vectors, cosine_table, sine_table):
    half_width = vectors.shape[-1] // 2
    former = vectors[..., :half_width]
    latter = vectors[..., half_width:]
    return jnp.concatenate(
        [former * cosine_table - latter * sine_table, latter * cosine_table + former * sine_table],
        axis=-1,
    )


def head_sum(partial_rows):
    return lax.psum(partial_rows.astype(jnp.bfloat16), "tp").astype(jnp.float32)


def weight_gather(shards):
    row_parts = (
        lax.all_gather(shards[0], ("fsdp", "ctx"), axis=0, tiled=True),
        lax.all_gather(shards[1], ("fsdp", "ctx"), axis=0, tiled=True),
        lax.all_gather(shards[2], ("fsdp", "ctx"), axis=0, tiled=True),
        lax.all_gather(shards[3], ("fsdp", "ctx"), axis=0, tiled=True),
        lax.all_gather(shards[4], ("fsdp", "ctx"), axis=0, tiled=True),
        lax.all_gather(shards[5], ("fsdp", "ctx"), axis=0, tiled=True),
        lax.all_gather(shards[6], ("fsdp", "ctx"), axis=0, tiled=True),
    )
    column_parts = (
        lax.all_gather(shards[7], ("fsdp", "ctx"), axis=1, tiled=True),
        lax.all_gather(shards[8], ("fsdp", "ctx"), axis=1, tiled=True),
    )
    return tuple(row_parts) + tuple(column_parts)


def grad_reduce(gradients):
    row_parts = (
        lax.psum_scatter(gradients[0], ("fsdp", "ctx"), scatter_dimension=0, tiled=True),
        lax.psum_scatter(gradients[1], ("fsdp", "ctx"), scatter_dimension=0, tiled=True),
        lax.psum_scatter(gradients[2], ("fsdp", "ctx"), scatter_dimension=0, tiled=True),
        lax.psum_scatter(gradients[3], ("fsdp", "ctx"), scatter_dimension=0, tiled=True),
        lax.psum_scatter(gradients[4], ("fsdp", "ctx"), scatter_dimension=0, tiled=True),
        lax.psum_scatter(gradients[5], ("fsdp", "ctx"), scatter_dimension=0, tiled=True),
        lax.psum_scatter(gradients[6], ("fsdp", "ctx"), scatter_dimension=0, tiled=True),
    )
    column_parts = (
        lax.psum_scatter(gradients[7], ("fsdp", "ctx"), scatter_dimension=1, tiled=True),
        lax.psum_scatter(gradients[8], ("fsdp", "ctx"), scatter_dimension=1, tiled=True),
    )
    return tuple(row_parts) + tuple(column_parts)


def block_scores(queries, key_block, query_seg, positions, key_seg, key_start):
    score_scale = 1.0 / math.sqrt(queries.shape[-1])
    key_positions = key_start + jnp.arange(key_block.shape[0], dtype=jnp.int32)
    allowed = (query_seg[:, None] == key_seg[None, :]) & (
        positions[:, None] >= key_positions[None, :]
    )
    raw_scores = jnp.einsum(
        "qhgd,khd->hgqk", queries, key_block, preferred_element_type=jnp.float32
    )
    return (jnp.where(allowed, raw_scores * score_scale, negative), allowed)


def block_fetch(
    key_all, value_all, segment_row, block_index, block_keys, last_position, first_segment
):
    key_start = block_index * block_keys
    key_block = lax.dynamic_slice_in_dim(key_all, key_start, block_keys, 0)
    value_block = lax.dynamic_slice_in_dim(value_all, key_start, block_keys, 0)
    key_seg = lax.dynamic_slice_in_dim(segment_row, key_start, block_keys, 0)
    needed = (key_start <= last_position) & (key_seg[block_keys - 1] >= first_segment)
    return (key_start, key_block, value_block, key_seg, needed)


def attention_forward(queries, key_all, value_all, segment_row, query_seg, positions):
    row_count, heads_kv, group_size, head_dim = queries.shape
    length = key_all.shape[0]
    block_keys = math.gcd(512, length)
    block_total = length // block_keys
    last_position = positions[row_count - 1]
    first_segment = query_seg[0]

    def stats_step(block_index, state):
        key_start, key_block, value_block, key_seg, needed = block_fetch(
            key_all, value_all, segment_row, block_index, block_keys, last_position, first_segment
        )
        top_old, total_old = state
        scores, allowed = block_scores(queries, key_block, query_seg, positions, key_seg, key_start)
        top_new = jnp.maximum(top_old, jnp.max(scores, axis=-1))
        weights = jnp.where(allowed, jnp.exp(scores - top_new[..., None]), 0.0)
        return (top_new, total_old * jnp.exp(top_old - top_new) + jnp.sum(weights, axis=-1))

    start_top = jnp.full((heads_kv, group_size, row_count), negative, jnp.float32)
    row_top, row_total = lax.fori_loop(
        0, block_total, stats_step, (start_top, jnp.zeros_like(start_top))
    )

    def output_step(block_index, state):
        key_start, key_block, value_block, key_seg, needed = block_fetch(
            key_all, value_all, segment_row, block_index, block_keys, last_position, first_segment
        )
        scores, allowed = block_scores(queries, key_block, query_seg, positions, key_seg, key_start)
        probability = (
            jnp.where(allowed, jnp.exp(scores - row_top[..., None]), 0.0) / row_total[..., None]
        )
        return state + jnp.einsum(
            "hgqk,khd->qhgd",
            probability.astype(jnp.bfloat16),
            value_block,
            preferred_element_type=jnp.float32,
        )

    start_out = jnp.zeros((row_count, heads_kv, group_size, head_dim), jnp.float32)
    out_low = lax.fori_loop(0, block_total, output_step, start_out)
    return (row_top, row_total, out_low)


def attention_backward(
    queries,
    key_all,
    value_all,
    segment_row,
    query_seg,
    positions,
    row_top,
    row_total,
    grad_mixed,
    row_delta,
):
    row_count, heads_kv, group_size, head_dim = queries.shape
    length = key_all.shape[0]
    block_keys = math.gcd(512, length)
    block_total = length // block_keys
    last_position = positions[row_count - 1]
    first_segment = query_seg[0]
    score_scale = 1.0 / math.sqrt(head_dim)

    def grad_step(block_index, state):
        key_start, key_block, value_block, key_seg, needed = block_fetch(
            key_all, value_all, segment_row, block_index, block_keys, last_position, first_segment
        )
        grad_query, grad_keys, grad_values = state
        scores, allowed = block_scores(queries, key_block, query_seg, positions, key_seg, key_start)
        probability = (
            jnp.where(allowed, jnp.exp(scores - row_top[..., None]), 0.0) / row_total[..., None]
        )
        grad_prob = jnp.einsum(
            "qhgd,khd->hgqk", grad_mixed, value_block, preferred_element_type=jnp.float32
        )
        grad_score = (probability * (grad_prob - row_delta[..., None]) * score_scale).astype(
            jnp.bfloat16
        )
        grad_query = grad_query + jnp.einsum(
            "hgqk,khd->qhgd", grad_score, key_block, preferred_element_type=jnp.float32
        )
        key_part = jnp.einsum(
            "hgqk,qhgd->khd", grad_score, queries, preferred_element_type=jnp.float32
        )
        value_part = jnp.einsum(
            "hgqk,qhgd->khd",
            probability.astype(jnp.bfloat16),
            grad_mixed,
            preferred_element_type=jnp.float32,
        )
        grad_keys = lax.dynamic_update_slice_in_dim(grad_keys, key_part, key_start, 0)
        grad_values = lax.dynamic_update_slice_in_dim(grad_values, value_part, key_start, 0)
        return (grad_query, grad_keys, grad_values)

    start_query = jnp.zeros((row_count, heads_kv, group_size, head_dim), jnp.float32)
    start_keys = jnp.zeros((length, heads_kv, head_dim), jnp.float32)
    return lax.fori_loop(0, block_total, grad_step, (start_query, start_keys, start_keys))


def micro_step(gathered, token_rows, segment_row, grad_in, positions, cosine_table, sine_table):
    gain_attn, w_query, w_key, w_value, gain_mlp, w_gate, w_up, w_out, w_down = gathered
    row_count = token_rows.shape[0]
    heads_kv = w_key.shape[1] // HD
    cos_four = cosine_table[:, None, None, :]
    sin_four = sine_table[:, None, None, :]
    cos_three = cosine_table[:, None, :]
    sin_three = sine_table[:, None, :]
    query_seg = lax.dynamic_slice_in_dim(segment_row, positions[0], row_count, 0)
    gain_first = gain_attn.astype(jnp.float32)
    gain_second = gain_mlp.astype(jnp.float32)
    inputs = token_rows.astype(jnp.float32)
    scale_first = lax.rsqrt(jnp.mean(inputs * inputs, axis=-1, keepdims=True) + epsilon)
    normal_first = inputs * scale_first
    normed = (normal_first * gain_first).astype(jnp.bfloat16)
    query_raw = jnp.dot(normed, w_query, preferred_element_type=jnp.float32).reshape(
        row_count, heads_kv, GROUP, HD
    )
    key_raw = jnp.dot(normed, w_key, preferred_element_type=jnp.float32).reshape(
        row_count, heads_kv, HD
    )
    value_low = (
        jnp.dot(normed, w_value, preferred_element_type=jnp.float32)
        .astype(jnp.bfloat16)
        .reshape(row_count, heads_kv, HD)
    )
    query_low = rotate(query_raw, cos_four, sin_four).astype(jnp.bfloat16)
    key_low = rotate(key_raw, cos_three, sin_three).astype(jnp.bfloat16)
    key_all, value_all = (
        lax.all_gather(key_low, "ctx", axis=0, tiled=True),
        lax.all_gather(value_low, "ctx", axis=0, tiled=True),
    )
    row_top, row_total, out_low = attention_forward(
        query_low, key_all, value_all, segment_row, query_seg, positions
    )
    mixed_low = out_low.reshape(row_count, -1).astype(jnp.bfloat16)
    middle = inputs + head_sum(jnp.dot(mixed_low, w_out, preferred_element_type=jnp.float32))
    scale_second = lax.rsqrt(jnp.mean(middle * middle, axis=-1, keepdims=True) + epsilon)
    normal_second = middle * scale_second
    second = (normal_second * gain_second).astype(jnp.bfloat16)
    gate_part = jnp.dot(second, w_gate, preferred_element_type=jnp.float32)
    upward = jnp.dot(second, w_up, preferred_element_type=jnp.float32)
    sigmoid_gate = jax.nn.sigmoid(gate_part)
    silu_gate = gate_part * sigmoid_gate
    hidden = (silu_gate * upward).astype(jnp.bfloat16)
    result_rows = middle + head_sum(jnp.dot(hidden, w_down, preferred_element_type=jnp.float32))
    output_rows = result_rows.astype(jnp.bfloat16)
    grad_final = grad_in.astype(jnp.float32)
    grad_down = jnp.einsum("tf,td->fd", hidden, grad_in, preferred_element_type=jnp.float32)
    grad_hidden = jnp.einsum("td,fd->tf", grad_in, w_down, preferred_element_type=jnp.float32)
    grad_gate_low = (
        grad_hidden * upward * sigmoid_gate * (1.0 + gate_part * (1.0 - sigmoid_gate))
    ).astype(jnp.bfloat16)
    grad_up_low = (grad_hidden * silu_gate).astype(jnp.bfloat16)
    grad_gate = jnp.einsum("td,tf->df", second, grad_gate_low, preferred_element_type=jnp.float32)
    grad_up = jnp.einsum("td,tf->df", second, grad_up_low, preferred_element_type=jnp.float32)
    grad_second = head_sum(
        jnp.einsum("tf,df->td", grad_gate_low, w_gate, preferred_element_type=jnp.float32)
        + jnp.einsum("tf,df->td", grad_up_low, w_up, preferred_element_type=jnp.float32)
    )
    scaled_second = grad_second * gain_second
    grad_gain_mlp = jnp.sum(grad_second * normal_second, axis=0)
    grad_middle = grad_final + scale_second * (
        scaled_second
        - normal_second * jnp.mean(scaled_second * normal_second, axis=-1, keepdims=True)
    )
    grad_middle_low = grad_middle.astype(jnp.bfloat16)
    grad_out = jnp.einsum(
        "tk,td->kd", mixed_low, grad_middle_low, preferred_element_type=jnp.float32
    )
    grad_mixed = (
        jnp.einsum("td,kd->tk", grad_middle_low, w_out, preferred_element_type=jnp.float32)
        .astype(jnp.bfloat16)
        .reshape(row_count, heads_kv, GROUP, HD)
    )
    row_delta = jnp.transpose(jnp.sum(grad_mixed.astype(jnp.float32) * out_low, axis=-1), (1, 2, 0))
    grad_query_rot, grad_keys, grad_values = attention_backward(
        query_low,
        key_all,
        value_all,
        segment_row,
        query_seg,
        positions,
        row_top,
        row_total,
        grad_mixed,
        row_delta,
    )
    grad_key_mine, grad_value_mine = (
        lax.psum_scatter(
            grad_keys.astype(jnp.bfloat16), "ctx", scatter_dimension=0, tiled=True
        ).astype(jnp.float32),
        lax.psum_scatter(
            grad_values.astype(jnp.bfloat16), "ctx", scatter_dimension=0, tiled=True
        ).astype(jnp.float32),
    )
    grad_query_low = (
        rotate(grad_query_rot, cos_four, -sin_four).astype(jnp.bfloat16).reshape(row_count, -1)
    )
    grad_key_low = (
        rotate(grad_key_mine, cos_three, -sin_three).astype(jnp.bfloat16).reshape(row_count, -1)
    )
    grad_value_low = grad_value_mine.astype(jnp.bfloat16).reshape(row_count, -1)
    grad_query = jnp.einsum("td,tk->dk", normed, grad_query_low, preferred_element_type=jnp.float32)
    grad_key = jnp.einsum("td,tk->dk", normed, grad_key_low, preferred_element_type=jnp.float32)
    grad_value = jnp.einsum("td,tk->dk", normed, grad_value_low, preferred_element_type=jnp.float32)
    grad_normed = head_sum(
        jnp.einsum("tk,dk->td", grad_query_low, w_query, preferred_element_type=jnp.float32)
        + jnp.einsum("tk,dk->td", grad_key_low, w_key, preferred_element_type=jnp.float32)
        + jnp.einsum("tk,dk->td", grad_value_low, w_value, preferred_element_type=jnp.float32)
    )
    scaled_first = grad_normed * gain_first
    grad_gain_attn = jnp.sum(grad_normed * normal_first, axis=0)
    grad_tokens = grad_middle + scale_first * (
        scaled_first - normal_first * jnp.mean(scaled_first * normal_first, axis=-1, keepdims=True)
    )
    gradients = (
        grad_gain_attn,
        grad_query,
        grad_key,
        grad_value,
        grad_gain_mlp,
        grad_gate,
        grad_up,
        grad_out,
        grad_down,
    )
    return (output_rows, grad_tokens, gradients)


def body(
    tokens,
    segments,
    cotangent,
    gain_attn,
    w_query,
    w_key,
    w_value,
    w_out,
    gain_mlp,
    w_gate,
    w_up,
    w_down,
):
    micro_count = tokens.shape[0]
    row_count = tokens.shape[1]
    positions = lax.axis_index("ctx") * row_count + jnp.arange(row_count, dtype=jnp.int32)
    cosine_table, sine_table = rope_tables(positions)
    shards = (gain_attn, w_query, w_key, w_value, gain_mlp, w_gate, w_up, w_out, w_down)
    outputs = []
    token_grads = []
    gathered = weight_gather(shards)
    totals = None
    for micro_index in range(micro_count):
        output_rows, grad_rows, grads_now = micro_step(
            gathered,
            tokens[micro_index],
            segments[micro_index],
            cotangent[micro_index],
            positions,
            cosine_table,
            sine_table,
        )
        outputs.append(output_rows)
        token_grads.append(grad_rows)
        totals = (
            grads_now
            if totals is None
            else tuple(earlier + addend for earlier, addend in zip(totals, grads_now))
        )
    reduced = tuple(
        tensor_piece.astype(jnp.float32)
        for tensor_piece in grad_reduce(tuple(total.astype(jnp.bfloat16) for total in totals))
    )
    return (
        jnp.stack(outputs),
        jnp.stack(token_grads),
        reduced[0],
        reduced[1],
        reduced[2],
        reduced[3],
        reduced[7],
        reduced[4],
        reduced[5],
        reduced[6],
        reduced[8],
    )


MESH = pl.DeviceIdType.MESH
UNIT = 384
ROWS = 512
SPAN = 256
WIDE = 1536
F32 = jnp.float32
BF16 = jnp.bfloat16
NT = (((1,), (1,)), ((), ()))
TN = (((0,), (0,)), ((), ()))


def dot_nn(a, b):
    return jnp.dot(a, b, preferred_element_type=F32)


def dot_nt(a, b):
    return lax.dot_general(a, b, NT, preferred_element_type=F32)


def dot_tn(a, b):
    return lax.dot_general(a, b, TN, preferred_element_type=F32)


class Place:
    def __init__(self):
        f, c, t = (lax.axis_index(axis) for axis in ("fsdp", "ctx", "tp"))
        self.f, self.c, self.t = f, c, t
        self.y, self.k = lax.div(c, 2), lax.rem(c, 2)
        self.oy, self.ok = 1 - self.y, 1 - self.k
        self.half = lax.div(f, 2)
        self.inner = (f == 1) | (f == 2)
        self.edge = (f == 0) | (f == 3)
        self.near_f = f + 1 - 2 * lax.rem(f, 2)
        self.mid_f = 2 - self.half
        self.far_f = 3 - 3 * self.half
        self.near = (self.near_f, c, t)
        self.mid = (self.mid_f, c, t)
        self.far = (self.far_f, c, t)
        self.ypeer = (f, c + 2 - 4 * self.y, t)
        self.sib = (f, c + 1 - 2 * self.k, t)
        self.xpeer = (f, c, 1 - t)

    def barrier(self):
        sem = pltpu.get_barrier_semaphore()
        others = [(lax.rem(self.f + step, 4), self.c, self.t) for step in (1, 2, 3)]
        others += [self.ypeer, self.sib, self.xpeer]
        for other in others:
            pl.semaphore_signal(sem, inc=1, device_id=other, device_id_type=MESH)
        pl.semaphore_wait(sem, len(others))


def remote(src, dst, send, recv, device):
    return pltpu.make_async_remote_copy(
        src_ref=src,
        dst_ref=dst,
        send_sem=send,
        recv_sem=recv,
        device_id=device,
        device_id_type=MESH,
    )


def lanes(rows, columns):
    return lax.broadcasted_iota(jnp.int32, (rows, columns), 1)


def unpack_heads(x):
    lane = lanes(x.shape[0], 128)
    one, two, three = x[:, :128], x[:, 128:256], x[:, 256:]
    heads = (
        one,
        pltpu.roll(jnp.where(lane < 64, two, one), 32, 1),
        pltpu.roll(jnp.where(lane < 32, three, two), 64, 1),
        pltpu.roll(three, 96, 1),
    )
    return [jnp.where(lane < HD, head, 0.0) for head in heads]


def pack_heads(heads):
    lane = lanes(heads[0].shape[0], 128)
    second = pltpu.roll(heads[1], 96, 1)
    third = pltpu.roll(heads[2], 64, 1)
    fourth = pltpu.roll(heads[3], 32, 1)
    return jnp.concatenate(
        [
            jnp.where(lane < 96, heads[0], second),
            jnp.where(lane < 64, second, third),
            jnp.where(lane < 32, third, fourth),
        ],
        axis=1,
    )


def turn(x, cosine, sine):
    lane = lax.rem(lanes(x.shape[0], UNIT), HD)
    swapped = jnp.where(lane < HD // 2, pltpu.roll(x, UNIT - HD // 2, 1), pltpu.roll(x, HD // 2, 1))
    return x * cosine + swapped * sine


def transpose_into(dst, src):
    @pl.loop(0, WIDE // 128)
    def _(i):
        at = pl.multiple_of(i * 128, 128)
        dst[pl.ds(at, 128), :] = src[:, pl.ds(at, 128)].astype(F32).T.astype(BF16)


def weight(buf, slot, lo, hi):
    return buf[slot, :, :, :, :, lo:hi].reshape(WIDE, hi - lo)


def allowed_keys(low_row, high_row):
    row = lax.broadcasted_iota(jnp.int32, (4 * SPAN, SPAN), 0)
    return (row >= low_row) & (row <= high_row)


RING = 5
GATHER_ALIKE = True
REDUCE_ALIKE = True
WIDE_A = 256
WIDE_B = 128


class GatherA:
    def __init__(self, me, buf, source, sems):
        self.me, self.buf, self.source = me, buf, source
        self.z_send, self.z_recv, self.y_send, self.y_recv, self.c_send, self.c_recv = sems

    def z_copy(self, j, i):
        me = self.me
        dst = self.buf.at[j, me.f, me.y, me.k]
        return remote(self.source.at[j], dst, self.z_send.at[j, i], self.z_recv.at[j], (me.near, me.mid)[i])

    def hand_copy(self, j):
        me = self.me
        part = self.buf.at[j, pl.ds(2 - 2 * me.half, 2), me.y, me.k]
        return remote(part, part, self.z_send.at[j, 2], self.z_recv.at[j], me.near)

    def y_copy(self, j):
        me = self.me
        part = self.buf.at[j, :, me.y, me.k]
        return remote(part, part, self.y_send.at[j], self.y_recv.at[j], me.ypeer)

    def core_copy(self, j):
        me = self.me
        part = self.buf.at[j, :, :, me.k]
        return remote(part, part, self.c_send.at[j], self.c_recv.at[j], me.sib)

    def z_wait(self, j):
        me = self.me
        three = self.buf.at[j, pl.ds(0, 3), me.y, me.k]
        remote(three, three, self.z_send.at[j, 0], self.z_recv.at[j], me.near).wait_recv()

    def start(self, j):
        for i in range(2):
            self.z_copy(j, i).start()

    def spread(self, j):
        pass

    def hand(self, j):
        @pl.when(self.me.inner)
        def _():
            self.z_wait(j)
            self.hand_copy(j).start()

    def turn(self, j):
        @pl.when(self.me.edge)
        def _():
            self.z_wait(j)

        self.y_copy(j).start()

    def core(self, j):
        self.y_copy(j).wait_recv()
        self.core_copy(j).start()

    def done(self, j):
        self.core_copy(j).wait_recv()

    def sent(self, j):
        for i in range(2):
            self.z_copy(j, i).wait_send()

        @pl.when(self.me.inner)
        def _():
            self.hand_copy(j).wait_send()

        self.y_copy(j).wait_send()
        self.core_copy(j).wait_send()


class GatherB(GatherA):
    def z_copy(self, j, i):
        me = self.me
        part = self.buf.at[j, me.f, :, me.k]
        return remote(part, part, self.z_send.at[j, i], self.z_recv.at[j], (me.near, me.mid)[i])

    def hand_copy(self, j):
        me = self.me
        part = self.buf.at[j, pl.ds(2 - 2 * me.half, 2), :, me.k]
        return remote(part, part, self.z_send.at[j, 2], self.z_recv.at[j], me.near)

    def y_copy(self, j):
        me = self.me
        dst = self.buf.at[j, me.f, me.y, me.k]
        return remote(self.source.at[j], dst, self.y_send.at[j], self.y_recv.at[j], me.ypeer)

    def z_wait(self, j):
        me = self.me
        three = self.buf.at[j, pl.ds(0, 3), :, me.k]
        remote(three, three, self.z_send.at[j, 0], self.z_recv.at[j], me.near).wait_recv()

    def start(self, j):
        self.y_copy(j).start()

    def spread(self, j):
        self.y_copy(j).wait_recv()
        for i in range(2):
            self.z_copy(j, i).start()

    def turn(self, j):
        pass

    def core(self, j):
        @pl.when(self.me.edge)
        def _():
            self.z_wait(j)

        self.core_copy(j).start()


class ReduceA:
    def __init__(self, me, r, other, mine, bufs, sems):
        self.me, self.r, self.other, self.mine = me, r, other, mine
        self.r1, self.r2, self.r3 = bufs
        (
            self.c_send,
            self.c_recv,
            self.y_send,
            self.y_recv,
            self.za_send,
            self.za_recv,
            self.zb_send,
            self.zb_recv,
        ) = sems
        self.zed = self.r2

    def core_copy(self):
        return remote(self.other, self.r1, self.c_send.at[self.r], self.c_recv.at[self.r], self.me.sib)

    def y_copy(self):
        src = self.r1.at[:, self.me.oy]
        return remote(src, self.r2, self.y_send.at[self.r], self.y_recv.at[self.r], self.me.ypeer)

    def za_copy(self):
        src = self.zed.at[pl.ds(1 - self.me.half, 3)]
        dst = self.r3.at[pl.ds(0, 3)]
        return remote(src, dst, self.za_send.at[self.r], self.za_recv.at[self.r], self.me.near)

    def zb_copy(self, i):
        me = self.me
        owner, at, device = ((me.near_f, 0, me.near), (me.mid_f, 3, me.mid), (me.far_f, 1, me.far))[i]
        recv = self.zb_recv.at[self.r, min(i, 1)]
        return remote(self.zed.at[owner], self.r3.at[at], self.zb_send.at[self.r, i], recv, device)

    def core(self):
        self.core_copy().start()

    def add_core(self):
        self.core_copy().wait_recv()
        self.r1[...] = self.r1[...] + self.mine[...]
        self.core_copy().wait_send()

    def z_first(self):
        @pl.when(self.me.edge)
        def _():
            self.za_copy().start()

    def z_second(self, before=None):
        me = self.me

        @pl.when(me.inner)
        def _():
            self.za_copy().wait_recv()
            for owner in (me.mid_f, me.far_f):
                self.zed[owner] = self.zed[owner] + self.r3[owner - (1 - me.half)]
            if before is not None:
                before()
            for i in range(3):
                self.zb_copy(i).start()

    def z_total(self):
        me = self.me
        self.zb_copy(1).wait_recv()

        @pl.when(me.edge)
        def _():
            self.zb_copy(0).wait_recv()

        one = jnp.where(me.edge, 0, me.f - (1 - me.half))
        two = jnp.where(me.edge, 1, 3)
        return self.zed[me.f].astype(F32) + self.r3[one].astype(F32) + self.r3[two].astype(F32)

    def z_sent(self):
        @pl.when(self.me.edge)
        def _():
            self.za_copy().wait_send()

        @pl.when(self.me.inner)
        def _():
            for i in range(3):
                self.zb_copy(i).wait_send()

    def y_start(self):
        self.y_copy().start()

    def y_add(self):
        self.y_copy().wait_recv()
        self.r2[...] = self.r2[...] + self.r1[:, self.me.y]
        self.y_copy().wait_send()


class ReduceB(ReduceA):
    def __init__(self, *args):
        super().__init__(*args)
        self.zed = self.r1

    def y_copy(self):
        src = self.r1.at[self.me.f, self.me.oy]
        return remote(src, self.r2, self.y_send.at[self.r], self.y_recv.at[self.r], self.me.ypeer)

    def z_end(self):
        self.r1[self.me.f] = self.z_total().astype(BF16)
        self.z_sent()
        self.y_copy().start()

    def total(self):
        self.y_copy().wait_recv()
        out = self.r1[self.me.f, self.me.y].astype(F32) + self.r2[...].astype(F32)
        self.y_copy().wait_send()
        return out


def layer_kernel(
    packed,
    gains,
    tokens,
    cot,
    cosine,
    sine,
    low,
    high,
    output,
    grad_tokens,
    grads,
    gain_grads,
    wa,
    wb,
    fed,
    out_peer,
    gw,
    gain_rows,
    a_buf,
    at,
    bt,
    et,
    eb,
    kvx,
    qh,
    kh,
    vh,
    lse,
    ob,
    x2,
    acc,
    out_acc,
    wbuf,
    part,
    stage,
    back,
    ra1,
    ra2,
    ra3,
    rb1,
    rb2,
    rb3,
    gout,
    xs,
    xr,
    doh,
    heads,
    dkh,
    dvh,
    rc,
    ry,
    dqb,
    gacc,
    g1,
    g2,
    g3,
    gs,
    ga_sems,
    gb_sems,
    gg_sems,
    ra_sems,
    rb_sems,
    rg_sems,
    c_cred,
    y_cred,
    z_cred,
    x_cred,
    x_send,
    x_recv,
    kv_send,
    kv_recv,
    g_sems,
    load_sem,
    w_sem,
    stage_sem,
    back_sem,
    out_sem,
    own_sem,
):
    me = Place()
    f, y, k = me.f, me.y, me.k
    units, depth = packed.shape[0], packed.shape[1]
    packed_a = packed.at[:, :, pl.ds(0, WIDE_A)]
    packed_b = packed.at[:, :, pl.ds(WIDE_A, WIDE_B)]
    groups = fed.shape[0]
    scale = 1.0 / math.sqrt(HD)

    def local(src, dst, i):
        return pltpu.make_async_copy(src, dst, load_sem.at[i])

    def own_copies(u):
        b = u // 2
        side = u % 2 * UNIT
        held = wbuf.at[0, b // 4, b // 2 % 2, b % 2]
        return (
            pltpu.make_async_copy(packed.at[u], held.at[:, pl.ds(side, UNIT)], own_sem.at[0, u]),
            pltpu.make_async_copy(held.at[:, pl.ds(side, WIDE_A)], wa.at[u, f, y, k], own_sem.at[1, u]),
            pltpu.make_async_copy(held.at[:, pl.ds(side + WIDE_A, WIDE_B)], wb.at[u, f, y, k], own_sem.at[2, u]),
        )

    own = [own_copies(u) for u in range(units)]
    own_gain = local(gains.at[0], gw.at[0, f, y, k], 2)
    own_gain.start()
    for copies in own:
        copies[0].start()
    local(cot, eb, 3).start()
    me.barrier()

    gather_a = GatherA(me, wa, packed_a, ga_sems)
    gather_b = (GatherA(me, wb, packed_b, gb_sems), GatherB(me, wb, packed_b, gb_sems))
    gather_g = GatherA(me, gw, gains, gg_sems)

    def within(i, count, act):
        if isinstance(i, int):
            if 0 <= i < count:
                act(i)
        else:
            pl.when((i >= 0) & (i < count))(lambda: act(i))

    def is_even(i):
        return jnp.array(False) if REDUCE_ALIKE else lax.rem(i, 2) == 0

    def by_parity(i, count, act, alike):
        def both(j):
            if alike:
                act(j, 1)
            elif isinstance(j, int):
                act(j, j % 2)
            else:
                pl.when(lax.rem(j, 2) == 0)(lambda: act(j, 0))
                pl.when(lax.rem(j, 2) == 1)(lambda: act(j, 1))

        within(i, count, both)

    def ag(t):
        def run(lag, gather, name):
            within(t + lag, units, getattr(gather, name))

        def split(lag, name):
            by_parity(t + lag, units, lambda j, kind: getattr(gather_b[kind], name)(j), GATHER_ALIKE)

        def even(j, kind):
            if kind == 0:
                gather_b[0].start(j)

        def odd(j, kind):
            if kind == 1:
                gather_b[1].start(j)

        by_parity(t + 6, units, odd, GATHER_ALIKE)
        run(4, gather_a, "start")
        by_parity(t + 4, units, even, GATHER_ALIKE)
        split(4, "spread")
        run(2, gather_a, "hand")
        split(2, "hand")
        run(0, gather_a, "turn")
        split(0, "turn")
        run(-1, gather_a, "core")
        split(-1, "core")
        run(-2, gather_a, "done")
        run(-2, gather_b[0], "done")

    def load(u, slot, side):
        at_b = side * UNIT + WIDE_A
        return (
            pltpu.make_async_copy(
                wa.at[u], wbuf.at[slot, :, :, :, :, pl.ds(side * UNIT, WIDE_A)], w_sem.at[slot, side, 0]
            ),
            pltpu.make_async_copy(
                wb.at[u], wbuf.at[slot, :, :, :, :, pl.ds(at_b, WIDE_B)], w_sem.at[slot, side, 1]
            ),
        )

    def load_start(u, slot, side):
        for copy in load(u, slot, side):
            copy.start()

    def load_wait(u, slot, side):
        for copy in load(u, slot, side):
            copy.wait()

    def ring(r):
        s = lax.rem(r, RING)
        slot = lax.rem(lax.div(r, 2), 2)
        start = lax.rem(r, 2) * UNIT
        cols_a = pl.ds(pl.multiple_of(start, 128), WIDE_A)
        cols_b = pl.ds(pl.multiple_of(start + WIDE_A, 128), WIDE_B)
        one = ReduceA(
            me,
            r,
            part.at[slot, :, :, me.ok, :, cols_a],
            part.at[slot, :, :, k, :, cols_a],
            (ra1.at[s], ra2.at[s], ra3.at[s]),
            ra_sems,
        )
        other, mine = part.at[slot, :, :, me.ok, :, cols_b], part.at[slot, :, :, k, :, cols_b]
        two = (
            ReduceA(me, r, other, mine, (rb1.at[s], rb2.at[s], rb3.at[s, :, 0]), rb_sems),
            ReduceB(me, r, other, mine, (rb1.at[s], rb2.at[s, 0], rb3.at[s]), rb_sems),
        )
        return one, two

    def credit(r, sem):
        within(r - RING, units, lambda i: pl.semaphore_wait(sem, 1))

    def give(r, sem, device):
        def act(i):
            pl.semaphore_signal(sem, inc=1, device_id=device, device_id_type=MESH)

        within(r + RING, units, act)

    def out_copy(i):
        slot = lax.rem(i, 2)
        return pltpu.make_async_copy(gout.at[slot], grads.at[i], out_sem.at[slot])

    def rs(r):
        def credit_near(i):
            @pl.when(me.edge)
            def _():
                credit(i, z_cred.at[0])

        def credit_inner(i):
            for j in range(3):
                credit(i, z_cred.at[j])

        def first_a(i):
            credit(i, c_cred)
            ring(i)[0].core()

        def second_a(i):
            one = ring(i)[0]
            one.add_core()
            credit(i, y_cred)
            one.y_start()

        def third_a(i):
            one = ring(i)[0]
            one.y_add()

            @pl.when(is_even(i))
            def _():
                credit_near(i)

            one.z_first()

        def fourth_a(i):
            ring(i)[0].z_second(lambda: pl.when(is_even(i))(lambda: credit_inner(i)))

        def fifth_a(i):
            one = ring(i)[0]
            within(i - 2, units, lambda j: out_copy(j).wait())
            gout[lax.rem(i, 2), :, 0:WIDE_A] = one.z_total()
            one.z_sent()

        def first_b(i):
            ring(i)[1][0].core()

        def second_b(i, kind):
            two = ring(i)[1][kind]
            two.add_core()
            if kind == 0:
                two.y_start()
            else:
                credit_near(i)
                two.z_first()

        def third_b(i, kind):
            two = ring(i)[1][kind]
            if kind == 0:
                two.y_add()
                two.z_first()
            else:
                two.z_second(lambda: credit_inner(i))

        def fourth_b(i, kind):
            two = ring(i)[1][kind]
            if kind == 0:
                two.z_second()
            else:
                two.z_end()

        def fifth_b(i, kind):
            two = ring(i)[1][kind]
            if kind == 0:
                gout[lax.rem(i, 2), :, WIDE_A:] = two.z_total()
                two.z_sent()
            else:
                gout[lax.rem(i, 2), :, WIDE_A:] = two.total()

        def last(i):
            out_copy(i).start()
            give(i, c_cred, me.sib)
            give(i, y_cred, me.ypeer)

            @pl.when(me.edge)
            def _():
                give(i, z_cred.at[0], me.near)
                give(i, z_cred.at[2], me.mid)

            @pl.when(me.inner)
            def _():
                give(i, z_cred.at[0], me.near)
                give(i, z_cred.at[1], me.mid)

        within(r - 4, units, fifth_a)
        within(r - 3, units, fourth_a)
        within(r - 2, units, third_a)
        within(r - 1, units, second_a)
        within(r, units, first_a)
        by_parity(r - 4, units, fifth_b, REDUCE_ALIKE)
        by_parity(r - 3, units, fourth_b, REDUCE_ALIKE)
        by_parity(r - 2, units, third_b, REDUCE_ALIKE)
        by_parity(r - 1, units, second_b, REDUCE_ALIKE)
        within(r, units, first_b)
        within(r - 4, units, last)

    def put(pair, i, value):
        columns = slice(i * 256, (i + 1) * 256)
        part[lax.rem(pair, 2), :, :, :, :, columns] = value.astype(BF16).reshape(4, 2, 2, depth, 256)

    def x_copy(e, r, src):
        rows = pl.ds(pl.multiple_of(r * 128, 128), 128)
        dst = out_peer if e == 2 else xr
        return remote(src.at[rows], dst.at[rows], x_send.at[e, r], x_recv.at[e, r], me.xpeer)

    def give_x():
        pl.semaphore_signal(x_cred, inc=1, device_id=me.xpeer, device_id_type=MESH)

    def take_x():
        pl.semaphore_wait(x_cred, 1)

    gather_g.start(0)
    ag(-6)
    for copies in own:
        copies[0].wait()
        copies[1].start()
        copies[2].start()
    ag(-5)
    own_gain.wait()
    for copies in own:
        copies[1].wait()
        copies[2].wait()
    gather_g.hand(0)
    gather_g.turn(0)
    ag(-4)
    local(cot, eb, 3).wait()
    transpose_into(et, eb)
    gather_g.core(0)
    ag(-3)
    gather_g.done(0)
    gain_rows[...] = gw[0].reshape(WIDE, 128).astype(F32).T[:8, :]
    ag(-2)
    ag(-1)

    @pl.loop(0, ROWS // 64)
    def _(i):
        rows = pl.ds(pl.multiple_of(i * 64, 64), 64)
        x = tokens[rows, :].astype(F32)
        r = lax.rsqrt(jnp.mean(x * x, axis=-1, keepdims=True) + epsilon)
        a_buf[rows, :] = (x * r * gain_rows[0:1, :]).astype(BF16)

    ag(0)
    transpose_into(at, a_buf)
    ag(1)
    ag(2)
    load_start(0, 0, 0)
    ag(3)
    load_start(1, 0, 1)
    load_wait(0, 0, 0)
    load_wait(1, 0, 1)

    def kv_copy(i, s):
        core = (y, k) if i == 0 else (slice(None), k)
        half = kvx.at[core[0], core[1], pl.ds(s * SPAN, SPAN)]
        return remote(half, half, kv_send.at[i, s], kv_recv.at[i, s], me.sib if i else me.ypeer)

    for s in range(2):
        rows = pl.ds(s * SPAN, SPAN)
        pair = dot_nn(a_buf[rows, :], weight(wbuf, 0, 0, 2 * UNIT))
        kvx[y, k, rows, :UNIT] = turn(pair[:, :UNIT], cosine[...], sine[...]).astype(BF16)
        kvx[y, k, rows, UNIT:] = pair[:, UNIT:].astype(BF16)
        kv_copy(0, s).start()
    ag(4)
    load_start(2, 1, 0)
    ag(5)
    load_start(3, 1, 1)
    load_wait(2, 1, 0)
    load_wait(3, 1, 1)
    for side in range(2):
        for s in range(2):
            rows = pl.ds(s * SPAN, SPAN)
            query = dot_nn(a_buf[rows, :], weight(wbuf, 1, side * UNIT, (side + 1) * UNIT))
            query = turn(query, cosine[...], sine[...])
            for i, head in enumerate(unpack_heads(query)):
                qh[s * 8 + side * 4 + i] = head.astype(BF16)
    kv_copy(0, 0).wait_recv()
    kv_copy(1, 0).start()
    ag(6)
    load_start(4, 0, 0)
    kv_copy(0, 1).wait_recv()
    kv_copy(1, 1).start()
    ag(7)
    load_start(5, 0, 1)

    def spread_heads(i):
        s, c = lax.div(i, 4), lax.rem(i, 4)
        block = kvx[lax.div(c, 2), lax.rem(c, 2), pl.ds(pl.multiple_of(s * SPAN, SPAN), SPAN), :]
        rows = pl.ds(pl.multiple_of(c * SPAN, SPAN), SPAN)
        for g, head in enumerate(unpack_heads(block[:, :UNIT].astype(F32))):
            kh[s * 4 + g, rows, :] = head.astype(BF16)
        for g, head in enumerate(unpack_heads(block[:, UNIT:].astype(F32))):
            vh[s * 4 + g, rows, :] = head.astype(BF16)

    def attend(i):
        s, h = lax.div(i, 8), lax.rem(i, 8)
        g = s * 4 + lax.div(h, 2)
        scores = dot_nt(kh[g], qh[i]) * scale
        scores = jnp.where(allowed_keys(low[s], high[...]), scores, negative)
        top = jnp.max(scores, axis=0, keepdims=True)
        p = jnp.exp(scores - top)
        total = jnp.sum(p, axis=0, keepdims=True)
        lse[i] = jnp.broadcast_to(top + jnp.log(total), (8, SPAN))
        heads[h] = (dot_tn(vh[g], p.astype(BF16)) / total).T

    for s in range(2):
        kv_copy(1, s).wait_recv()
        pl.loop(4 * s, 4 * s + 4)(spread_heads)
        pl.loop(8 * s, 8 * s + 4)(attend)
        ag(8 + 2 * s)
        pl.loop(8 * s + 4, 8 * s + 8)(attend)
        rows = slice(s * SPAN, (s + 1) * SPAN)
        for side in range(2):
            mixed = pack_heads([heads[side * 4 + i] for i in range(4)])
            ob[rows, side * UNIT : (side + 1) * UNIT] = mixed.astype(BF16)
        if s == 0:
            load_wait(4, 0, 0)
            load_wait(5, 0, 1)
        xs[rows, :] = dot_nt(ob[rows, :], weight(wbuf, 0, 0, 2 * UNIT)).astype(BF16)
        x_copy(0, 2 * s, xs).start()
        x_copy(0, 2 * s + 1, xs).start()
        ag(9 + 2 * s)

    def norm_second(r):
        x_copy(0, r, xs).wait()
        rows = pl.ds(pl.multiple_of(r * 128, 128), 128)
        x = tokens[rows, :].astype(F32) + (xs[rows, :].astype(F32) + xr[rows, :].astype(F32))
        x2[rows, :] = x
        r2 = lax.rsqrt(jnp.mean(x * x, axis=-1, keepdims=True) + epsilon)
        a_buf[rows, :] = (x * r2 * gain_rows[1:2, :]).astype(BF16)

    acc[...] = jnp.zeros_like(acc)
    out_acc[...] = jnp.zeros_like(out_acc)
    pl.loop(0, 2)(norm_second)
    ag(12)
    ag(13)
    ag(14)
    pl.loop(2, 4)(norm_second)
    give_x()
    ag(15)
    transpose_into(bt, a_buf)
    ag(16)

    def stage_copy(n):
        slot = lax.rem(n, 2)
        return pltpu.make_async_copy(stage.at[slot], fed.at[n], stage_sem.at[slot])

    def back_copy(n):
        slot = lax.rem(n, 2)
        return pltpu.make_async_copy(fed.at[n], back.at[slot], back_sem.at[slot])

    def feed_grads(n, pair, ready):
        slot = lax.rem(n, 2)
        back_copy(n).wait()
        put(pair, 0, dot_nn(bt[...], back[slot, 0]))
        put(pair, 1, dot_nn(bt[...], back[slot, 1]))
        put(pair, 2, dot_nn(et[...], back[slot, 2]))
        if ready:
            within(n + 1, groups, lambda i: back_copy(i).start())

    @pl.loop(0, groups)
    def _(n):
        slot = lax.rem(n, 2)
        for side in range(2):
            load_start(6 + 2 * n + side, slot, side)

        @pl.when(n >= 1)
        def _():
            stage_copy(n - 1).wait()

        @pl.when(n == 1)
        def _():
            back_copy(0).start()

        @pl.when((lax.rem(n, 2) == 0) & (n >= 2))
        def _():
            back_copy(lax.div(n, 2)).start()

        @pl.when(n < groups - 1)
        def _():
            ag(17 + n)

        @pl.when(lax.rem(n, 2) == 1)
        def _():
            feed_grads(lax.div(n, 2), lax.div(n, 2), False)

        @pl.when(n >= 1)
        def _():
            rs(n - 1)

        for side in range(2):
            load_wait(6 + 2 * n + side, slot, side)
        gate = dot_nn(a_buf[...], weight(wbuf, slot, 0, 256))
        up = dot_nn(a_buf[...], weight(wbuf, slot, 256, 512))
        sg = jax.nn.sigmoid(gate)
        silu = gate * sg
        stage[slot, 2] = (silu * up).astype(BF16)
        dh = dot_nn(eb[...], weight(wbuf, slot, 512, 768))
        stage[slot, 0] = (dh * up * sg * (1.0 + gate * (1.0 - sg))).astype(BF16)
        stage[slot, 1] = (dh * silu).astype(BF16)
        stage_copy(n).start()

        @pl.loop(0, 4)
        def _(i):
            columns = pl.ds(pl.multiple_of(i * 4 * depth, 128), 4 * depth)

            def rows_of(lo):
                return wbuf[slot, i, :, :, :, lo : lo + 256].reshape(4 * depth, 256)

            out_acc[:, columns] += dot_nt(stage[slot, 2], rows_of(512))
            acc[:, columns] += dot_nt(stage[slot, 0], rows_of(0)) + dot_nt(stage[slot, 1], rows_of(256))

    load_start(4, 0, 0)
    load_start(5, 0, 1)
    take_x()
    for r in range(4):
        rows = slice(r * 128, (r + 1) * 128)
        xs[rows, :] = acc[rows, :].astype(BF16)
        x_copy(1, r, xs).start()
    for r in range(4):
        rows = slice(r * 128, (r + 1) * 128)
        a_buf[rows, :] = out_acc[rows, :].astype(BF16)
        x_copy(2, r, a_buf).start()
    stage_copy(groups - 1).wait()
    back_copy(4).start()
    rs(7)
    feed_grads(4, 4, True)
    rs(8)

    gacc[...] = jnp.zeros_like(gacc)

    def norm_back(r):
        x_copy(1, r, xs).wait()
        rows = pl.ds(pl.multiple_of(r * 128, 128), 128)
        mine = xs[rows, :].astype(F32)
        db = mine + xr[rows, :].astype(F32)
        x = x2[rows, :]
        r2 = lax.rsqrt(jnp.mean(x * x, axis=-1, keepdims=True) + epsilon)
        n2 = x * r2
        gacc[1:2, :] += jnp.sum(mine * n2, axis=0, keepdims=True)
        scaled = db * gain_rows[1:2, :]
        dx2 = eb[rows, :].astype(F32) + r2 * (scaled - n2 * jnp.mean(scaled * n2, axis=-1, keepdims=True))
        acc[rows, :] = dx2
        eb[rows, :] = dx2.astype(BF16)

    def attend_back(i):
        s, g = lax.div(i, 4), lax.rem(i, 4)
        mask = allowed_keys(low[s], high[...])
        dk = jnp.zeros((4 * SPAN, 128), F32)
        dv = jnp.zeros((4 * SPAN, 128), F32)
        for hh in range(2):
            h = s * 8 + 2 * g + hh
            scores = jnp.where(mask, dot_nt(kh[i], qh[h]) * scale, negative)
            p = jnp.exp(scores - lse[h][0:1, :])
            dp = dot_nt(vh[i], doh[h])
            delta = jnp.sum(p * dp, axis=0, keepdims=True)
            ds = (p * (dp - delta) * scale).astype(BF16)
            dv += dot_nn(p.astype(BF16), doh[h])
            dk += dot_nn(ds, qh[h])
            heads[2 * g + hh] = dot_tn(kh[i], ds).T
        dkh[g] = dk.astype(BF16)
        dvh[g] = dv.astype(BF16)

    def dkv_mine(s, core):
        return kvx.at[:, core, pl.ds(pl.multiple_of(s * SPAN, SPAN), SPAN)]

    def kv_core(s):
        return remote(dkv_mine(s, me.ok), rc.at[s], kv_send.at[2, s], kv_recv.at[2, s], me.sib)

    def kv_y(s):
        return remote(rc.at[s, me.oy], ry.at[s], kv_send.at[3, s], kv_recv.at[3, s], me.ypeer)

    def kv_add(s):
        kv_core(s).wait_recv()
        rc[s] = rc[s] + dkv_mine(s, k)[...]
        kv_y(s).start()

    for s in range(2):
        kv_copy(0, s).wait_send()
        kv_copy(1, s).wait_send()
    load_wait(4, 0, 0)
    load_wait(5, 0, 1)

    @pl.loop(0, 2)
    def _(s):
        rows = pl.ds(pl.multiple_of(s * SPAN, SPAN), SPAN)
        norm_back(2 * s)
        norm_back(2 * s + 1)

        rs(9 + 4 * s)
        for side in range(2):
            mixed = dot_nn(eb[rows, :], weight(wbuf, 0, side * UNIT, (side + 1) * UNIT)).astype(BF16)
            for i, head in enumerate(unpack_heads(mixed.astype(F32))):
                doh[s * 8 + side * 4 + i] = head.astype(BF16)
        attend_back(4 * s)
        attend_back(4 * s + 1)
        feed_grads(5 + 2 * s, 5 + 2 * s, True)
        rs(10 + 4 * s)
        attend_back(4 * s + 2)
        attend_back(4 * s + 3)
        rs(11 + 4 * s)
        for c in range(4):
            at_c = slice(c * SPAN, (c + 1) * SPAN)
            for j, src in enumerate((dkh, dvh)):
                kvx[c // 2, c % 2, rows, j * UNIT : (j + 1) * UNIT] = pack_heads(
                    [src[g, at_c, :].astype(F32) for g in range(4)]
                ).astype(BF16)
        kv_core(s).start()
        for side in range(2):
            dq = turn(pack_heads([heads[side * 4 + j] for j in range(4)]), cosine[...], -sine[...])
            dqb[rows, side * UNIT : (side + 1) * UNIT] = dq.astype(BF16)

        @pl.when(s == 0)
        def _():
            feed_grads(6, 6, True)

        @pl.when(s == 1)
        def _():
            transpose_into(bt, eb)
            for i in range(3):
                put(8, i, dot_nn(bt[...], ob[:, i * 256 : (i + 1) * 256]))

        rs(12 + 4 * s)
        kv_add(s)

    give_x()
    for side in range(2):
        load_start(2 + side, 0, side)
        load_start(side, 1, side)
    rs(17)
    for i in range(3):
        put(9, i, dot_nn(at[...], dqb[:, i * 256 : (i + 1) * 256]))
    rs(18)
    for side in range(2):
        load_wait(2 + side, 0, side)
        load_wait(side, 1, side)

    def norm_grad(s):
        rows = slice(s * SPAN, (s + 1) * SPAN)
        kv_y(s).wait_recv()
        total = rc[s, y].astype(F32) + ry[s].astype(F32)
        ob[rows, :UNIT] = turn(total[:, :UNIT], cosine[...], -sine[...]).astype(BF16)
        ob[rows, UNIT:] = total[:, UNIT:].astype(BF16)
        da = dot_nt(dqb[rows, :], weight(wbuf, 0, 0, 768)) + dot_nt(ob[rows, :], weight(wbuf, 1, 0, 768))
        xs[rows, :] = da.astype(BF16)
        x_copy(3, 2 * s, xs).start()
        x_copy(3, 2 * s + 1, xs).start()

    take_x()
    norm_grad(0)
    rs(19)
    norm_grad(1)
    for i in range(3):
        put(10, i, dot_nn(at[...], ob[:, i * 256 : (i + 1) * 256]))
    rs(20)

    for r in range(4):
        x_copy(2, r, a_buf).wait()
    local(out_peer, eb, 0).start()
    local(out_peer, eb, 0).wait()
    for r in range(4):
        rows = slice(r * 128, (r + 1) * 128)
        a_buf[rows, :] = (x2[rows, :] + (a_buf[rows, :].astype(F32) + eb[rows, :].astype(F32))).astype(BF16)
    local(a_buf, output, 0).start()

    def first_norm(rows):
        x = tokens[rows, :].astype(F32)
        r1 = lax.rsqrt(jnp.mean(x * x, axis=-1, keepdims=True) + epsilon)
        return r1, x * r1

    rs(21)

    @pl.loop(0, 4)
    def _(r):
        rows = pl.ds(pl.multiple_of(r * 128, 128), 128)
        gacc[0:1, :] += jnp.sum(xs[rows, :].astype(F32) * first_norm(rows)[1], axis=0, keepdims=True)

    gain_columns = jnp.concatenate([gacc[...], jnp.zeros((120, WIDE), F32)], axis=0).T
    gather_g.sent(0)
    gw[0] = gain_columns.astype(BF16).reshape(4, 2, 2, depth, 128)
    gain = ReduceA(me, 0, gw.at[0, :, :, me.ok], gw.at[0, :, :, k], (g1, g2, g3), rg_sems)
    gain.core()
    rs(22)
    gain.add_core()
    gain.y_start()
    rs(23)
    gain.y_add()
    gain.z_first()

    @pl.loop(0, 4)
    def _(r):
        x_copy(3, r, xs).wait()
        rows = pl.ds(pl.multiple_of(r * 128, 128), 128)
        da = xs[rows, :].astype(F32) + xr[rows, :].astype(F32)
        r1, n1 = first_norm(rows)
        scaled = da * gain_rows[0:1, :]
        acc[rows, :] += r1 * (scaled - n1 * jnp.mean(scaled * n1, axis=-1, keepdims=True))

    local(acc, grad_tokens, 1).start()
    gain.z_second()
    rs(24)
    gs[0] = gain.z_total()
    gain.z_sent()
    pair_copy = remote(gs.at[0], gs.at[1], g_sems.at[0], g_sems.at[1], me.xpeer)
    pair_copy.start()
    rs(25)
    pair_copy.wait()
    gain_grads[...] = gs[0] + gs[1]
    for s in range(2):
        kv_core(s).wait_send()
        kv_y(s).wait_send()

    @pl.loop(0, units)
    def _(u):
        gather_a.sent(u)
        by_parity(u, units, lambda j, kind: gather_b[kind].sent(j), GATHER_ALIKE)

    out_copy(units - 2).wait()
    out_copy(units - 1).wait()
    local(acc, grad_tokens, 1).wait()
    local(a_buf, output, 0).wait()


def rope_inputs(row_count):
    positions = lax.axis_index("ctx") * row_count + jnp.arange(row_count, dtype=jnp.int32)
    lane = jnp.arange(UNIT, dtype=jnp.int32) % HD
    half_lane = (lane % (HD // 2)).astype(jnp.float32)
    angles = positions.astype(jnp.float32)[:, None] * (rope_base ** (-(2.0 * half_lane) / HD))[None, :]
    cosine = jnp.cos(angles)
    sine = jnp.where(lane[None, :] < HD // 2, -jnp.sin(angles), jnp.sin(angles))
    return positions, cosine, sine


def pack_weights(w_query, w_key, w_value, w_out, w_gate, w_up, w_down):
    depth = w_query.shape[0]
    groups = w_gate.shape[1] // 256
    fed = jnp.concatenate(
        [part.reshape(depth, groups, 256) for part in (w_gate, w_up, w_down.T)], axis=2
    ).reshape(depth, groups * 2 * UNIT)
    flat = jnp.concatenate([w_key, w_value, w_query, w_out.T, fed], axis=1)
    return jnp.transpose(flat.reshape(depth, flat.shape[1] // UNIT, UNIT), (1, 0, 2))


def pack_gains(gain_attn, gain_mlp):
    return jnp.pad(jnp.stack([gain_attn, gain_mlp], axis=1), ((0, 0), (0, 126)))[None]


def call_layer(packed, gains, tokens, cot, cosine, sine, low, high):
    units, depth = packed.shape[0], packed.shape[1]
    groups = (units - 6) // 2
    struct = jax.ShapeDtypeStruct
    vmem = pltpu.VMEM
    any_spec = pl.BlockSpec(memory_space=pl.ANY)
    vmem_spec = pl.BlockSpec(memory_space=pltpu.VMEM)
    block = (4, 2, 2, depth)
    dma = pltpu.SemaphoreType.DMA
    regular = pltpu.SemaphoreType.REGULAR

    def gather_sems(count):
        return (dma((count, 3)),) + tuple(dma((count,)) for _ in range(5))

    def reduce_sems(count):
        return tuple(dma((count,)) for _ in range(6)) + (dma((count, 3)), dma((count, 2)))

    return pl.pallas_call(
        layer_kernel,
        out_shape=(
            struct((ROWS, WIDE), BF16),
            struct((ROWS, WIDE), F32),
            struct((units, depth, UNIT), F32),
            struct((depth, 128), F32),
            struct((units,) + block + (WIDE_A,), BF16),
            struct((units,) + block + (WIDE_B,), BF16),
            struct((groups, 3, ROWS, 256), BF16),
            struct((ROWS, WIDE), BF16),
        ),
        in_specs=[any_spec, vmem_spec, vmem_spec, any_spec] + [vmem_spec] * 4,
        out_specs=(any_spec,) * 3 + (vmem_spec,) + (any_spec,) * 4,
        scratch_shapes=[
            vmem((1,) + block + (128,), BF16),
            vmem((8, WIDE), F32),
            vmem((ROWS, WIDE), BF16),
            vmem((WIDE, ROWS), BF16),
            vmem((WIDE, ROWS), BF16),
            vmem((WIDE, ROWS), BF16),
            vmem((ROWS, WIDE), BF16),
            vmem((2, 2, ROWS, 2 * UNIT), BF16),
            vmem((16, SPAN, 128), BF16),
            vmem((8, 4 * SPAN, 128), BF16),
            vmem((8, 4 * SPAN, 128), BF16),
            vmem((16, 8, SPAN), F32),
            vmem((ROWS, 2 * UNIT), BF16),
            vmem((ROWS, WIDE), F32),
            vmem((ROWS, WIDE), F32),
            vmem((ROWS, WIDE), F32),
            vmem((2,) + block + (2 * UNIT,), BF16),
            vmem((2,) + block + (2 * UNIT,), BF16),
            vmem((2, 3, ROWS, 256), BF16),
            vmem((2, 3, ROWS, 256), BF16),
            vmem((RING, 4, 2, depth, WIDE_A), BF16),
            vmem((RING, 4, depth, WIDE_A), BF16),
            vmem((RING, 4, depth, WIDE_A), BF16),
            vmem((RING, 4, 2, depth, WIDE_B), BF16),
            vmem((RING, 4, depth, WIDE_B), BF16),
            vmem((RING, 4, 2, depth, WIDE_B), BF16),
            vmem((2, depth, UNIT), F32),
            vmem((ROWS, WIDE), BF16),
            vmem((ROWS, WIDE), BF16),
            vmem((16, SPAN, 128), BF16),
            vmem((8, SPAN, 128), F32),
            vmem((4, 4 * SPAN, 128), BF16),
            vmem((4, 4 * SPAN, 128), BF16),
            vmem((2, 2, SPAN, 2 * UNIT), BF16),
            vmem((2, SPAN, 2 * UNIT), BF16),
            vmem((ROWS, 2 * UNIT), BF16),
            vmem((8, WIDE), F32),
            vmem((4, 2, depth, 128), BF16),
            vmem((4, depth, 128), BF16),
            vmem((4, depth, 128), BF16),
            vmem((2, depth, 128), F32),
            gather_sems(units),
            gather_sems(units),
            gather_sems(1),
            reduce_sems(units),
            reduce_sems(units),
            reduce_sems(1),
            regular,
            regular,
            regular((3,)),
            regular,
            dma((4, 4)),
            dma((4, 4)),
            dma((4, 2)),
            dma((4, 2)),
            dma((2,)),
            dma((4,)),
            dma((2, 2, 2)),
            dma((2,)),
            dma((2,)),
            dma((2,)),
            dma((3, units)),
        ],
        compiler_params=pltpu.CompilerParams(
            collective_id=1, has_side_effects=True, vmem_limit_bytes=64 << 20
        ),
        name="layer",
    )(packed, gains, tokens, cot, cosine, sine, low, high)


def unpack_kernel(grads, query, key, value, out, gate, up, down):
    groups = gate.shape[1] // 256
    for n in range(groups):
        gate[:, n * 256 : (n + 1) * 256] = grads[2 * n, :, :256]
        up[:, n * 256 : n * 256 + 128] = grads[2 * n, :, 256:]
        up[:, n * 256 + 128 : (n + 1) * 256] = grads[2 * n + 1, :, :128]
        down[:, n * 256 : (n + 1) * 256] = grads[2 * n + 1, :, 128:]
    for side in range(2):
        out[:, side * UNIT : (side + 1) * UNIT] = grads[2 * groups + side]
        query[:, side * UNIT : (side + 1) * UNIT] = grads[2 * groups + 2 + side]
    key[...] = grads[2 * groups + 4]
    value[...] = grads[2 * groups + 5]


def call_unpack(grads):
    units, depth = grads.shape[0], grads.shape[1]
    hidden = (units - 6) // 2 * 256
    vmem_spec = pl.BlockSpec(memory_space=pltpu.VMEM)
    shapes = (
        (depth, 2 * UNIT),
        (depth, UNIT),
        (depth, UNIT),
        (depth, 2 * UNIT),
        (depth, hidden),
        (depth, hidden),
        (depth, hidden),
    )
    return pl.pallas_call(
        unpack_kernel,
        out_shape=tuple(jax.ShapeDtypeStruct(shape, F32) for shape in shapes),
        in_specs=[vmem_spec],
        out_specs=(vmem_spec,) * 7,
        compiler_params=pltpu.CompilerParams(vmem_limit_bytes=32 << 20),
        name="unpack",
    )(grads)


def fast_body(
    tokens,
    segments,
    cotangent,
    gain_attn,
    w_query,
    w_key,
    w_value,
    w_out,
    gain_mlp,
    w_gate,
    w_up,
    w_down,
):
    positions, cosine, sine = rope_inputs(SPAN)
    mine = lax.dynamic_slice_in_dim(segments, positions[0], SPAN, 1)
    low = jnp.sum((segments[:, None, :] < mine[:, :, None]).astype(jnp.int32), axis=-1)[:, None, :]
    high = positions[None, :]
    packed = pack_weights(w_query, w_key, w_value, w_out, w_gate, w_up, w_down)
    output, grad_tokens, grads, gain_grads = call_layer(
        packed,
        pack_gains(gain_attn, gain_mlp),
        tokens.reshape(ROWS, WIDE),
        cotangent.reshape(ROWS, WIDE),
        cosine,
        sine,
        low,
        high,
    )[:4]

    query, key, value, out, gate, up, down = call_unpack(grads)
    return (
        output.reshape(tokens.shape),
        grad_tokens.reshape(tokens.shape),
        gain_grads[:, 0],
        query,
        key,
        value,
        out.T,
        gain_grads[:, 1],
        gate,
        up,
        down.T,
    )


def fits(mesh):
    return mesh.shape["fsdp"] == 4 and mesh.shape["ctx"] == 4 and mesh.shape["tp"] == 2


def solution(mesh):
    placed = (
        P("fsdp", "ctx", None),
        P("fsdp", None),
        P("fsdp", "ctx", None),
        P(("fsdp", "ctx")),
        P(("fsdp", "ctx"), "tp"),
        P(("fsdp", "ctx"), "tp"),
        P(("fsdp", "ctx"), "tp"),
        P("tp", ("fsdp", "ctx")),
        P(("fsdp", "ctx")),
        P(("fsdp", "ctx"), "tp"),
        P(("fsdp", "ctx"), "tp"),
        P("tp", ("fsdp", "ctx")),
    )
    return jax.shard_map(
        fast_body if fits(mesh) else body,
        mesh=mesh,
        in_specs=placed,
        out_specs=(
            P("fsdp", "ctx", None),
            P("fsdp", "ctx", None),
            P(("fsdp", "ctx")),
            P(("fsdp", "ctx"), "tp"),
            P(("fsdp", "ctx"), "tp"),
            P(("fsdp", "ctx"), "tp"),
            P("tp", ("fsdp", "ctx")),
            P(("fsdp", "ctx")),
            P(("fsdp", "ctx"), "tp"),
            P(("fsdp", "ctx"), "tp"),
            P("tp", ("fsdp", "ctx")),
        ),
        check_vma=False,
    )
```
